128 devices in a mesh: replica: 64 (over z, y, x), shard: 2 (over core).
Axes of the slice: x: 4, y: 4, z: 4, core: 2. Of those that a mesh axis runs over, the one named last changes fastest.
Arguments:
- tokens: bfloat16 [65536, 768], P(('replica', 'shard')), may hold values from -6 to 6
- lengths: int32 [64], P('replica'), may hold values from 513 to 1024, as said below
- project_weight: bfloat16 [768, 2304], P('shard'), may hold values from -0.21875 to 0.21875
- project_bias: bfloat16 [2304], P('shard'), may hold values from -2 to 2
- dense_weight: bfloat16 [768, 768], P('shard'), may hold values from -0.875 to 0.875
- dense_bias: bfloat16 [768], P('shard'), may hold values from -1.1953125 to 1.1953125
- expand_weight: bfloat16 [768, 3072], P('shard'), may hold values from -0.21875 to 0.21875
- expand_bias: bfloat16 [3072], P('shard'), may hold values from -2 to 2
- contract_weight: bfloat16 [3072, 768], P('shard'), may hold values from -0.109375 to 0.109375
- contract_bias: bfloat16 [768], P('shard'), may hold values from -1.1953125 to 1.1953125
- first_gain: bfloat16 [768], P('shard'), may hold values from 0.5 to 1.5
- first_shift: bfloat16 [768], P('shard'), may hold values from -1.1953125 to 1.1953125
- second_gain: bfloat16 [768], P('shard'), may hold values from 0.5 to 1.5
- second_shift: bfloat16 [768], P('shard'), may hold values from -1.1953125 to 1.1953125
- out_grad: bfloat16 [65536, 768], P(('replica', 'shard')), may hold values from -6 to 6
Outputs:
- outputs: bfloat16 [65536, 768], P(('replica', 'shard'))
- input_grad: float32 [65536, 768], P(('replica', 'shard'))
- project_weight_grad: float32 [768, 2304], P('shard')
- project_bias_grad: float32 [2304], P('shard')
- dense_weight_grad: float32 [768, 768], P('shard')
- dense_bias_grad: float32 [768], P('shard')
- expand_weight_grad: float32 [768, 3072], P('shard')
- expand_bias_grad: float32 [3072], P('shard')
- contract_weight_grad: float32 [3072, 768], P('shard')
- contract_bias_grad: float32 [768], P('shard')
- first_gain_grad: float32 [768], P('shard')
- first_shift_grad: float32 [768], P('shard')
- second_gain_grad: float32 [768], P('shard')
- second_shift_grad: float32 [768], P('shard')
The draws below stay inside these ranges and needn't reach their ends.
Inputs may be any that keep to these rules, and one draw needn't show every extreme that they name: `lengths`: each group's sequence fills positions 0 to its length - 1; in every draw one group has length 1024 and another 1024 - 511.
All inputs are finite; a program needn't handle non-finite values.
Results may differ from the reference program's by a relative error of at most 0.0095.
Values may be sent and summed in bfloat16 or wider, within the bound.
No kernel may reach another device: no remote copies, remote signals or barrier semaphores. Data moves between devices by JAX's collectives and lax.ppermute only.
A program may use at most 192 MiB of HBM per device.

```python
import jax
import jax.numpy as jnp
from jax import lax

HEADS = 12
HEAD_DIM = 64
D = 768
ROT = 16
FF = 3072
SEQ_LEN = 1024
TOK_DEV = 512
TOKENS = 65536
N_REPLICA = 64


def draw_lengths(key, part):
    key = jax.random.fold_in(key, 7)
    first_key, second_key, third_key = jax.random.split(key, 3)
    shortest = SEQ_LEN - TOK_DEV + 1
    drawn = jax.random.randint(first_key, (N_REPLICA,), shortest, SEQ_LEN + 1)
    full_at = jax.random.randint(second_key, (), 0, N_REPLICA)
    short_at = (full_at + jax.random.randint(third_key, (), 1, N_REPLICA)) % N_REPLICA
    drawn = drawn.at[full_at].set(SEQ_LEN)
    drawn = drawn.at[short_at].set(shortest)
    return drawn.astype(jnp.int32)


def levels(own_key, extent, pieces, low, high):
    gain = 1.0
    for position, shards_of in pieces:
        heights = jax.random.uniform(jax.random.fold_in(jax.random.fold_in(own_key, 6), position), (shards_of,), jnp.float32, low / len(pieces), high / len(pieces))
        gain = gain * jnp.repeat(jnp.exp(heights), extent[position] // shards_of).reshape((-1,) + (1,) * (len(extent) - 1 - position))
    return gain


def gaussian(stream_key, dims, spread, bound, cuts=(), kind=jnp.bfloat16):
    result = jax.random.normal(stream_key, dims, jnp.float32) * spread
    if len(cuts) > 0:
        result = levels(stream_key, dims, cuts, -0.22, 0.18) * result
    return jnp.clip(result, min=-bound, max=bound).astype(kind)


def setup_inputs(seed: int = 0) -> dict:
    arg_keys = jax.random.split(jax.random.key(seed), 16)
    return {
        "tokens": gaussian(arg_keys[0], (TOKENS, D), 1.0, 6.0, ((0, 128),)),
        "lengths": draw_lengths(jax.random.fold_in(arg_keys[15], 71), 0),
        "project_weight": gaussian(arg_keys[2], (D, 3 * D), D ** -0.5, 0.21875, ((0, 2),)),
        "project_bias": gaussian(arg_keys[3], (3 * D,), 0.3, 2.0, ((0, 2),)),
        "dense_weight": gaussian(arg_keys[4], (D, D), (max(D // 16, 1)) ** -0.5, 0.875, ((0, 2),)),
        "dense_bias": gaussian(arg_keys[5], (D,), 0.2, 1.1953125, ((0, 2),)),
        "expand_weight": gaussian(arg_keys[6], (D, FF), D ** -0.5, 0.21875, ((0, 2),)),
        "expand_bias": gaussian(arg_keys[7], (FF,), 0.3, 2.0, ((0, 2),)),
        "contract_weight": gaussian(arg_keys[8], (FF, D), FF ** -0.5, 0.109375, ((0, 2),)),
        "contract_bias": gaussian(arg_keys[9], (D,), 0.2, 1.1953125, ((0, 2),)),
        "first_gain": jnp.clip(1.0 + 0.1 * jax.random.normal(arg_keys[10], (D,), jnp.float32), 0.5, 1.5).astype(jnp.bfloat16),
        "first_shift": gaussian(arg_keys[11], (D,), 0.2, 1.1953125, ((0, 2),)),
        "second_gain": jnp.clip(1.0 + 0.1 * jax.random.normal(arg_keys[12], (D,), jnp.float32), 0.5, 1.5).astype(jnp.bfloat16),
        "second_shift": gaussian(arg_keys[13], (D,), 0.2, 1.1953125, ((0, 2),)),
        "out_grad": gaussian(arg_keys[14], (TOKENS, D), 1.0, 6.0, ((0, 128),)),
    }


@jax.custom_vjp
def low(v):
    return lax.optimization_barrier(v.astype(jnp.bfloat16)).astype(jnp.float32)

@jax.custom_vjp
def low_back(v):
    return v

def low_keep(v):
    return (low(v), None)

def low_pass(kept, grad):
    return (grad,)

def back_keep(v):
    return (v, None)

def back_low(kept, grad):
    return (low(grad),)
low.defvjp(low_keep, low_pass)
low_back.defvjp(back_keep, back_low)
EPSILON = 1e-05

def norm_rows(values, gain_row, shift_row):
    row_mean = lax.optimization_barrier(jnp.mean(values, axis=-1, keepdims=True))
    centered = values - row_mean
    row_var = lax.optimization_barrier(jnp.mean(centered * centered, axis=-1, keepdims=True))
    return centered * lax.rsqrt(row_var + EPSILON) * gain_row + shift_row

def matmul(left_side, right_side):
    return jnp.dot(left_side, right_side, precision=lax.Precision.HIGHEST, preferred_element_type=jnp.float32)

def rotary_tables(positions):
    frequency = 10000.0 ** (-jnp.arange(0, ROT, 2, dtype=jnp.float32) / ROT)
    angles = positions[:, None] * frequency[None, :]
    cos_table = jnp.cos(angles)
    sin_table = jnp.sin(angles)
    return (jnp.concatenate([cos_table, cos_table], axis=-1), jnp.concatenate([sin_table, sin_table], axis=-1))

def rotate(head_rows, cos_table, sin_table):
    rotated = head_rows[..., :ROT]
    tail_dims = head_rows[..., ROT:]
    first_half = rotated[..., :ROT // 2]
    second_half = rotated[..., ROT // 2:]
    turned = jnp.concatenate([-second_half, first_half], axis=-1)
    mixed_part = rotated * cos_table[:, None, :] + turned * sin_table[:, None, :]
    return jnp.concatenate([mixed_part, tail_dims], axis=-1)

def block_forward(inputs, params):
    w_project, b_project, w_dense, b_dense, w_expand, b_expand, w_contract, b_contract, gain_one, shift_one, gain_two, shift_two = params
    positions = jnp.arange(SEQ_LEN, dtype=jnp.float32)
    cos_table, sin_table = rotary_tables(positions)
    normed_one = low(norm_rows(inputs, gain_one, shift_one))
    packed = low_back(matmul(normed_one, w_project) + b_project)
    queries = low(rotate(packed[:, :D].reshape(SEQ_LEN, HEADS, HEAD_DIM), cos_table, sin_table))
    keys_rot = low(rotate(packed[:, D:2 * D].reshape(SEQ_LEN, HEADS, HEAD_DIM), cos_table, sin_table))
    value_heads = low(packed[:, 2 * D:].reshape(SEQ_LEN, HEADS, HEAD_DIM))
    scores = low_back(jnp.einsum('qhd,khd->hqk', queries, keys_rot, precision=lax.Precision.HIGHEST) * 0.125)
    causal = jnp.arange(SEQ_LEN, dtype=jnp.int32)[:, None] >= jnp.arange(SEQ_LEN, dtype=jnp.int32)[None, :]
    scores = jnp.where(causal[None], scores, -1e+30)
    row_max = lax.optimization_barrier(jnp.max(scores, axis=-1, keepdims=True))
    exponent = jnp.exp(scores - row_max)
    prob_low = low(exponent / lax.optimization_barrier(jnp.sum(exponent, axis=-1, keepdims=True)))
    context = jnp.einsum('hqk,khd->qhd', prob_low, value_heads, precision=lax.Precision.HIGHEST)
    context = low(low_back(context)).reshape(SEQ_LEN, D)
    attended = low_back(matmul(context, w_dense) + b_dense)
    normed_two = low(norm_rows(inputs, gain_two, shift_two))
    hidden = low_back(matmul(normed_two, w_expand) + b_expand)
    activated = low(jax.nn.gelu(hidden, approximate=False))
    mlp_out = low_back(matmul(activated, w_contract) + b_contract)
    return inputs + attended + mlp_out

def reference(tokens, lengths, project_weight, project_bias, dense_weight, dense_bias, expand_weight, expand_bias, contract_weight, contract_bias, first_gain, first_shift, second_gain, second_shift, out_grad):
    params = tuple((member.astype(jnp.float32) for member in (project_weight, project_bias, dense_weight, dense_bias, expand_weight, expand_bias, contract_weight, contract_bias, first_gain, first_shift, second_gain, second_shift)))
    inputs = tokens.astype(jnp.float32).reshape(N_REPLICA, SEQ_LEN, D)

    def forward(group_inputs, group_params):
        return lax.map(jax.checkpoint(lambda one_group: block_forward(one_group, group_params)), group_inputs)
    outputs, pullback = jax.vjp(forward, inputs, params)
    live_rows = (jnp.arange(SEQ_LEN, dtype=jnp.int32)[None, :] < lengths[:, None]).astype(jnp.float32)
    seed_grad = out_grad.astype(jnp.float32).reshape(N_REPLICA, SEQ_LEN, D) * live_rows[..., None]
    input_grad, param_grads = pullback(seed_grad)
    g_project, g_project_bias, g_dense, g_dense_bias, g_expand, g_expand_bias, g_contract, g_contract_bias, g_gain_one, g_shift_one, g_gain_two, g_shift_two = param_grads
    return (outputs.reshape(TOKENS, D).astype(jnp.bfloat16), input_grad.reshape(TOKENS, D), g_project, g_project_bias, g_dense, g_dense_bias, g_expand, g_expand_bias, g_contract, g_contract_bias, g_gain_one, g_shift_one, g_gain_two, g_shift_two)
```

```python
import jax
import jax.numpy as jnp
import numpy as np
from jax import lax
from jax.experimental import pallas as pl
from jax.experimental.pallas import tpu as pltpu
from jax.sharding import PartitionSpec as P

HEADS = 12
HEAD_DIM = 64
D = 768
ROT = 16
FF = 3072
SEQ = 1024
TOK_DEV = 512
EPSILON = 1e-05
SCORE_SCALE = 0.125
F32 = jnp.float32
BF16 = jnp.bfloat16
VMEM_LIMIT = 60 * 1024 * 1024
OWN_FF = FF // 2
OWN_D = D // 2
PAIR = 2 * HEAD_DIM
PAIRS = OWN_D // PAIR
HIDDEN_BLOCK = 256
CHUNK = 256
CHUNKS = SEQ // CHUNK
BOTH = ("replica", "shard")


def product(left, right):
    return lax.dot_general(left, right, (((1,), (0,)), ((), ())), preferred_element_type=F32)


def product_nt(left, right):
    return lax.dot_general(left, right, (((1,), (1,)), ((), ())), preferred_element_type=F32)


def product_tn(left, right):
    return lax.dot_general(left, right, (((0,), (0,)), ((), ())), preferred_element_type=F32)


def chunk_rows(c):
    return slice(c * CHUNK, (c + 1) * CHUNK)


def params(**kw):
    return pltpu.CompilerParams(vmem_limit_bytes=VMEM_LIMIT, **kw)


def cost(flops, size=8 << 20, exps=0):
    return pl.CostEstimate(flops=int(flops), bytes_accessed=int(size), transcendentals=int(exps))


VMEM_SPEC = pl.BlockSpec(memory_space=pltpu.VMEM)
SMEM_SPEC = pl.BlockSpec(memory_space=pltpu.SMEM)
ANY_SPEC = pl.BlockSpec(memory_space=pl.ANY)


def shaped(*dims, kind=BF16):
    return jax.ShapeDtypeStruct(dims, kind)


def standardise(rows):
    mean = jnp.mean(rows, axis=-1, keepdims=True)
    centered = rows - mean
    scale = lax.rsqrt(jnp.mean(centered * centered, axis=-1, keepdims=True) + EPSILON)
    return centered * scale, scale


def prep_kernel(place_ref, mine_ref, other_ref, grad_ref, other_grad_ref, vec_ref,
                n1_ref, n1t_ref, n2_ref, n2t_ref, seed_ref, tok_ref, sum_ref):
    side = place_ref[0]
    length = place_ref[1]
    total = jnp.zeros((1, D), F32)
    for part in range(2):
        source, cot = (mine_ref, grad_ref) if part == 0 else (other_ref, other_grad_ref)
        base = (side if part == 0 else 1 - side) * TOK_DEV
        for c in range(TOK_DEV // CHUNK):
            rows = chunk_rows(c)
            start = pl.multiple_of(base + c * CHUNK, CHUNK)
            dest = pl.ds(start, CHUNK)
            low = source[rows, :]
            tok_ref[dest, :] = low
            normal, _ = standardise(low.astype(F32))
            one = (normal * vec_ref[0:1, :] + vec_ref[1:2, :]).astype(BF16)
            two = (normal * vec_ref[2:3, :] + vec_ref[3:4, :]).astype(BF16)
            n1_ref[dest, :] = one
            n2_ref[dest, :] = two
            n1t_ref[:, dest] = one.T
            n2t_ref[:, dest] = two.T
            position = start + lax.broadcasted_iota(jnp.int32, (CHUNK, D), 0)
            seed = jnp.where(position < length, cot[rows, :].astype(F32), 0.0)
            total += jnp.sum(seed, axis=0, keepdims=True)
            seed_ref[dest, :] = seed.astype(BF16)
    sum_ref[...] = total


def prep(place, mine, other, grad, other_grad, vec):
    return pl.pallas_call(
        prep_kernel,
        in_specs=[SMEM_SPEC] + [VMEM_SPEC] * 5,
        out_specs=[VMEM_SPEC] * 7,
        out_shape=[shaped(SEQ, D), shaped(D, SEQ), shaped(SEQ, D), shaped(D, SEQ), shaped(SEQ, D), shaped(SEQ, D),
                   shaped(1, D, kind=F32)],
        compiler_params=params(),
        cost_estimate=cost(4e9),
        name="prep",
    )(place, mine, other, grad, other_grad, vec)


def gelu_pair(hidden):
    size = jnp.abs(hidden)
    near = 1.0 / (1.0 + (0.3275911 * 0.7071067811865476) * size)
    bell = jnp.exp(-0.5 * hidden * hidden)
    poly = 0.5 * 1.061405429 * near - 0.5 * 1.453152027
    poly = poly * near + 0.5 * 1.421413741
    poly = poly * near - 0.5 * 0.284496736
    poly = poly * near + 0.5 * 0.254829592
    tail = poly * near * bell
    phi = jnp.where(hidden >= 0, 1.0 - tail, tail)
    return hidden * phi, phi + hidden * bell * 0.3989422804014327


def ffn_kernel(n2_ref, n2t_ref, seed_ref, we_ref, be_ref, wc_ref,
               gc_ref, ge_ref, gbe_ref, mlp_ref, q2_ref, act_ref, gh_ref):
    step = pl.program_id(0)

    @pl.when(step == 0)
    def _():
        mlp_ref[...] = jnp.zeros_like(mlp_ref)
        q2_ref[...] = jnp.zeros_like(q2_ref)

    bias = be_ref[...].astype(F32)
    total = jnp.zeros((1, HIDDEN_BLOCK), F32)
    for c in range(CHUNKS):
        rows = chunk_rows(c)
        hidden = product(n2_ref[rows, :], we_ref[...]) + bias
        value, slope = gelu_pair(hidden)
        act = value.astype(BF16)
        gh = (product_nt(seed_ref[rows, :], wc_ref[...]) * slope).astype(BF16)
        act_ref[rows, :] = act
        gh_ref[rows, :] = gh
        total += jnp.sum(gh.astype(F32), axis=0, keepdims=True)
        mlp_ref[rows, :] += product(act, wc_ref[...])
        q2_ref[rows, :] += product_nt(gh, we_ref[...])
    gbe_ref[...] = total
    gc_ref[...] = product_tn(act_ref[...], seed_ref[...]).astype(BF16)
    ge_ref[...] = product(n2t_ref[...], gh_ref[...]).astype(BF16)


def whole(*dims):
    return pl.BlockSpec(dims, lambda i: (0,) * len(dims))


def ffn(n2, n2t, seed, we, be, wc):
    rows_block = pl.BlockSpec((HIDDEN_BLOCK, D), lambda i: (i, 0))
    cols_block = pl.BlockSpec((D, HIDDEN_BLOCK), lambda i: (0, i))
    bias_block = pl.BlockSpec((1, HIDDEN_BLOCK), lambda i: (0, i))
    return pl.pallas_call(
        ffn_kernel,
        grid=(OWN_FF // HIDDEN_BLOCK,),
        in_specs=[whole(SEQ, D), whole(D, SEQ), whole(SEQ, D), cols_block, bias_block, rows_block],
        out_specs=[rows_block, cols_block, bias_block, whole(SEQ, D), whole(SEQ, D)],
        out_shape=[shaped(OWN_FF, D), shaped(D, OWN_FF), shaped(1, OWN_FF, kind=F32),
                   shaped(SEQ, D, kind=F32), shaped(SEQ, D, kind=F32)],
        scratch_shapes=[pltpu.VMEM((SEQ, HIDDEN_BLOCK), BF16), pltpu.VMEM((SEQ, HIDDEN_BLOCK), BF16)],
        compiler_params=params(dimension_semantics=("arbitrary",)),
        cost_estimate=cost(12 * SEQ * D * OWN_FF, 20 << 20, 2 * SEQ * OWN_FF),
        name="ffn",
    )(n2, n2t, seed, we, be, wc)


def rotary_arrays():
    frequency = (np.float32(10000.0) ** (-np.arange(0, ROT, 2, dtype=np.float32) / np.float32(ROT))).astype(np.float32)
    angles = (np.arange(SEQ, dtype=np.float32)[:, None] * frequency[None, :]).astype(np.float64)
    cos, sin = np.cos(angles), np.sin(angles)
    half = ROT // 2
    keep = np.ones((SEQ, HEAD_DIM))
    up = np.zeros((SEQ, HEAD_DIM))
    down = np.zeros((SEQ, HEAD_DIM))
    keep[:, :half] = cos
    keep[:, half:ROT] = cos
    down[:, :half] = -sin
    up[:, half:ROT] = sin
    return [np.tile(t, (1, 2)).astype(np.float32) for t in (keep, up, down)]


def turn(rows, keep, up, down):
    return rows * keep + pltpu.roll(rows, ROT // 2, 1) * up + pltpu.roll(rows, PAIR - ROT // 2, 1) * down


def heads_kernel(n1_ref, seed_ref, keep_ref, up_ref, down_ref, wp_ref, bp_ref, wd_ref, *rest):
    q_ref, k_ref, v_ref, c_ref = rest[-4:]
    for c in range(CHUNKS):
        rows = chunk_rows(c)
        packed = product(n1_ref[rows, :], wp_ref[...]) + bp_ref[...].astype(F32)
        tables = keep_ref[rows, :], up_ref[rows, :], down_ref[rows, :]
        for p in range(PAIRS):
            cols = slice(p * PAIR, (p + 1) * PAIR)
            q = packed[:, p * PAIR:(p + 1) * PAIR]
            k = packed[:, OWN_D + p * PAIR:OWN_D + (p + 1) * PAIR]
            q_ref[rows, cols] = (turn(q, *tables).astype(BF16) * SCORE_SCALE).astype(BF16)
            k_ref[rows, cols] = turn(k, *tables).astype(BF16)
        v_ref[rows, :] = packed[:, 2 * OWN_D:].astype(BF16)
        c_ref[rows, :] = product_nt(seed_ref[rows, :], wd_ref[...]).astype(BF16)


def heads(n1, seed, tables, wp, bp, wd, after):
    return pl.pallas_call(
        heads_kernel,
        in_specs=[VMEM_SPEC] * 8 + [ANY_SPEC] * len(after),
        out_specs=[VMEM_SPEC] * 4,
        out_shape=[shaped(SEQ, OWN_D)] * 4,
        compiler_params=params(),
        cost_estimate=cost(2 * SEQ * D * 4 * OWN_D),
        name="heads",
    )(n1, seed, *tables, wp, bp, wd, *after)


def attend_kernel(head, waits, *refs):
    q_ref, k_ref, v_ref, c_ref, keep_ref, up_ref, down_ref = refs[:7]
    before = refs[7:11] if head == 1 else ()
    ctx_ref, gq_ref, gk_ref, gv_ref, dk_s, dv_s = refs[-6:]
    lane = lax.broadcasted_iota(jnp.int32, (CHUNK, PAIR), 1)
    mine = (lane < HEAD_DIM) if head == 0 else (lane >= HEAD_DIM)
    diagonal = lax.broadcasted_iota(jnp.int32, (CHUNK, CHUNK), 0) >= lax.broadcasted_iota(jnp.int32, (CHUNK, CHUNK), 1)

    def put(ref, at, rows, value):
        low = jnp.where(mine, value, 0.0).astype(BF16)
        ref[rows, :] = low if head == 0 else jnp.where(mine, low, before[at][rows, :])

    for c in reversed(range(CHUNKS)):
        rows = chunk_rows(c)
        span = (c + 1) * CHUNK
        q = jnp.where(mine, q_ref[rows, :], 0)
        gc = jnp.where(mine, c_ref[rows, :], 0)
        scores = jnp.where(diagonal, product_nt(q, k_ref[c * CHUNK:span, :]), -1e30)
        if c > 0:
            scores = jnp.concatenate([product_nt(q, k_ref[:c * CHUNK, :]), scores], axis=1)
        top = jnp.max(scores, axis=1, keepdims=True)
        power = jnp.exp(scores - top)
        inverse = 1.0 / jnp.sum(power, axis=1, keepdims=True)
        power_low = power.astype(BF16)
        ctx = jnp.where(mine, product(power_low, v_ref[:span, :]), 0.0) * inverse
        put(ctx_ref, 0, rows, ctx)
        gc_scaled = (gc.astype(F32) * inverse).astype(BF16)
        delta = jnp.sum(ctx * gc_scaled.astype(F32), axis=1, keepdims=True)
        grad_prob = product_nt(gc_scaled, v_ref[:span, :])
        grad_scores = (power * (grad_prob - delta)).astype(BF16)
        back = keep_ref[rows, :], -up_ref[rows, :], -down_ref[rows, :]
        grad_q = jnp.where(mine, product(grad_scores, k_ref[:span, :]), 0.0) * SCORE_SCALE
        put(gq_ref, 1, rows, turn(grad_q, *back))
        dv = product_tn(power_low, gc_scaled)
        dk = product_tn(grad_scores, q)
        if c == CHUNKS - 1:
            dv_s[...] = dv
            dk_s[...] = dk
        else:
            dv_s[:span, :] += dv
            dk_s[:span, :] += dk
    for c in range(CHUNKS):
        rows = chunk_rows(c)
        back = keep_ref[rows, :], -up_ref[rows, :], -down_ref[rows, :]
        put(gk_ref, 2, rows, turn(dk_s[rows, :], *back))
        put(gv_ref, 3, rows, dv_s[rows, :])


def attend(pair, head, qkvc, tables, before, after):
    def kernel(*refs):
        attend_kernel(head, len(after), *refs)

    spec = pl.BlockSpec((SEQ, PAIR), lambda i: (0, pair))
    return pl.pallas_call(
        kernel,
        grid=(1,),
        in_specs=[spec] * 4 + [whole(SEQ, PAIR)] * (3 + len(before)) + [ANY_SPEC] * len(after),
        out_specs=[whole(SEQ, PAIR)] * 4,
        out_shape=[shaped(SEQ, PAIR)] * 4,
        scratch_shapes=[pltpu.VMEM((SEQ, PAIR), F32)] * 2,
        compiler_params=params(dimension_semantics=("arbitrary",)),
        cost_estimate=cost(5e9, 4 << 20, SEQ * SEQ),
        name="attend",
    )(*qkvc, *tables, *before, *after)


def weights_kernel(n1t_ref, seed_ref, *refs):
    ins, (gw_ref, gd_ref, gb_ref) = refs[:4 * PAIRS], refs[-3:]
    ctx = jnp.concatenate([ins[4 * p][...] for p in range(PAIRS)], axis=1)
    gd_ref[...] = product_tn(ctx, seed_ref[...]).astype(BF16)
    for t in range(3):
        grads = jnp.concatenate([ins[4 * p + 1 + t][...] for p in range(PAIRS)], axis=1)
        gw_ref[:, t * OWN_D:(t + 1) * OWN_D] = product(n1t_ref[...], grads).astype(BF16)
        gb_ref[:, t * OWN_D:(t + 1) * OWN_D] = jnp.sum(grads.astype(F32), axis=0, keepdims=True)


def weights(n1t, seed, pieces):
    return pl.pallas_call(
        weights_kernel,
        in_specs=[VMEM_SPEC] * (2 + 4 * PAIRS),
        out_specs=[VMEM_SPEC] * 3,
        out_shape=[shaped(D, 3 * OWN_D), shaped(OWN_D, D), shaped(1, 3 * OWN_D, kind=F32)],
        compiler_params=params(),
        cost_estimate=cost(2 * SEQ * D * 4 * OWN_D),
        name="weights",
    )(n1t, seed, *pieces)


def tail_kernel(place_ref, tok_ref, mlp_ref, q2_ref, wp_ref, wd_ref, vec_ref, *refs):
    ins, (keep_out, send_out, keep_in, send_in, sums_ref) = refs[:4 * PAIRS], refs[-5:]
    side = place_ref[0]
    sums = [jnp.zeros((1, D), F32) for _ in range(4)]
    for part in (1, 0):
        base = (side if part == 0 else 1 - side) * TOK_DEV
        for c in range(TOK_DEV // CHUNK):
            rows = chunk_rows(c)
            source = pl.ds(pl.multiple_of(base + c * CHUNK, CHUNK), CHUNK)
            ctx = jnp.concatenate([ins[4 * p][source, :] for p in range(PAIRS)], axis=1)
            grads = jnp.concatenate([ins[4 * p + 1 + t][source, :] for t in range(3) for p in range(PAIRS)], axis=1)
            out = mlp_ref[source, :] + product(ctx, wd_ref[...])
            q1 = product_nt(grads, wp_ref[...])
            q2 = q2_ref[source, :]
            normal, _ = standardise(tok_ref[source, :].astype(F32))
            for i, term in enumerate((q1 * normal, q1, q2 * normal, q2)):
                sums[i] += jnp.sum(term, axis=0, keepdims=True)
            mixed = q1 * vec_ref[0:1, :] + q2 * vec_ref[2:3, :]
            if part == 0:
                keep_out[rows, :] = out
                keep_in[rows, :] = mixed
            else:
                send_out[rows, :] = out.astype(BF16)
                send_in[rows, :] = mixed.astype(BF16)
    sums_ref[...] = jnp.concatenate(sums, axis=0)


def tail(place, tok, mlp, q2, wp, wd, vec, pieces):
    return pl.pallas_call(
        tail_kernel,
        in_specs=[SMEM_SPEC] + [VMEM_SPEC] * (6 + 4 * PAIRS),
        out_specs=[VMEM_SPEC] * 5,
        out_shape=[shaped(TOK_DEV, D, kind=F32), shaped(TOK_DEV, D), shaped(TOK_DEV, D, kind=F32), shaped(TOK_DEV, D),
                   shaped(4, D, kind=F32)],
        compiler_params=params(),
        cost_estimate=cost(2 * SEQ * D * 4 * OWN_D, 16 << 20),
        name="tail",
    )(place, tok, mlp, q2, wp, wd, vec, *pieces)


def last_kernel(place_ref, tok_ref, grad_ref, keep_out, got_out, keep_in, got_in, bias_ref, out_ref, in_ref):
    side = place_ref[0]
    length = place_ref[1]
    bias = bias_ref[0:1, :] + bias_ref[1:2, :]
    for c in range(TOK_DEV // CHUNK):
        rows = chunk_rows(c)
        tok = tok_ref[rows, :].astype(F32)
        out_ref[rows, :] = (tok + keep_out[rows, :] + got_out[rows, :].astype(F32) + bias).astype(BF16)
        normal, scale = standardise(tok)
        mixed = keep_in[rows, :] + got_in[rows, :].astype(F32)
        position = side * TOK_DEV + c * CHUNK + lax.broadcasted_iota(jnp.int32, (CHUNK, D), 0)
        seed = jnp.where(position < length, grad_ref[rows, :].astype(F32), 0.0)
        mean = jnp.mean(mixed, axis=-1, keepdims=True)
        along = jnp.mean(mixed * normal, axis=-1, keepdims=True)
        in_ref[rows, :] = seed + scale * (mixed - mean - normal * along)


def last(place, tok, grad, keep_out, got_out, keep_in, got_in, bias):
    return pl.pallas_call(
        last_kernel,
        in_specs=[SMEM_SPEC] + [VMEM_SPEC] * 7,
        out_specs=[VMEM_SPEC] * 2,
        out_shape=[shaped(TOK_DEV, D), shaped(TOK_DEV, D, kind=F32)],
        compiler_params=params(),
        cost_estimate=cost(1e9),
        name="last",
    )(place, tok, grad, keep_out, got_out, keep_in, got_in, bias)


def partner(chip, dim):
    step = 4 ** (dim % 3)
    at = (chip // step) % 4
    return chip + ((at ^ 1 if dim < 3 else 3 - at) - at) * step


def side_of(chip, dim):
    at = (chip // (4 ** (dim % 3))) % 4
    return (at ^ (at // 2)) & 1 if dim < 3 else at // 2


def first_dims(axis):
    return [(r * 2 + s, partner(r, axis + 3 * s) * 2 + s) for r in range(64) for s in range(2)]


def second_dims(axis):
    return [(r * 2 + s, partner(r, axis + 3 * (1 - s)) * 2 + s) for r in range(64) for s in range(2)]


def first_side(axis):
    chip, core = lax.axis_index("replica"), lax.axis_index("shard")
    return jnp.where(core == 0, side_of(chip, axis), side_of(chip, axis + 3))


def cubes():
    groups = {}
    for r in range(64):
        for s in range(2):
            fixed = tuple(side_of(r, a + 3 * (1 - s)) for a in range(3))
            place = sum(side_of(r, a + 3 * s) << (2 - a) for a in range(3))
            groups.setdefault((s, fixed), [0] * 8)[place] = r * 2 + s
    return list(groups.values())


def add_low(left, right):
    return (left.astype(F32) + right.astype(F32)).astype(BF16)


def halves(part, axis):
    side = first_side(axis)
    send = lax.dynamic_slice_in_dim(part, 1 - side, 1, axis)
    keep = lax.dynamic_slice_in_dim(part, side, 1, axis)
    return send, keep


def scatter_start(parts, k):
    cut = [halves(part, (c + k) % 3) for c, part in enumerate(parts)]
    got = [lax.ppermute(send, BOTH, first_dims((c + k) % 3)) for c, (send, _) in enumerate(cut)]
    return [send for send, _ in cut], [keep for _, keep in cut], got


def scatter_end(keeps, got):
    return [add_low(a, b) for a, b in zip(keeps, got)]


def gather_step(parts, k, rider):
    out = []
    for c, part in enumerate(parts):
        axis = (c + k) % 3
        if c == 0 and rider is not None:
            flat = part.reshape(-1, D)
            got = lax.ppermute(jnp.concatenate([flat, rider], axis=0), BOTH, first_dims(axis))
            rider = add_low(rider, got[flat.shape[0]:])
            got = got[:flat.shape[0]].reshape(part.shape)
        else:
            got = lax.ppermute(part, BOTH, first_dims(axis))
        side = first_side(axis)
        out.append(jnp.concatenate([jnp.where(side == 0, part, got), jnp.where(side == 0, got, part)], axis=axis))
    return out, rider


def on_device(tokens, lengths, project_weight, project_bias, dense_weight, dense_bias, expand_weight, expand_bias,
              contract_weight, contract_bias, first_gain, first_shift, second_gain, second_shift, out_grad):
    core = lax.axis_index("shard")
    swap = lambda rows: lax.ppermute(rows, "shard", [(0, 1), (1, 0)])
    both = lambda mine, got: (jnp.where(core == 0, mine, got), jnp.where(core == 0, got, mine))
    join = lambda mine, got, axis: jnp.concatenate(both(mine, got), axis=axis)
    pick = lambda rows, index, axis: lax.dynamic_index_in_dim(rows, index, axis, keepdims=False)

    place = jnp.stack([core.astype(jnp.int32), lengths[0]])
    other_tokens = swap(tokens)
    other_grad = swap(out_grad)
    small = jnp.concatenate([project_bias, dense_bias, contract_bias, first_gain, first_shift, second_gain, second_shift])
    other_small = swap(small)
    expand = expand_weight.reshape(OWN_D, 2, OWN_FF)
    other_expand = swap(pick(expand, 1 - core, 1))
    project = project_weight.reshape(OWN_D, 3, 2, OWN_D)
    other_project = swap(pick(project, 1 - core, 2).reshape(OWN_D, 3 * OWN_D))

    low, high = both(small, other_small)
    b_project = jnp.concatenate([low[:1152], high[:1152]]).reshape(3, 2, OWN_D)
    b_project = pick(b_project, core, 1).reshape(1, 3 * OWN_D)
    rest = jnp.stack([low[1152:].reshape(6, OWN_D), high[1152:].reshape(6, OWN_D)], axis=1).reshape(6, D).astype(F32)
    bias, vec = rest[:2], rest[2:]

    n1, n1t, n2, n2t, seed, tok, seed_sum = prep(place, tokens, other_tokens, out_grad, other_grad, vec)
    w_expand = join(pick(expand, core, 1), other_expand, 0)
    gc, ge, gbe, mlp, q2 = ffn(n2, n2t, seed, w_expand, expand_bias.reshape(1, OWN_FF), contract_weight)

    ge = ge.reshape(2, OWN_D, OWN_FF)
    other_ge = swap(pick(ge, 1 - core, 0))
    blocks = [b[:, i * D:(i + 1) * D] for b in both(pick(ge, core, 0), other_ge) for i in range(2)]
    unit = jnp.concatenate([gc] + blocks, axis=0)
    parts = [unit[c * 1024:(c + 1) * 1024].reshape(2, 2, 2, 128, D) for c in range(3)]

    w_project = join(pick(project, core, 2).reshape(OWN_D, 3 * OWN_D), other_project, 0)
    tables = [jnp.asarray(t) for t in rotary_arrays()]

    sends, keeps, got = scatter_start(parts, 0)
    qkvc = heads(n1, seed, tables, w_project, b_project, dense_weight, sends)
    pieces = []
    parts = scatter_end(keeps, got)
    sends, keeps, got = scatter_start(parts, 1)
    piece = attend(0, 0, qkvc, tables, [], sends)
    parts = scatter_end(keeps, got)
    sends, keeps, got = scatter_start(parts, 2)
    piece = attend(0, 1, qkvc, tables, piece, sends)
    pieces += piece
    parts = scatter_end(keeps, got)
    block = jnp.concatenate([p.reshape(128, D) for p in parts], axis=0)
    for axis in range(3):
        got = lax.ppermute(block, BOTH, second_dims(axis))
        piece = attend(1 + axis // 2, axis % 2, qkvc, tables, piece if axis == 1 else [], [block])
        if axis == 1:
            pieces += piece
        block = add_low(block, got)
    piece = attend(2, 1, qkvc, tables, piece, [block])
    pieces += piece
    ffn_sum = lax.all_gather(block.reshape(3, 128, D), BOTH, axis=0, tiled=False, axis_index_groups=cubes())
    ffn_sum = ffn_sum.transpose(1, 0, 2, 3).reshape(2 * OWN_FF, D).astype(F32)

    gw, gd, gb = weights(n1t, seed, pieces)
    gw = gw.reshape(2, OWN_D, 3 * OWN_D)
    other_gw = swap(pick(gw, 1 - core, 0))
    first, second = both(pick(gw, core, 0), other_gw)
    blocks = [jnp.concatenate([h[:, t * OWN_D:(t + 1) * OWN_D] for h in (first, second)], axis=1) for t in range(3)]
    unit = jnp.concatenate(blocks + [gd], axis=0)
    parts = [unit[c * 512:(c + 1) * 512].reshape(2, 2, 2, 64, D) for c in range(3)]
    for k in range(3):
        sends, keeps, got = scatter_start(parts, k)
        parts = scatter_end(keeps, got)

    keep_out, send_out, keep_in, send_in, sums = tail(place, tok, mlp, q2, w_project, dense_weight, vec, pieces)
    outputs, input_grad = last(place, tokens, out_grad, keep_out, swap(send_out), keep_in, swap(send_in), bias)
    vectors = jnp.concatenate([gb.reshape(-1), sums.reshape(-1)])
    other_vectors = swap(vectors)
    gb_low, gb_high = both(vectors[:1152], other_vectors[:1152])
    gb_all = jnp.stack([gb_low.reshape(3, OWN_D), gb_high.reshape(3, OWN_D)], axis=1).reshape(2, 1152)
    gains = (vectors[1152:] + other_vectors[1152:]).reshape(4, 2, OWN_D)
    rider = jnp.concatenate([
        pick(gb_all, core, 0), gbe.reshape(-1), pick(seed_sum.reshape(2, OWN_D), core, 0),
        pick(gains, core, 1).reshape(-1), jnp.zeros((2 * D,), F32),
    ]).reshape(8, D).astype(BF16)

    block = jnp.concatenate([p.reshape(64, D) for p in parts] + [rider], axis=0)
    for axis in range(3):
        block = add_low(block, lax.ppermute(block, BOTH, second_dims(axis)))
    parts = [block[c * 64:(c + 1) * 64].reshape(1, 1, 1, 64, D) for c in range(3)]
    rider = block[192:]
    for k in (2, 1, 0):
        parts, rider = gather_step(parts, k, rider)
    attn_sum = jnp.concatenate([p.reshape(512, D) for p in parts], axis=0).astype(F32)
    small_sum = rider.reshape(-1).astype(F32)
    bias_grad = small_sum[2688:3072]
    gain_grads = small_sum[3072:4608].reshape(4, OWN_D)

    expand_blocks = ffn_sum[OWN_FF:].reshape(4, OWN_D, D)
    return (
        outputs,
        input_grad,
        jnp.concatenate([attn_sum[t * OWN_D:(t + 1) * OWN_D] for t in range(3)], axis=1),
        small_sum[:1152],
        attn_sum[3 * OWN_D:],
        bias_grad,
        jnp.concatenate([expand_blocks[i] for i in range(4)], axis=1),
        small_sum[1152:2688],
        ffn_sum[:OWN_FF],
        bias_grad,
        gain_grads[0],
        gain_grads[1],
        gain_grads[2],
        gain_grads[3],
    )


def solution(mesh):
    rows, first = P(("replica", "shard"), None), P("shard", None)
    one = P("shard")
    return jax.shard_map(
        on_device,
        mesh=mesh,
        in_specs=(rows, P("replica"), first, one, first, one, first, one, first, one, one, one, one, one, rows),
        out_specs=(rows, rows, first, one, first, one, first, one, first, one, one, one, one, one),
        check_vma=False,
    )
```

```python
import jax
import jax.numpy as jnp
import numpy as np
from jax import lax
from jax.experimental import pallas as pl
from jax.experimental.pallas import tpu as pltpu
from jax.sharding import PartitionSpec as P

HEADS = 12
HEAD_DIM = 64
D = 768
ROT = 16
FF = 3072
SEQ = 1024
TOK_DEV = 512
EPSILON = 1e-05
SCORE_SCALE = 0.125
F32 = jnp.float32
BF16 = jnp.bfloat16
MIB = 1024 * 1024
OWN_FF = FF // 2
OWN_D = D // 2
PAIR = 2 * HEAD_DIM
PAIRS = OWN_D // PAIR
HIDDEN_BLOCK = 256
CHUNK = 256
CHUNKS = SEQ // CHUNK
BOTH = ("replica", "shard")


def product(left, right):
    return lax.dot_general(left, right, (((1,), (0,)), ((), ())), preferred_element_type=F32)


def product_nt(left, right):
    return lax.dot_general(left, right, (((1,), (1,)), ((), ())), preferred_element_type=F32)


def product_tn(left, right):
    return lax.dot_general(left, right, (((0,), (0,)), ((), ())), preferred_element_type=F32)


def chunk_rows(c):
    return slice(c * CHUNK, (c + 1) * CHUNK)


def params(mib, **kw):
    return pltpu.CompilerParams(vmem_limit_bytes=mib * MIB, **kw)


def cost(flops, size=8 << 20, exps=0):
    return pl.CostEstimate(flops=int(flops), bytes_accessed=int(size), transcendentals=int(exps))


VMEM_SPEC = pl.BlockSpec(memory_space=pltpu.VMEM)
SMEM_SPEC = pl.BlockSpec(memory_space=pltpu.SMEM)
ANY_SPEC = pl.BlockSpec(memory_space=pl.ANY)


def shaped(*dims, kind=BF16):
    return jax.ShapeDtypeStruct(dims, kind)


def standardise(rows):
    mean = jnp.mean(rows, axis=-1, keepdims=True)
    centered = rows - mean
    scale = lax.rsqrt(jnp.mean(centered * centered, axis=-1, keepdims=True) + EPSILON)
    return centered * scale, scale


def whole(*dims):
    return pl.BlockSpec(dims, lambda *i: (0,) * len(dims))


def pack_kernel(project_ref, *refs):
    out_ref, expand_out = refs[-2:]
    expand_out[...] = refs[-3][...].astype(F32).reshape(1, OWN_FF)
    for t in range(3):
        out_ref[t:t + 1, :] = project_ref[t * OWN_D:(t + 1) * OWN_D].astype(F32).reshape(1, OWN_D)
    for i, ref in enumerate(refs[:-3]):
        out_ref[3 + i:4 + i, :] = ref[...].astype(F32).reshape(1, OWN_D)


def pack(*vectors):
    return pl.pallas_call(
        pack_kernel,
        grid=(1,),
        in_specs=[whole(v.shape[0]) for v in vectors],
        out_specs=[whole(16, OWN_D), whole(1, OWN_FF)],
        out_shape=[shaped(16, OWN_D, kind=F32), shaped(1, OWN_FF, kind=F32)],
        compiler_params=params(60, dimension_semantics=("arbitrary",)),
        cost_estimate=cost(1e5, 1 << 16),
        name="pack",
    )(*vectors)


def prep_kernel(place_ref, mine_ref, other_ref, grad_ref, other_grad_ref, pack_ref, other_pack_ref,
                n1_ref, n2_ref, seed_ref, tok_ref, sum_ref, head_bias_ref, vec_ref):
    side = place_ref[0]
    length = place_ref[1]
    first = jnp.where(side == 0, pack_ref[...], other_pack_ref[...])
    second = jnp.where(side == 0, other_pack_ref[...], pack_ref[...])
    for t in range(3):
        blocks = [half[row % 3:row % 3 + 1, :] for row in (2 * t, 2 * t + 1) for half in ((first, second)[row // 3],)]
        head_bias_ref[:, t * OWN_D:(t + 1) * OWN_D] = jnp.where(side == 0, blocks[0], blocks[1])
    full = [jnp.concatenate([first[r:r + 1, :], second[r:r + 1, :]], axis=1) for r in range(3, 9)]
    vec_ref[0:1, :] = full[0] + full[1]
    vec_ref[1:2, :] = full[2]
    vec_ref[2:3, :] = full[4]
    step = pl.program_id(0)
    own = step // 2 == side
    low = jnp.where(own, mine_ref[...], other_ref[...])
    tok_ref[...] = low
    normal, _ = standardise(low.astype(F32))
    n1_ref[...] = (normal * full[2] + full[3]).astype(BF16)
    n2_ref[...] = (normal * full[4] + full[5]).astype(BF16)
    position = step * CHUNK + lax.broadcasted_iota(jnp.int32, (CHUNK, D), 0)
    cot = jnp.where(own, grad_ref[...], other_grad_ref[...])
    seed = jnp.where(position < length, cot.astype(F32), 0.0)
    seed_ref[...] = seed.astype(BF16)

    @pl.when(step == 0)
    def _():
        sum_ref[...] = jnp.zeros_like(sum_ref)

    sum_ref[...] += jnp.sum(seed, axis=0, keepdims=True)


def prep(place, mine, other, grad, other_grad, packed, other_packed):
    return pl.pallas_call(
        prep_kernel,
        grid=(CHUNKS,),
        in_specs=[SMEM_SPEC] + [pl.BlockSpec((CHUNK, D), lambda i: (i % 2, 0))] * 4 + [whole(16, OWN_D)] * 2,
        out_specs=[pl.BlockSpec((CHUNK, D), lambda i: (i, 0))] * 4 + [whole(1, D), whole(1, 3 * OWN_D), whole(8, D)],
        out_shape=[shaped(SEQ, D)] * 4 + [shaped(1, D, kind=F32), shaped(1, 3 * OWN_D, kind=F32), shaped(8, D, kind=F32)],
        compiler_params=params(60, dimension_semantics=("arbitrary",)),
        cost_estimate=cost(4e9),
        name="prep",
    )(place, mine, other, grad, other_grad, packed, other_packed)


def gelu_pair(hidden):
    size = jnp.abs(hidden)
    near = 1.0 / (1.0 + (0.3275911 * 0.7071067811865476) * size)
    bell = jnp.exp(-0.5 * hidden * hidden)
    poly = 0.5 * 1.061405429 * near - 0.5 * 1.453152027
    poly = poly * near + 0.5 * 1.421413741
    poly = poly * near - 0.5 * 0.284496736
    poly = poly * near + 0.5 * 0.254829592
    tail = poly * near * bell
    phi = jnp.where(hidden >= 0, 1.0 - tail, tail)
    return hidden * phi, phi + hidden * bell * 0.3989422804014327


def ffn_kernel(place_ref, n2_ref, seed_ref, mine_ref, other_ref, be_ref, wc_ref,
               gc0_ref, gc1_ref, gc2_ref, keep0_ref, keep1_ref, send0_ref, send1_ref, gbe_ref, act_ref, gh_ref, we_ref,
               n2t_ref):
    step = pl.program_id(0)

    @pl.when(step == 0)
    def _():
        for c in range(CHUNKS):
            rows = chunk_rows(c)
            n2t_ref[:, rows] = n2_ref[rows, :].T

    start = pl.multiple_of(place_ref[0] * OWN_D, OWN_D)
    we_ref[pl.ds(start, OWN_D), :] = mine_ref[...]
    we_ref[pl.ds(OWN_D - start, OWN_D), :] = other_ref[...]
    bias = be_ref[...]
    total = jnp.zeros((1, HIDDEN_BLOCK), F32)
    for c in range(CHUNKS):
        rows = chunk_rows(c)
        hidden = product(n2_ref[rows, :], we_ref[...]) + bias
        value, slope = gelu_pair(hidden)
        act_ref[rows, :] = value.astype(BF16)
        gh = (product_nt(seed_ref[rows, :], wc_ref[...]) * slope).astype(BF16)
        gh_ref[rows, :] = gh
        total += jnp.sum(gh.astype(F32), axis=0, keepdims=True)
    gbe_ref[...] = total
    gc = product_tn(act_ref[...], seed_ref[...]).astype(BF16)

    keep = product(n2t_ref[pl.ds(start, OWN_D), :], gh_ref[...]).astype(BF16)
    send = product(n2t_ref[pl.ds(OWN_D - start, OWN_D), :], gh_ref[...]).astype(BF16)
    for low, high, ref in ((0, 2, gc0_ref), (2, 4, gc1_ref), (4, 6, gc2_ref)):
        @pl.when((step >= low) & (step < high))
        def _(ref=ref):
            ref[...] = gc

    for low, high, ref, value in ((0, 4, keep0_ref, keep), (4, 6, keep1_ref, keep), (0, 2, send0_ref, send), (2, 6, send1_ref, send)):
        @pl.when((step >= low) & (step < high))
        def _(ref=ref, value=value):
            for g in range(3):
                ref[:, g * HIDDEN_BLOCK:(g + 1) * HIDDEN_BLOCK] = value[g * 128:(g + 1) * 128, :]


def ffn(place, n2, seed, mine, other, be, wc):
    steps = OWN_FF // HIDDEN_BLOCK
    rows_block = pl.BlockSpec((HIDDEN_BLOCK, D), lambda i, at: (i, 0))
    cols_block = pl.BlockSpec((OWN_D, HIDDEN_BLOCK), lambda i, at: (0, at[0] * steps + i))
    bias_block = pl.BlockSpec((1, HIDDEN_BLOCK), lambda i, at: (0, i))
    part = lambda rows, low, high: pl.BlockSpec((rows, D), lambda i, at: (jnp.clip(i, low, high - 1) - low, 0))
    tall_block = pl.BlockSpec((SEQ, HIDDEN_BLOCK), lambda i, at: (0, i))
    return pl.pallas_call(
        ffn_kernel,
        grid_spec=pltpu.PrefetchScalarGridSpec(
            num_scalar_prefetch=1,
            grid=(steps,),
            in_specs=[whole(SEQ, D), whole(SEQ, D), cols_block, cols_block, bias_block, rows_block],
            out_specs=[part(HIDDEN_BLOCK, 0, 2), part(HIDDEN_BLOCK, 2, 4), part(HIDDEN_BLOCK, 4, 6),
                       part(128, 0, 4), part(128, 4, 6), part(128, 0, 2), part(128, 2, 6), bias_block, tall_block, tall_block,
                       pl.BlockSpec((D, HIDDEN_BLOCK), lambda i, at: (0, i))],
            scratch_shapes=[pltpu.VMEM((D, SEQ), BF16)],
        ),
        out_shape=[shaped(512, D)] * 4 + [shaped(256, D)] * 2 + [shaped(512, D), shaped(1, OWN_FF, kind=F32),
                   shaped(SEQ, OWN_FF), shaped(SEQ, OWN_FF), shaped(D, OWN_FF)],
        compiler_params=params(60, dimension_semantics=("arbitrary",)),
        cost_estimate=cost(8 * SEQ * D * OWN_FF, 20 << 20, 2 * SEQ * OWN_FF),
        name="ffn",
    )(place, n2, seed, mine, other, be, wc)


def merge_kernel(act_ref, gh_ref, we_ref, wc_ref, *refs):
    mlp_ref, q2_ref = refs[-2:]
    mlp_ref[...] = product(act_ref[...], wc_ref[...])
    q2_ref[...] = product_nt(gh_ref[...], we_ref[...])


def merge(half, act, gh, we, wc, held, after):
    rows = lambda cols: pl.BlockSpec((CHUNK, cols), lambda i: (2 * half + i, 0))
    return pl.pallas_call(
        merge_kernel,
        grid=(2,),
        in_specs=[rows(OWN_FF), rows(OWN_FF), whole(D, OWN_FF), whole(OWN_FF, D)] + [ANY_SPEC] * (len(held) + len(after)),
        out_specs=[rows(D), rows(D)],
        out_shape=[shaped(SEQ, D, kind=F32)] * 2,
        input_output_aliases={4: 0, 5: 1} if held else {},
        compiler_params=params(28, dimension_semantics=("arbitrary",)),
        cost_estimate=cost(2 * SEQ * D * OWN_FF),
        name="merge",
    )(act, gh, we, wc, *held, *after)


def rotary_arrays():
    frequency = (np.float32(10000.0) ** (-np.arange(0, ROT, 2, dtype=np.float32) / np.float32(ROT))).astype(np.float32)
    angles = (np.arange(SEQ, dtype=np.float32)[:, None] * frequency[None, :]).astype(np.float64)
    cos, sin = np.cos(angles), np.sin(angles)
    half = ROT // 2
    keep = np.ones((SEQ, HEAD_DIM))
    up = np.zeros((SEQ, HEAD_DIM))
    down = np.zeros((SEQ, HEAD_DIM))
    keep[:, :half] = cos
    keep[:, half:ROT] = cos
    down[:, :half] = -sin
    up[:, half:ROT] = sin
    return [np.tile(t, (1, 2)).astype(np.float32) for t in (keep, up, down)]


def turn(rows, keep, up, down):
    return rows * keep + pltpu.roll(rows, ROT // 2, 1) * up + pltpu.roll(rows, PAIR - ROT // 2, 1) * down


def heads_kernel(place_ref, n1_ref, seed_ref, keep_ref, up_ref, down_ref, mine_ref, other_ref, bp_ref, wd_ref, *rest):
    q_ref, k_ref, v_ref, c_ref, wp_ref = rest[-5:]

    @pl.when(pl.program_id(0) == 0)
    def _():
        start = pl.multiple_of(place_ref[0] * OWN_D, OWN_D)
        for t in range(3):
            cols = pl.ds(pl.multiple_of(start + t * D, 128), OWN_D)
            wp_ref[pl.ds(start, OWN_D), t * OWN_D:(t + 1) * OWN_D] = mine_ref[:, cols]
            wp_ref[pl.ds(OWN_D - start, OWN_D), t * OWN_D:(t + 1) * OWN_D] = other_ref[:, cols]

    packed = product(n1_ref[...], wp_ref[...]) + bp_ref[...]
    tables = keep_ref[...], up_ref[...], down_ref[...]
    for p in range(PAIRS):
        cols = slice(p * PAIR, (p + 1) * PAIR)
        q = packed[:, p * PAIR:(p + 1) * PAIR]
        k = packed[:, OWN_D + p * PAIR:OWN_D + (p + 1) * PAIR]
        q_ref[:, cols] = (turn(q, *tables).astype(BF16) * SCORE_SCALE).astype(BF16)
        k_ref[:, cols] = turn(k, *tables).astype(BF16)
    v_ref[...] = packed[:, 2 * OWN_D:].astype(BF16)
    c_ref[...] = product_nt(seed_ref[...], wd_ref[...]).astype(BF16)


def by_rows(columns):
    return pl.BlockSpec((CHUNK, columns), lambda i, *at: (i, 0))


def heads(place, n1, seed, tables, mine, other, bp, wd, after):
    return pl.pallas_call(
        heads_kernel,
        grid=(CHUNKS,),
        in_specs=[SMEM_SPEC] + [by_rows(D)] * 2 + [by_rows(PAIR)] * 3
        + [whole(OWN_D, 3 * D), whole(OWN_D, 3 * D), whole(1, 3 * OWN_D), whole(OWN_D, D)] + [ANY_SPEC] * len(after),
        out_specs=[by_rows(OWN_D)] * 4 + [whole(D, 3 * OWN_D)],
        out_shape=[shaped(SEQ, OWN_D)] * 4 + [shaped(D, 3 * OWN_D)],
        compiler_params=params(28, dimension_semantics=("arbitrary",)),
        cost_estimate=cost(2 * SEQ * D * 4 * OWN_D),
        name="heads",
    )(place, n1, seed, *tables, mine, other, bp, wd, *after)


def attend_kernel(head, *refs):
    q_ref, k_ref, v_ref, c_ref, keep_ref, up_ref, down_ref = refs[:7]
    before_ref = refs[7]
    out_ref, done_ref, dk_s, dv_s = refs[-4:]
    done_ref[...] = jnp.zeros_like(done_ref)
    lane = lax.broadcasted_iota(jnp.int32, (CHUNK, PAIR), 1)
    mine = (lane < HEAD_DIM) if head == 0 else (lane >= HEAD_DIM)
    diagonal = lax.broadcasted_iota(jnp.int32, (CHUNK, CHUNK), 0) >= lax.broadcasted_iota(jnp.int32, (CHUNK, CHUNK), 1)

    def put(at, rows, value):
        low = value.astype(BF16)
        out_ref[at, rows, :] = low if head == 0 else jnp.where(mine, low, before_ref[at, rows, :])

    for c in reversed(range(CHUNKS)):
        rows = chunk_rows(c)
        span = (c + 1) * CHUNK
        q = jnp.where(mine, q_ref[rows, :], 0)
        gc = jnp.where(mine, c_ref[rows, :], 0)
        scores = jnp.where(diagonal, product_nt(q, k_ref[c * CHUNK:span, :]), -1e30)
        if c > 0:
            scores = jnp.concatenate([product_nt(q, k_ref[:c * CHUNK, :]), scores], axis=1)
        top = jnp.max(scores, axis=1, keepdims=True)
        power = jnp.exp(scores - top)
        inverse = 1.0 / jnp.sum(power, axis=1, keepdims=True)
        power_low = power.astype(BF16)
        ctx = jnp.where(mine, product(power_low, v_ref[:span, :]), 0.0) * inverse
        put(0, rows, ctx)
        gc_scaled = (gc.astype(F32) * inverse).astype(BF16)
        delta = jnp.sum(ctx * gc_scaled.astype(F32), axis=1, keepdims=True)
        grad_prob = product_nt(gc_scaled, v_ref[:span, :])
        grad_scores = (power * (grad_prob - delta)).astype(BF16)
        back = keep_ref[rows, :], -up_ref[rows, :], -down_ref[rows, :]
        grad_q = jnp.where(mine, product(grad_scores, k_ref[:span, :]), 0.0) * SCORE_SCALE
        put(1, rows, turn(grad_q, *back))
        dv = product_tn(power_low, gc_scaled)
        dk = product_tn(grad_scores, q)
        if c == CHUNKS - 1:
            dv_s[...] = dv
            dk_s[...] = dk
        else:
            dv_s[:span, :] += dv
            dk_s[:span, :] += dk
    for c in range(CHUNKS):
        rows = chunk_rows(c)
        back = keep_ref[rows, :], -up_ref[rows, :], -down_ref[rows, :]
        put(2, rows, turn(dk_s[rows, :], *back))
        put(3, rows, dv_s[rows, :])


def attend(pair, head, qkvc, tables, pieces, after):
    def kernel(*refs):
        attend_kernel(head, *refs)

    spec = pl.BlockSpec((SEQ, PAIR), lambda i: (0, pair))
    block = pl.BlockSpec((4, SEQ, PAIR), lambda i: (0, 0, pair))
    first = pieces is None
    held = [] if first else [pieces]
    return pl.pallas_call(
        kernel,
        grid=(1,),
        in_specs=[spec] * 4 + [whole(SEQ, PAIR)] * 3 + ([] if first else [block if head == 1 else ANY_SPEC]) + [ANY_SPEC] * len(after),
        out_specs=[block, whole(1, 128)],
        out_shape=[shaped(4, SEQ, OWN_D), shaped(1, 128, kind=F32)],
        input_output_aliases={} if first else {7: 0},
        scratch_shapes=[pltpu.VMEM((SEQ, PAIR), F32)] * 2,
        compiler_params=params(28, dimension_semantics=("arbitrary",)),
        cost_estimate=cost(5e9, 4 << 20, SEQ * SEQ),
        name="attend",
    )(*qkvc, *tables, *held, *after)


def weights_kernel(place_ref, n1_ref, seed_ref, piece_ref, *refs):
    low_ref, mid_ref, send0_ref, send1_ref, gb_ref, done_ref, n1t_ref = refs[-7:]
    done_ref[...] = jnp.zeros_like(done_ref)
    step = pl.program_id(0)
    half = OWN_D // 2

    @pl.when(step == 0)
    def _():
        low_ref[:OWN_D, :] = product_tn(piece_ref[0], seed_ref[...]).astype(BF16)
        for c in range(CHUNKS):
            rows = chunk_rows(c)
            n1t_ref[:, rows] = n1_ref[rows, :].T

    for t in range(3):
        @pl.when(step == t + 1)
        def _(t=t):
            start = pl.multiple_of(place_ref[0] * OWN_D, OWN_D)
            grads = piece_ref[0]
            for refs, cut, at in (((send0_ref, send1_ref), 64, OWN_D - start), ((low_ref, mid_ref), 128, start)):
                full = product(n1t_ref[pl.ds(at, OWN_D), :], grads).astype(BF16)
                first = t * half
                for ref, low, high, shift in ((refs[0], 0, cut, OWN_D if cut == 128 else 0), (refs[1], cut, 3 * half, -cut)):
                    a, b = max(first, low), min(first + half, high)
                    if a < b:
                        ref[a + shift:b + shift, :OWN_D] = full[a - first:b - first]
                        ref[a + shift:b + shift, OWN_D:] = full[half + a - first:half + b - first]
            gb_ref[0] = jnp.sum(grads.astype(F32), axis=0, keepdims=True)


def weights(place, n1, seed, pieces, after):
    return pl.pallas_call(
        weights_kernel,
        grid=(4,),
        in_specs=[SMEM_SPEC, whole(SEQ, D), whole(SEQ, D), pl.BlockSpec((1, SEQ, OWN_D), lambda i: (i, 0, 0))]
        + [ANY_SPEC] * len(after),
        out_specs=[whole(512, D), whole(448, D), whole(64, D), whole(512, D),
                   pl.BlockSpec((1, 1, OWN_D), lambda i: (jnp.maximum(i - 1, 0), 0, 0)), whole(1, 128)],
        out_shape=[shaped(512, D), shaped(448, D), shaped(64, D), shaped(512, D), shaped(3, 1, OWN_D, kind=F32),
                   shaped(1, 128, kind=F32)],
        scratch_shapes=[pltpu.VMEM((D, SEQ), BF16)],
        compiler_params=params(28, dimension_semantics=("arbitrary",)),
        cost_estimate=cost(2 * SEQ * D * 4 * OWN_D),
        name="weights",
    )(place, n1, seed, pieces, *after)


def tail_kernel(place_ref, tok_ref, mlp_ref, q2_ref, wp_ref, wd_ref, vec_ref, gb_ref, piece_ref, *refs):
    keep_out, send_out, keep_in, send_in, sums_ref, done_ref = refs[-6:]
    done_ref[...] = jnp.zeros_like(done_ref)
    step = pl.program_id(0)
    grads = jnp.concatenate([piece_ref[t] for t in (1, 2, 3)], axis=1)
    out = mlp_ref[...] + product(piece_ref[0], wd_ref[...])
    q1 = product_nt(grads, wp_ref[...])
    q2 = q2_ref[...]
    normal, _ = standardise(tok_ref[...].astype(F32))
    sums = jnp.concatenate([jnp.sum(term, axis=0, keepdims=True) for term in (q1 * normal, q1, q2 * normal, q2)], axis=0)
    mixed = q1 * vec_ref[1:2, :] + q2 * vec_ref[2:3, :]

    @pl.when(step < CHUNKS // 2)
    def _():
        send_out[...] = out.astype(BF16)
        send_in[...] = mixed.astype(BF16)

    @pl.when(step >= CHUNKS // 2)
    def _():
        keep_out[...] = out
        keep_in[...] = mixed

    @pl.when(step == 0)
    def _():
        sums_ref[0:4, :] = sums
        for t in range(3):
            sums_ref[4 + t:5 + t, :OWN_D] = gb_ref[t]
            sums_ref[4 + t:5 + t, OWN_D:] = gb_ref[t]

    @pl.when(step > 0)
    def _():
        sums_ref[0:4, :] += sums


def tail(place, tok, mlp, q2, wp, wd, vec, gb, pieces, after):
    half = CHUNKS // 2
    rows = lambda cols: pl.BlockSpec((CHUNK, cols), lambda i, at: ((i + half * (1 - at[0])) % CHUNKS, 0))
    still = lambda *dims: pl.BlockSpec(dims, lambda i, at: (0,) * len(dims))
    sent = pl.BlockSpec((CHUNK, D), lambda i, at: (jnp.minimum(i, half - 1), 0))
    kept = pl.BlockSpec((CHUNK, D), lambda i, at: (jnp.maximum(i - half, 0), 0))
    return pl.pallas_call(
        tail_kernel,
        grid_spec=pltpu.PrefetchScalarGridSpec(
            num_scalar_prefetch=1,
            grid=(CHUNKS,),
            in_specs=[rows(D)] * 3 + [still(D, 3 * OWN_D), still(OWN_D, D), still(8, D), still(3, 1, OWN_D)]
            + [pl.BlockSpec((4, CHUNK, OWN_D), lambda i, at: (0, (i + half * (1 - at[0])) % CHUNKS, 0))]
            + [ANY_SPEC] * len(after),
            out_specs=[kept, sent, kept, sent, still(8, D), still(1, 128)],
        ),
        out_shape=[shaped(TOK_DEV, D, kind=F32), shaped(TOK_DEV, D), shaped(TOK_DEV, D, kind=F32), shaped(TOK_DEV, D),
                   shaped(8, D, kind=F32), shaped(1, 128, kind=F32)],
        compiler_params=params(28, dimension_semantics=("arbitrary",)),
        cost_estimate=cost(2 * SEQ * D * 4 * OWN_D, 16 << 20),
        name="tail",
    )(place, tok, mlp, q2, wp, wd, vec, gb, pieces, *after)


def last_kernel(place_ref, tok_ref, grad_ref, keep_out, got_out, keep_in, got_in, vec_ref, *refs):
    out_ref, in_ref = refs[-2:]
    tok = tok_ref[...].astype(F32)
    out_ref[...] = (tok + keep_out[...] + got_out[...].astype(F32) + vec_ref[0:1, :]).astype(BF16)
    normal, scale = standardise(tok)
    mixed = keep_in[...] + got_in[...].astype(F32)
    base = place_ref[0] * TOK_DEV + pl.program_id(0) * CHUNK
    position = base + lax.broadcasted_iota(jnp.int32, (CHUNK, D), 0)
    seed = jnp.where(position < place_ref[1], grad_ref[...].astype(F32), 0.0)
    mean = jnp.mean(mixed, axis=-1, keepdims=True)
    along = jnp.mean(mixed * normal, axis=-1, keepdims=True)
    in_ref[...] = seed + scale * (mixed - mean - normal * along)


def last(place, tok, grad, keep_out, got_out, keep_in, got_in, vec, after):
    return pl.pallas_call(
        last_kernel,
        grid=(TOK_DEV // CHUNK,),
        in_specs=[SMEM_SPEC] + [by_rows(D)] * 6 + [whole(8, D)] + [ANY_SPEC] * len(after),
        out_specs=[by_rows(D)] * 2,
        out_shape=[shaped(TOK_DEV, D), shaped(TOK_DEV, D, kind=F32)],
        compiler_params=params(60, dimension_semantics=("arbitrary",)),
        cost_estimate=cost(1e9),
        name="last",
    )(place, tok, grad, keep_out, got_out, keep_in, got_in, vec, *after)


def rider_kernel(place_ref, mine_ref, other_ref, expand_ref, seed_ref, out_ref):
    first = place_ref[0] == 0
    mine, other = mine_ref[...], other_ref[...]
    left = jnp.where(first, mine[4:7, :OWN_D], other[4:7, :OWN_D])
    right = jnp.where(first, other[4:7, OWN_D:], mine[4:7, OWN_D:])
    out_ref[...] = jnp.concatenate([
        jnp.concatenate([left, right], axis=1), expand_ref[:, :D], expand_ref[:, D:], seed_ref[...],
        mine[0:4, :] + other[0:4, :], jnp.zeros((6, D), F32),
    ], axis=0).astype(BF16)


def make_rider(place, mine, other, expand, seed):
    return pl.pallas_call(
        rider_kernel,
        grid=(1,),
        in_specs=[SMEM_SPEC, whole(8, D), whole(8, D), whole(1, OWN_FF), whole(1, D)],
        out_specs=whole(16, D),
        out_shape=shaped(16, D),
        compiler_params=params(60, dimension_semantics=("arbitrary",)),
        cost_estimate=cost(1e5, 1 << 16),
        name="rider",
    )(place, mine, other, expand, seed)


def ordered(c, at, place_ref, held, rows):
    sides = [place_ref[2 + (c + k) % 3] for k in range(3)]
    which = 2 * c + (at // 4 ^ sides[0])
    start = ((at // 2 % 2 ^ sides[1]) * 2 + (at % 2 ^ sides[2])) * rows
    return held[which, pl.ds(pl.multiple_of(start, rows), rows), :].astype(F32)


def finish_ffn_kernel(place_ref, *refs):
    ins, (contract_out, expand_out, held, contract, expand, in_sems, out_sems) = refs[:6], refs[-7:]
    core = place_ref[0]
    loads = [pltpu.make_async_copy(ins[i], held.at[i], in_sems.at[i]) for i in range(6)]
    stores = [pltpu.make_async_copy(contract, contract_out, out_sems.at[0]),
              pltpu.make_async_copy(expand, expand_out, out_sems.at[1])]
    for load in loads:
        load.start()
    for c in range(3):
        loads[2 * c].wait()
        loads[2 * c + 1].wait()
        for at in range(8):
            value = ordered(c, at, place_ref, held, 128)
            row = c * 1024 + at * 128
            if row < OWN_FF:
                contract[row:row + 128, :] = value
            else:
                half, block = divmod((row - OWN_FF) // 128, 6)
                base = (core if half == 0 else 1 - core) * OWN_FF + block * HIDDEN_BLOCK
                for g in range(3):
                    expand[g * 128:(g + 1) * 128, pl.ds(pl.multiple_of(base, 128), HIDDEN_BLOCK)] = (
                        value[:, g * HIDDEN_BLOCK:(g + 1) * HIDDEN_BLOCK])
        if c == 1:
            stores[0].start()
    stores[1].start()
    for store in stores:
        store.wait()


def finish_ffn(place, parts):
    big = [(OWN_FF, D), (OWN_D, FF)]
    return pl.pallas_call(
        finish_ffn_kernel,
        in_specs=[SMEM_SPEC] + [ANY_SPEC] * 6,
        out_specs=[ANY_SPEC] * 2,
        out_shape=[shaped(*dims, kind=F32) for dims in big],
        scratch_shapes=[pltpu.VMEM((6, 512, D), BF16)] + [pltpu.VMEM(dims, F32) for dims in big]
        + [pltpu.SemaphoreType.DMA((6,)), pltpu.SemaphoreType.DMA((2,))],
        compiler_params=params(40),
        cost_estimate=cost(1e8, 16 << 20),
        name="finish_ffn",
    )(place, *parts)


def finish_kernel(place_ref, *refs):
    ins = refs[:6]
    rider_ref = refs[6]
    outs = refs[-14:-12]
    small = refs[-12:-5]
    held, project, dense, in_sems, out_sems = refs[-5:]
    core = place_ref[0]
    loads = [pltpu.make_async_copy(ins[i], held.at[i], in_sems.at[i]) for i in range(6)]
    stores = [pltpu.make_async_copy(stage, outs[i], out_sems.at[i]) for i, stage in enumerate((project, dense))]
    for load in loads:
        load.start()
    rows = rider_ref[...].astype(F32)
    pieces = [(0, 0, 1, 1), (0, 1, 2, 0), (1, 0, 2, 1)]
    for t, (r0, h0, r1, h1) in enumerate(pieces):
        small[0][t * OWN_D:(t + 1) * OWN_D] = jnp.where(
            core == 0, rows[r0:r0 + 1, h0 * OWN_D:(h0 + 1) * OWN_D], rows[r1:r1 + 1, h1 * OWN_D:(h1 + 1) * OWN_D]).reshape(OWN_D)
    small[1][:D] = rows[3:4, :].reshape(D)
    small[1][D:] = rows[4:5, :].reshape(D)
    for i in range(5):
        row = rows[5 + i:6 + i, :]
        small[2 + i][...] = jnp.where(core == 0, row[:, :OWN_D], row[:, OWN_D:]).reshape(OWN_D)
    for c in range(3):
        loads[2 * c].wait()
        loads[2 * c + 1].wait()
        for at in range(8):
            value = ordered(c, at, place_ref, held, 64)
            row = c * 512 + at * 64
            if row < OWN_D:
                dense[row:row + 64, :] = value
            else:
                half, row = divmod(row - OWN_D, 3 * OWN_D // 2)
                t, row = divmod(row, OWN_D // 2)
                cols = pl.ds(pl.multiple_of((core if half == 0 else 1 - core) * OWN_D + t * D, 128), OWN_D)
                project[row:row + 64, cols] = value[:, :OWN_D]
                project[OWN_D // 2 + row:OWN_D // 2 + row + 64, cols] = value[:, OWN_D:]
        if c == 0:
            stores[1].start()
    stores[0].start()
    for store in stores:
        store.wait()


def finish(place, parts, rider, after):
    big = [(OWN_D, 3 * D), (OWN_D, D)]
    vectors = [3 * OWN_D, OWN_FF] + [OWN_D] * 5
    return pl.pallas_call(
        finish_kernel,
        in_specs=[SMEM_SPEC] + [ANY_SPEC] * 6 + [VMEM_SPEC] + [ANY_SPEC] * len(after),
        out_specs=[ANY_SPEC] * 2 + [VMEM_SPEC] * 7,
        out_shape=[shaped(*dims, kind=F32) for dims in big] + [shaped(n, kind=F32) for n in vectors],
        scratch_shapes=[pltpu.VMEM((6, 256, D), BF16)] + [pltpu.VMEM(dims, F32) for dims in big]
        + [pltpu.SemaphoreType.DMA((6,)), pltpu.SemaphoreType.DMA((2,))],
        compiler_params=params(28),
        cost_estimate=cost(1e8, 8 << 20),
        name="finish",
    )(place, *parts, rider, *after)


def partner(chip, dim):
    step = 4 ** (dim % 3)
    at = (chip // step) % 4
    return chip + ((at ^ 1 if dim < 3 else 3 - at) - at) * step


def side_of(chip, dim):
    at = (chip // (4 ** (dim % 3))) % 4
    return (at ^ (at // 2)) & 1 if dim < 3 else at // 2


def first_dims(axis):
    return [(r * 2 + s, partner(r, axis + 3 * s) * 2 + s) for r in range(64) for s in range(2)]


def second_dims(axis):
    return [(r * 2 + s, partner(r, axis + 3 * (1 - s)) * 2 + s) for r in range(64) for s in range(2)]


def first_side(axis):
    chip, core = lax.axis_index("replica"), lax.axis_index("shard")
    return jnp.where(core == 0, side_of(chip, axis), side_of(chip, axis + 3))


def add_low(left, right, done=None):
    total = left.astype(F32) + right.astype(F32)
    return (total if done is None else total + done[:, :1]).astype(BF16)


def scatter_start(parts, k):
    sends, keeps, got = [], [], []
    for c, part in enumerate(parts):
        side = first_side((c + k) % 3)
        if isinstance(part, tuple):
            sends.append(jnp.where(side == 0, part[1], part[0]))
            keeps.append(jnp.where(side == 0, part[0], part[1]))
        else:
            half = part.shape[0] // 2
            sends.append(lax.dynamic_slice_in_dim(part, (1 - side) * half, half, 0))
            keeps.append(lax.dynamic_slice_in_dim(part, side * half, half, 0))
    for c, send in enumerate(sends):
        got.append(lax.ppermute(send, BOTH, first_dims((c + k) % 3)))
    return sends, keeps, got


def scatter_end(keeps, got, done=None):
    return [add_low(a, b, done) for a, b in zip(keeps, got)]


def on_device(tokens, lengths, project_weight, project_bias, dense_weight, dense_bias, expand_weight, expand_bias,
              contract_weight, contract_bias, first_gain, first_shift, second_gain, second_shift, out_grad):
    core = lax.axis_index("shard")
    swap = lambda rows: lax.ppermute(rows, "shard", [(0, 1), (1, 0)])
    place = jnp.stack([core.astype(jnp.int32), lengths[0]] + [first_side(axis).astype(jnp.int32) for axis in range(3)])
    other_tokens = swap(tokens)
    other_grad = swap(out_grad)
    packed, b_expand = pack(
        project_bias, dense_bias, contract_bias, first_gain, first_shift, second_gain, second_shift, expand_bias)
    other_packed = swap(packed)
    other_expand = swap(expand_weight)
    other_project = swap(project_weight)
    tables = [jnp.asarray(t) for t in rotary_arrays()]

    n1, n2, seed, tok, seed_sum, b_project, vec = prep(
        place, tokens, other_tokens, out_grad, other_grad, packed, other_packed)
    gc0, gc1, gc2, ge0, ge1, ge_send0, ge_send1, gbe, act, gh, w_expand = ffn(
        place, n2, seed, expand_weight, other_expand, b_expand, contract_weight)

    parts = [(gc0, gc1), (gc2, ge0), (jnp.concatenate([ge1, swap(ge_send0)], axis=0), swap(ge_send1))]

    sends, keeps, got = scatter_start(parts, 0)
    *qkvc, w_project = heads(place, n1, seed, tables, project_weight, other_project, b_project, dense_weight, sends)
    pieces, done = attend(0, 0, qkvc, tables, None, [])
    parts = scatter_end(keeps, got, done)
    sends, keeps, got = scatter_start(parts, 1)
    pieces, done = attend(0, 1, qkvc, tables, pieces, sends)
    parts = scatter_end(keeps, got, done)
    sends, keeps, got = scatter_start(parts, 2)
    pieces, done = attend(1, 0, qkvc, tables, pieces, sends)
    parts = scatter_end(keeps, got, done)
    block = jnp.concatenate(parts, axis=0)
    for axis, (pair, head) in enumerate(((1, 1), (2, 0), (2, 1))):
        got = lax.ppermute(block, BOTH, second_dims(axis))
        pieces, done = attend(pair, head, qkvc, tables, pieces, [block])
        if axis == 0:
            *merged, done = (*merge(0, act, gh, w_expand, contract_weight, [], [pieces]), done)
        if axis == 1:
            mlp, q2 = merge(1, act, gh, w_expand, contract_weight, merged, [pieces])
        if axis == 2:
            low, mid, gw_send0, gw_send1, gb, done = weights(place, n1, seed, pieces, [got])
        block = add_low(block, got, done)
    units = [low, jnp.concatenate([mid, swap(gw_send0)], axis=0), swap(gw_send1)]
    sends, keeps, late = scatter_start(units, 0)
    keep_out, send_out, keep_in, send_in, sums, done = tail(
        place, tok, mlp, q2, w_project, dense_weight, vec, gb, pieces, sends + [block])

    parts = [block[c * 128:(c + 1) * 128] for c in range(3)]
    for k in (2, 1, 0):
        got = [lax.ppermute(part, BOTH, first_dims((c + k) % 3)) for c, part in enumerate(parts)]
        if k > 0:
            parts = [jnp.concatenate(pair, axis=0) for pair in zip(parts, got)]
    contract, expand = finish_ffn(place, [a for pair in zip(parts, got) for a in pair])

    units = scatter_end(keeps, late, done)
    for k in (1, 2):
        sends, keeps, late = scatter_start(units, k)
        units = scatter_end(keeps, late)
    other_out, other_in = swap(send_out), swap(send_in)
    rider = make_rider(place, sums, swap(sums), gbe, seed_sum)

    block = jnp.concatenate(units + [rider], axis=0)
    for axis in range(3):
        block = add_low(block, lax.ppermute(block, BOTH, second_dims(axis)))
    rider = block[192:]
    parts = [block[c * 64:(c + 1) * 64] for c in range(3)]
    ends = []
    for k in (2, 1, 0):
        size = parts[0].shape[0]
        sends = [jnp.concatenate([parts[0], rider], axis=0)] + parts[1:]
        late = [lax.ppermute(part, BOTH, first_dims((c + k) % 3)) for c, part in enumerate(sends)]
        rider = add_low(rider, late[0][size:])
        late[0] = late[0][:size]
        if k == 0:
            ends = [a for pair in zip(parts, late) for a in pair]
            outputs, input_grad = last(
                place, tokens, out_grad, keep_out, other_out, keep_in, other_in, vec, [sends[0]] + parts[1:])
        else:
            parts = [jnp.concatenate(pair, axis=0) for pair in zip(parts, late)]
    project, dense, g_project, g_expand, g_out, gain_one, shift_one, gain_two, shift_two = finish(
        place, ends, rider, [contract])
    return (outputs, input_grad, project, g_project, dense, g_out, expand, g_expand, contract, g_out,
            gain_one, shift_one, gain_two, shift_two)


def solution(mesh):
    rows, first = P(("replica", "shard"), None), P("shard", None)
    one = P("shard")
    return jax.shard_map(
        on_device,
        mesh=mesh,
        in_specs=(rows, P("replica"), first, one, first, one, first, one, first, one, one, one, one, one, rows),
        out_specs=(rows, rows, first, one, first, one, first, one, first, one, one, one, one, one),
        check_vma=False,
    )
```

```python
import jax
import jax.numpy as jnp
import numpy as np
from jax import lax
from jax.experimental import pallas as pl
from jax.experimental.pallas import tpu as pltpu
from jax.sharding import PartitionSpec as P

HEADS = 12
HEAD_DIM = 64
D = 768
ROT = 16
FF = 3072
SEQ = 1024
TOK_DEV = 512
EPSILON = 1e-05
SCORE_SCALE = 0.125
F32 = jnp.float32
BF16 = jnp.bfloat16
MIB = 1024 * 1024
OWN_FF = FF // 2
OWN_D = D // 2
PAIR = 2 * HEAD_DIM
PAIRS = OWN_D // PAIR
HIDDEN_BLOCK = 256
CHUNK = 256
CHUNKS = SEQ // CHUNK
BOTH = ("replica", "shard")


def product(left, right):
    return lax.dot_general(left, right, (((1,), (0,)), ((), ())), preferred_element_type=F32)


def product_nt(left, right):
    return lax.dot_general(left, right, (((1,), (1,)), ((), ())), preferred_element_type=F32)


def product_tn(left, right):
    return lax.dot_general(left, right, (((0,), (0,)), ((), ())), preferred_element_type=F32)


def chunk_rows(c):
    return slice(c * CHUNK, (c + 1) * CHUNK)


def params(mib, **kw):
    return pltpu.CompilerParams(vmem_limit_bytes=mib * MIB, **kw)


def cost(flops, size=8 << 20, exps=0):
    return pl.CostEstimate(flops=int(flops), bytes_accessed=int(size), transcendentals=int(exps))


VMEM_SPEC = pl.BlockSpec(memory_space=pltpu.VMEM)
SMEM_SPEC = pl.BlockSpec(memory_space=pltpu.SMEM)
ANY_SPEC = pl.BlockSpec(memory_space=pl.ANY)


def shaped(*dims, kind=BF16):
    return jax.ShapeDtypeStruct(dims, kind)


def standardise(rows):
    mean = jnp.mean(rows, axis=-1, keepdims=True)
    centered = rows - mean
    scale = lax.rsqrt(jnp.mean(centered * centered, axis=-1, keepdims=True) + EPSILON)
    return centered * scale, scale


def whole(*dims):
    return pl.BlockSpec(dims, lambda *i: (0,) * len(dims))


def pack_kernel(project_ref, *refs):
    out_ref, expand_out = refs[-2:]
    expand_out[...] = refs[-3][...].astype(F32).reshape(1, OWN_FF)
    for t in range(3):
        out_ref[t:t + 1, :] = project_ref[t * OWN_D:(t + 1) * OWN_D].astype(F32).reshape(1, OWN_D)
    for i, ref in enumerate(refs[:-3]):
        out_ref[3 + i:4 + i, :] = ref[...].astype(F32).reshape(1, OWN_D)


def pack(*vectors):
    return pl.pallas_call(
        pack_kernel,
        grid=(1,),
        in_specs=[whole(v.shape[0]) for v in vectors],
        out_specs=[whole(16, OWN_D), whole(1, OWN_FF)],
        out_shape=[shaped(16, OWN_D, kind=F32), shaped(1, OWN_FF, kind=F32)],
        compiler_params=params(60, dimension_semantics=("arbitrary",)),
        cost_estimate=cost(1e5, 1 << 16),
        name="pack",
    )(*vectors)


def prep_kernel(place_ref, mine_ref, other_ref, grad_ref, other_grad_ref, pack_ref, other_pack_ref,
                n1_ref, n2_ref, seed_ref, tok_ref, sum_ref, head_bias_ref, vec_ref):
    side = place_ref[0]
    length = place_ref[1]
    first = jnp.where(side == 0, pack_ref[...], other_pack_ref[...])
    second = jnp.where(side == 0, other_pack_ref[...], pack_ref[...])
    for t in range(3):
        blocks = [half[row % 3:row % 3 + 1, :] for row in (2 * t, 2 * t + 1) for half in ((first, second)[row // 3],)]
        head_bias_ref[:, t * OWN_D:(t + 1) * OWN_D] = jnp.where(side == 0, blocks[0], blocks[1])
    full = [jnp.concatenate([first[r:r + 1, :], second[r:r + 1, :]], axis=1) for r in range(3, 9)]
    vec_ref[0:1, :] = full[0] + full[1]
    vec_ref[1:2, :] = full[2]
    vec_ref[2:3, :] = full[4]
    step = pl.program_id(0)
    own = step // 2 == side
    low = jnp.where(own, mine_ref[...], other_ref[...])
    tok_ref[...] = low
    normal, _ = standardise(low.astype(F32))
    n1_ref[...] = (normal * full[2] + full[3]).astype(BF16)
    n2_ref[...] = (normal * full[4] + full[5]).astype(BF16)
    position = step * CHUNK + lax.broadcasted_iota(jnp.int32, (CHUNK, D), 0)
    cot = jnp.where(own, grad_ref[...], other_grad_ref[...])
    seed = jnp.where(position < length, cot.astype(F32), 0.0)
    seed_ref[...] = seed.astype(BF16)

    @pl.when(step == 0)
    def _():
        sum_ref[...] = jnp.zeros_like(sum_ref)

    sum_ref[...] += jnp.sum(seed, axis=0, keepdims=True)


def prep(place, mine, other, grad, other_grad, packed, other_packed):
    return pl.pallas_call(
        prep_kernel,
        grid=(CHUNKS,),
        in_specs=[SMEM_SPEC] + [pl.BlockSpec((CHUNK, D), lambda i: (i % 2, 0))] * 4 + [whole(16, OWN_D)] * 2,
        out_specs=[pl.BlockSpec((CHUNK, D), lambda i: (i, 0))] * 4 + [whole(1, D), whole(1, 3 * OWN_D), whole(8, D)],
        out_shape=[shaped(SEQ, D)] * 4 + [shaped(1, D, kind=F32), shaped(1, 3 * OWN_D, kind=F32), shaped(8, D, kind=F32)],
        compiler_params=params(60, dimension_semantics=("arbitrary",)),
        cost_estimate=cost(4e9),
        name="prep",
    )(place, mine, other, grad, other_grad, packed, other_packed)


def gelu_pair(hidden):
    size = jnp.abs(hidden)
    near = 1.0 / (1.0 + (0.3275911 * 0.7071067811865476) * size)
    bell = jnp.exp(-0.5 * hidden * hidden)
    poly = 0.5 * 1.061405429 * near - 0.5 * 1.453152027
    poly = poly * near + 0.5 * 1.421413741
    poly = poly * near - 0.5 * 0.284496736
    poly = poly * near + 0.5 * 0.254829592
    tail = poly * near * bell
    phi = jnp.where(hidden >= 0, 1.0 - tail, tail)
    return hidden * phi, phi + hidden * bell * 0.3989422804014327


def ffn_kernel(place_ref, n2_ref, seed_ref, mine_ref, other_ref, be_ref, wc_ref,
               gc0_ref, gc1_ref, gc2_ref, keep0_ref, keep1_ref, send0_ref, send1_ref, gbe_ref, act_ref, gh_ref, we_ref,
               n2t_ref):
    step = pl.program_id(0)

    @pl.when(step == 0)
    def _():
        for c in range(CHUNKS):
            rows = chunk_rows(c)
            n2t_ref[:, rows] = n2_ref[rows, :].T

    start = pl.multiple_of(place_ref[0] * OWN_D, OWN_D)
    we_ref[pl.ds(start, OWN_D), :] = mine_ref[...]
    we_ref[pl.ds(OWN_D - start, OWN_D), :] = other_ref[...]
    bias = be_ref[...]
    total = jnp.zeros((1, HIDDEN_BLOCK), F32)
    for c in range(CHUNKS):
        rows = chunk_rows(c)
        hidden = product(n2_ref[rows, :], we_ref[...]) + bias
        value, slope = gelu_pair(hidden)
        act_ref[rows, :] = value.astype(BF16)
        gh = (product_nt(seed_ref[rows, :], wc_ref[...]) * slope).astype(BF16)
        gh_ref[rows, :] = gh
        total += jnp.sum(gh.astype(F32), axis=0, keepdims=True)
    gbe_ref[...] = total
    gc = product_tn(act_ref[...], seed_ref[...]).astype(BF16)

    keep = product(n2t_ref[pl.ds(start, OWN_D), :], gh_ref[...]).astype(BF16)
    send = product(n2t_ref[pl.ds(OWN_D - start, OWN_D), :], gh_ref[...]).astype(BF16)
    for low, high, ref in ((0, 2, gc0_ref), (2, 4, gc1_ref), (4, 6, gc2_ref)):
        @pl.when((step >= low) & (step < high))
        def _(ref=ref):
            ref[...] = gc

    for low, high, ref, value in ((0, 4, keep0_ref, keep), (4, 6, keep1_ref, keep), (0, 2, send0_ref, send), (2, 6, send1_ref, send)):
        @pl.when((step >= low) & (step < high))
        def _(ref=ref, value=value):
            for g in range(3):
                ref[:, g * HIDDEN_BLOCK:(g + 1) * HIDDEN_BLOCK] = value[g * 128:(g + 1) * 128, :]


def ffn(place, n2, seed, mine, other, be, wc):
    steps = OWN_FF // HIDDEN_BLOCK
    rows_block = pl.BlockSpec((HIDDEN_BLOCK, D), lambda i, at: (i, 0))
    cols_block = pl.BlockSpec((OWN_D, HIDDEN_BLOCK), lambda i, at: (0, at[0] * steps + i))
    bias_block = pl.BlockSpec((1, HIDDEN_BLOCK), lambda i, at: (0, i))
    part = lambda rows, low, high: pl.BlockSpec((rows, D), lambda i, at: (jnp.clip(i, low, high - 1) - low, 0))
    tall_block = pl.BlockSpec((SEQ, HIDDEN_BLOCK), lambda i, at: (0, i))
    return pl.pallas_call(
        ffn_kernel,
        grid_spec=pltpu.PrefetchScalarGridSpec(
            num_scalar_prefetch=1,
            grid=(steps,),
            in_specs=[whole(SEQ, D), whole(SEQ, D), cols_block, cols_block, bias_block, rows_block],
            out_specs=[part(HIDDEN_BLOCK, 0, 2), part(HIDDEN_BLOCK, 2, 4), part(HIDDEN_BLOCK, 4, 6),
                       part(128, 0, 4), part(128, 4, 6), part(128, 0, 2), part(128, 2, 6), bias_block, tall_block, tall_block,
                       pl.BlockSpec((D, HIDDEN_BLOCK), lambda i, at: (0, i))],
            scratch_shapes=[pltpu.VMEM((D, SEQ), BF16)],
        ),
        out_shape=[shaped(512, D)] * 4 + [shaped(256, D)] * 2 + [shaped(512, D), shaped(1, OWN_FF, kind=F32),
                   shaped(SEQ, OWN_FF), shaped(SEQ, OWN_FF), shaped(D, OWN_FF)],
        compiler_params=params(60, dimension_semantics=("arbitrary",)),
        cost_estimate=cost(8 * SEQ * D * OWN_FF, 20 << 20, 2 * SEQ * OWN_FF),
        name="ffn",
    )(place, n2, seed, mine, other, be, wc)


def merge_kernel(act_ref, gh_ref, we_ref, wc_ref, *refs):
    mlp_ref, q2_ref, done_ref = refs[-3:]
    done_ref[...] = jnp.zeros_like(done_ref)
    mlp_ref[...] = product(act_ref[...], wc_ref[...])
    q2_ref[...] = product_nt(gh_ref[...], we_ref[...])


def merge(half, act, gh, we, wc, held, after):
    rows = lambda cols: pl.BlockSpec((CHUNK, cols), lambda i: (2 * half + i, 0))
    return pl.pallas_call(
        merge_kernel,
        grid=(2,),
        in_specs=[rows(OWN_FF), rows(OWN_FF), whole(D, OWN_FF), whole(OWN_FF, D)] + [ANY_SPEC] * (len(held) + len(after)),
        out_specs=[rows(D), rows(D), whole(1, 128)],
        out_shape=[shaped(SEQ, D, kind=F32)] * 2 + [shaped(1, 128, kind=F32)],
        input_output_aliases={4: 0, 5: 1} if held else {},
        compiler_params=params(28, dimension_semantics=("arbitrary",)),
        cost_estimate=cost(2 * SEQ * D * OWN_FF),
        name="merge",
    )(act, gh, we, wc, *held, *after)


def rotary_arrays():
    frequency = (np.float32(10000.0) ** (-np.arange(0, ROT, 2, dtype=np.float32) / np.float32(ROT))).astype(np.float32)
    angles = (np.arange(SEQ, dtype=np.float32)[:, None] * frequency[None, :]).astype(np.float64)
    cos, sin = np.cos(angles), np.sin(angles)
    half = ROT // 2
    keep = np.ones((SEQ, HEAD_DIM))
    up = np.zeros((SEQ, HEAD_DIM))
    down = np.zeros((SEQ, HEAD_DIM))
    keep[:, :half] = cos
    keep[:, half:ROT] = cos
    down[:, :half] = -sin
    up[:, half:ROT] = sin
    return [np.tile(t, (1, 2)).astype(np.float32) for t in (keep, up, down)]


def turn(rows, keep, up, down):
    return rows * keep + pltpu.roll(rows, ROT // 2, 1) * up + pltpu.roll(rows, PAIR - ROT // 2, 1) * down


def heads_kernel(place_ref, n1_ref, seed_ref, keep_ref, up_ref, down_ref, mine_ref, other_ref, bp_ref, wd_ref, *rest):
    q_ref, k_ref, v_ref, c_ref, wp_ref = rest[-5:]

    @pl.when(pl.program_id(0) == 0)
    def _():
        start = pl.multiple_of(place_ref[0] * OWN_D, OWN_D)
        for t in range(3):
            cols = pl.ds(pl.multiple_of(start + t * D, 128), OWN_D)
            wp_ref[pl.ds(start, OWN_D), t * OWN_D:(t + 1) * OWN_D] = mine_ref[:, cols]
            wp_ref[pl.ds(OWN_D - start, OWN_D), t * OWN_D:(t + 1) * OWN_D] = other_ref[:, cols]

    packed = product(n1_ref[...], wp_ref[...]) + bp_ref[...]
    tables = keep_ref[...], up_ref[...], down_ref[...]
    for p in range(PAIRS):
        cols = slice(p * PAIR, (p + 1) * PAIR)
        q = packed[:, p * PAIR:(p + 1) * PAIR]
        k = packed[:, OWN_D + p * PAIR:OWN_D + (p + 1) * PAIR]
        q_ref[:, cols] = (turn(q, *tables).astype(BF16) * SCORE_SCALE).astype(BF16)
        k_ref[:, cols] = turn(k, *tables).astype(BF16)
    v_ref[...] = packed[:, 2 * OWN_D:].astype(BF16)
    c_ref[...] = product_nt(seed_ref[...], wd_ref[...]).astype(BF16)


def by_rows(columns):
    return pl.BlockSpec((CHUNK, columns), lambda i, *at: (i, 0))


def heads(place, n1, seed, tables, mine, other, bp, wd, after):
    return pl.pallas_call(
        heads_kernel,
        grid=(CHUNKS,),
        in_specs=[SMEM_SPEC] + [by_rows(D)] * 2 + [by_rows(PAIR)] * 3
        + [whole(OWN_D, 3 * D), whole(OWN_D, 3 * D), whole(1, 3 * OWN_D), whole(OWN_D, D)] + [ANY_SPEC] * len(after),
        out_specs=[by_rows(OWN_D)] * 4 + [whole(D, 3 * OWN_D)],
        out_shape=[shaped(SEQ, OWN_D)] * 4 + [shaped(D, 3 * OWN_D)],
        compiler_params=params(28, dimension_semantics=("arbitrary",)),
        cost_estimate=cost(2 * SEQ * D * 4 * OWN_D),
        name="heads",
    )(place, n1, seed, *tables, mine, other, bp, wd, *after)


def attend_kernel(head, *refs):
    q_ref, k_ref, v_ref, c_ref, keep_ref, up_ref, down_ref = refs[:7]
    before_ref = refs[7]
    out_ref, done_ref, dk_s, dv_s = refs[-4:]
    done_ref[...] = jnp.zeros_like(done_ref)
    lane = lax.broadcasted_iota(jnp.int32, (CHUNK, PAIR), 1)
    mine = (lane < HEAD_DIM) if head == 0 else (lane >= HEAD_DIM)
    diagonal = lax.broadcasted_iota(jnp.int32, (CHUNK, CHUNK), 0) >= lax.broadcasted_iota(jnp.int32, (CHUNK, CHUNK), 1)

    def put(at, rows, value):
        low = value.astype(BF16)
        out_ref[at, rows, :] = low if head == 0 else jnp.where(mine, low, before_ref[at, rows, :])

    for c in reversed(range(CHUNKS)):
        rows = chunk_rows(c)
        span = (c + 1) * CHUNK
        q = jnp.where(mine, q_ref[rows, :], 0)
        gc = jnp.where(mine, c_ref[rows, :], 0)
        scores = jnp.where(diagonal, product_nt(q, k_ref[c * CHUNK:span, :]), -1e30)
        if c > 0:
            scores = jnp.concatenate([product_nt(q, k_ref[:c * CHUNK, :]), scores], axis=1)
        top = jnp.max(scores, axis=1, keepdims=True)
        power = jnp.exp(scores - top)
        inverse = 1.0 / jnp.sum(power, axis=1, keepdims=True)
        power_low = power.astype(BF16)
        ctx = jnp.where(mine, product(power_low, v_ref[:span, :]), 0.0) * inverse
        put(0, rows, ctx)
        gc_scaled = (gc.astype(F32) * inverse).astype(BF16)
        delta = jnp.sum(ctx * gc_scaled.astype(F32), axis=1, keepdims=True)
        grad_prob = product_nt(gc_scaled, v_ref[:span, :])
        grad_scores = (power * (grad_prob - delta)).astype(BF16)
        back = keep_ref[rows, :], -up_ref[rows, :], -down_ref[rows, :]
        grad_q = jnp.where(mine, product(grad_scores, k_ref[:span, :]), 0.0) * SCORE_SCALE
        put(1, rows, turn(grad_q, *back))
        dv = product_tn(power_low, gc_scaled)
        dk = product_tn(grad_scores, q)
        if c == CHUNKS - 1:
            dv_s[...] = dv
            dk_s[...] = dk
        else:
            dv_s[:span, :] += dv
            dk_s[:span, :] += dk
    for c in range(CHUNKS):
        rows = chunk_rows(c)
        back = keep_ref[rows, :], -up_ref[rows, :], -down_ref[rows, :]
        put(2, rows, turn(dk_s[rows, :], *back))
        put(3, rows, dv_s[rows, :])


def attend(pair, head, qkvc, tables, pieces, after):
    def kernel(*refs):
        attend_kernel(head, *refs)

    spec = pl.BlockSpec((SEQ, PAIR), lambda i: (0, pair))
    block = pl.BlockSpec((4, SEQ, PAIR), lambda i: (0, 0, pair))
    first = pieces is None
    held = [] if first else [pieces]
    return pl.pallas_call(
        kernel,
        grid=(1,),
        in_specs=[spec] * 4 + [whole(SEQ, PAIR)] * 3 + ([] if first else [block if head == 1 else ANY_SPEC]) + [ANY_SPEC] * len(after),
        out_specs=[block, whole(1, 128)],
        out_shape=[shaped(4, SEQ, OWN_D), shaped(1, 128, kind=F32)],
        input_output_aliases={} if first else {7: 0},
        scratch_shapes=[pltpu.VMEM((SEQ, PAIR), F32)] * 2,
        compiler_params=params(28, dimension_semantics=("arbitrary",)),
        cost_estimate=cost(5e9, 4 << 20, SEQ * SEQ),
        name="attend",
    )(*qkvc, *tables, *held, *after)


def weights_kernel(place_ref, n1_ref, seed_ref, piece_ref, *refs):
    low_ref, mid_ref, send0_ref, send1_ref, gb_ref, done_ref, n1t_ref = refs[-7:]
    done_ref[...] = jnp.zeros_like(done_ref)
    step = pl.program_id(0)
    half = OWN_D // 2

    @pl.when(step == 0)
    def _():
        low_ref[:OWN_D, :] = product_tn(piece_ref[0], seed_ref[...]).astype(BF16)
        for c in range(CHUNKS):
            rows = chunk_rows(c)
            n1t_ref[:, rows] = n1_ref[rows, :].T

    for t in range(3):
        @pl.when(step == t + 1)
        def _(t=t):
            start = pl.multiple_of(place_ref[0] * OWN_D, OWN_D)
            grads = piece_ref[0]
            for refs, cut, at in (((send0_ref, send1_ref), 64, OWN_D - start), ((low_ref, mid_ref), 128, start)):
                full = product(n1t_ref[pl.ds(at, OWN_D), :], grads).astype(BF16)
                first = t * half
                for ref, low, high, shift in ((refs[0], 0, cut, OWN_D if cut == 128 else 0), (refs[1], cut, 3 * half, -cut)):
                    a, b = max(first, low), min(first + half, high)
                    if a < b:
                        ref[a + shift:b + shift, :OWN_D] = full[a - first:b - first]
                        ref[a + shift:b + shift, OWN_D:] = full[half + a - first:half + b - first]
            gb_ref[0] = jnp.sum(grads.astype(F32), axis=0, keepdims=True)


def weights(place, n1, seed, pieces, after):
    return pl.pallas_call(
        weights_kernel,
        grid=(4,),
        in_specs=[SMEM_SPEC, whole(SEQ, D), whole(SEQ, D), pl.BlockSpec((1, SEQ, OWN_D), lambda i: (i, 0, 0))]
        + [ANY_SPEC] * len(after),
        out_specs=[whole(512, D), whole(448, D), whole(64, D), whole(512, D),
                   pl.BlockSpec((1, 1, OWN_D), lambda i: (jnp.maximum(i - 1, 0), 0, 0)), whole(1, 128)],
        out_shape=[shaped(512, D), shaped(448, D), shaped(64, D), shaped(512, D), shaped(3, 1, OWN_D, kind=F32),
                   shaped(1, 128, kind=F32)],
        scratch_shapes=[pltpu.VMEM((D, SEQ), BF16)],
        compiler_params=params(28, dimension_semantics=("arbitrary",)),
        cost_estimate=cost(2 * SEQ * D * 4 * OWN_D),
        name="weights",
    )(place, n1, seed, pieces, *after)


def tail_kernel(place_ref, tok_ref, mlp_ref, q2_ref, wp_ref, wd_ref, vec_ref, gb_ref, piece_ref, *refs):
    keep_out, send_out, keep_in, send_in, sums_ref = refs[-5:]
    step = pl.program_id(0)
    grads = jnp.concatenate([piece_ref[t] for t in (1, 2, 3)], axis=1)
    out = mlp_ref[...] + product(piece_ref[0], wd_ref[...])
    q1 = product_nt(grads, wp_ref[...])
    q2 = q2_ref[...]
    normal, _ = standardise(tok_ref[...].astype(F32))
    sums = jnp.concatenate([jnp.sum(term, axis=0, keepdims=True) for term in (q1 * normal, q1, q2 * normal, q2)], axis=0)
    mixed = q1 * vec_ref[1:2, :] + q2 * vec_ref[2:3, :]

    @pl.when(step < CHUNKS // 2)
    def _():
        send_out[...] = out.astype(BF16)
        send_in[...] = mixed.astype(BF16)

    @pl.when(step >= CHUNKS // 2)
    def _():
        keep_out[...] = out
        keep_in[...] = mixed

    @pl.when(step == 0)
    def _():
        sums_ref[0:4, :] = sums
        for t in range(3):
            sums_ref[4 + t:5 + t, :OWN_D] = gb_ref[t]
            sums_ref[4 + t:5 + t, OWN_D:] = gb_ref[t]

    @pl.when(step > 0)
    def _():
        sums_ref[0:4, :] += sums


def tail(place, tok, mlp, q2, wp, wd, vec, gb, pieces, after):
    half = CHUNKS // 2
    rows = lambda cols: pl.BlockSpec((CHUNK, cols), lambda i, at: ((i + half * (1 - at[0])) % CHUNKS, 0))
    still = lambda *dims: pl.BlockSpec(dims, lambda i, at: (0,) * len(dims))
    sent = pl.BlockSpec((CHUNK, D), lambda i, at: (jnp.minimum(i, half - 1), 0))
    kept = pl.BlockSpec((CHUNK, D), lambda i, at: (jnp.maximum(i - half, 0), 0))
    return pl.pallas_call(
        tail_kernel,
        grid_spec=pltpu.PrefetchScalarGridSpec(
            num_scalar_prefetch=1,
            grid=(CHUNKS,),
            in_specs=[rows(D)] * 3 + [still(D, 3 * OWN_D), still(OWN_D, D), still(8, D), still(3, 1, OWN_D)]
            + [pl.BlockSpec((4, CHUNK, OWN_D), lambda i, at: (0, (i + half * (1 - at[0])) % CHUNKS, 0))]
            + [ANY_SPEC] * len(after),
            out_specs=[kept, sent, kept, sent, still(8, D)],
        ),
        out_shape=[shaped(TOK_DEV, D, kind=F32), shaped(TOK_DEV, D), shaped(TOK_DEV, D, kind=F32), shaped(TOK_DEV, D),
                   shaped(8, D, kind=F32)],
        compiler_params=params(28, dimension_semantics=("arbitrary",)),
        cost_estimate=cost(2 * SEQ * D * 4 * OWN_D, 16 << 20),
        name="tail",
    )(place, tok, mlp, q2, wp, wd, vec, gb, pieces, *after)


def last_kernel(place_ref, tok_ref, grad_ref, keep_out, got_out, keep_in, got_in, vec_ref, *refs):
    out_ref, in_ref, done_ref = refs[-3:]
    done_ref[...] = jnp.zeros_like(done_ref)
    tok = tok_ref[...].astype(F32)
    out_ref[...] = (tok + keep_out[...] + got_out[...].astype(F32) + vec_ref[0:1, :]).astype(BF16)
    normal, scale = standardise(tok)
    mixed = keep_in[...] + got_in[...].astype(F32)
    base = place_ref[0] * TOK_DEV + pl.program_id(0) * CHUNK
    position = base + lax.broadcasted_iota(jnp.int32, (CHUNK, D), 0)
    seed = jnp.where(position < place_ref[1], grad_ref[...].astype(F32), 0.0)
    mean = jnp.mean(mixed, axis=-1, keepdims=True)
    along = jnp.mean(mixed * normal, axis=-1, keepdims=True)
    in_ref[...] = seed + scale * (mixed - mean - normal * along)


def last(place, tok, grad, keep_out, got_out, keep_in, got_in, vec, after):
    return pl.pallas_call(
        last_kernel,
        grid=(TOK_DEV // CHUNK,),
        in_specs=[SMEM_SPEC] + [by_rows(D)] * 6 + [whole(8, D)] + [ANY_SPEC] * len(after),
        out_specs=[by_rows(D)] * 2 + [whole(1, 128)],
        out_shape=[shaped(TOK_DEV, D), shaped(TOK_DEV, D, kind=F32), shaped(1, 128, kind=F32)],
        compiler_params=params(60, dimension_semantics=("arbitrary",)),
        cost_estimate=cost(1e9),
        name="last",
    )(place, tok, grad, keep_out, got_out, keep_in, got_in, vec, *after)


def rider_kernel(place_ref, mine_ref, other_ref, expand_ref, seed_ref, out_ref, done_ref):
    done_ref[...] = jnp.zeros_like(done_ref)
    first = place_ref[0] == 0
    mine, other = mine_ref[...], other_ref[...]
    left = jnp.where(first, mine[4:7, :OWN_D], other[4:7, :OWN_D])
    right = jnp.where(first, other[4:7, OWN_D:], mine[4:7, OWN_D:])
    out_ref[...] = jnp.concatenate([
        jnp.concatenate([left, right], axis=1), expand_ref[:, :D], expand_ref[:, D:], seed_ref[...],
        mine[0:4, :] + other[0:4, :], jnp.zeros((6, D), F32),
    ], axis=0).astype(BF16)


def make_rider(place, mine, other, expand, seed):
    return pl.pallas_call(
        rider_kernel,
        grid=(1,),
        in_specs=[SMEM_SPEC, whole(8, D), whole(8, D), whole(1, OWN_FF), whole(1, D)],
        out_specs=[whole(16, D), whole(1, 128)],
        out_shape=[shaped(16, D), shaped(1, 128, kind=F32)],
        compiler_params=params(60, dimension_semantics=("arbitrary",)),
        cost_estimate=cost(1e5, 1 << 16),
        name="rider",
    )(place, mine, other, expand, seed)


def ordered(c, at, place_ref, held, rows):
    sides = [place_ref[2 + (c + k) % 3] for k in range(3)]
    which = 2 * c + (at // 4 ^ sides[0])
    start = ((at // 2 % 2 ^ sides[1]) * 2 + (at % 2 ^ sides[2])) * rows
    return held[which, pl.ds(pl.multiple_of(start, rows), rows), :].astype(F32)


def finish_ffn_kernel(place_ref, *refs):
    ins, (contract_out, expand_out, held, contract, expand, in_sems, out_sems) = refs[:6], refs[-7:]
    core = place_ref[0]
    loads = [pltpu.make_async_copy(ins[i], held.at[i], in_sems.at[i]) for i in range(6)]
    stores = [pltpu.make_async_copy(contract, contract_out, out_sems.at[0]),
              pltpu.make_async_copy(expand, expand_out, out_sems.at[1])]
    for load in loads:
        load.start()
    for c in range(3):
        loads[2 * c].wait()
        loads[2 * c + 1].wait()
        for at in range(8):
            value = ordered(c, at, place_ref, held, 128)
            row = c * 1024 + at * 128
            if row < OWN_FF:
                contract[row:row + 128, :] = value
            else:
                half, block = divmod((row - OWN_FF) // 128, 6)
                base = (core if half == 0 else 1 - core) * OWN_FF + block * HIDDEN_BLOCK
                for g in range(3):
                    expand[g * 128:(g + 1) * 128, pl.ds(pl.multiple_of(base, 128), HIDDEN_BLOCK)] = (
                        value[:, g * HIDDEN_BLOCK:(g + 1) * HIDDEN_BLOCK])
        if c == 1:
            stores[0].start()
    stores[1].start()
    for store in stores:
        store.wait()


def finish_ffn(place, parts, after):
    big = [(OWN_FF, D), (OWN_D, FF)]
    return pl.pallas_call(
        finish_ffn_kernel,
        in_specs=[SMEM_SPEC] + [ANY_SPEC] * (6 + len(after)),
        out_specs=[ANY_SPEC] * 2,
        out_shape=[shaped(*dims, kind=F32) for dims in big],
        scratch_shapes=[pltpu.VMEM((6, 512, D), BF16)] + [pltpu.VMEM(dims, F32) for dims in big]
        + [pltpu.SemaphoreType.DMA((6,)), pltpu.SemaphoreType.DMA((2,))],
        compiler_params=params(40),
        cost_estimate=cost(1e8, 16 << 20),
        name="finish_ffn",
    )(place, *parts, *after)


def finish_kernel(place_ref, *refs):
    ins = refs[:6]
    rider_ref = refs[6]
    outs = refs[-15:-13]
    small = refs[-13:-5]
    held, project, dense, in_sems, out_sems = refs[-5:]
    core = place_ref[0]
    loads = [pltpu.make_async_copy(ins[i], held.at[i], in_sems.at[i]) for i in range(6)]
    stores = [pltpu.make_async_copy(stage, outs[i], out_sems.at[i]) for i, stage in enumerate((project, dense))]
    for load in loads:
        load.start()
    rows = rider_ref[...].astype(F32)
    pieces = [(0, 0, 1, 1), (0, 1, 2, 0), (1, 0, 2, 1)]
    for t, (r0, h0, r1, h1) in enumerate(pieces):
        small[0][t * OWN_D:(t + 1) * OWN_D] = jnp.where(
            core == 0, rows[r0:r0 + 1, h0 * OWN_D:(h0 + 1) * OWN_D], rows[r1:r1 + 1, h1 * OWN_D:(h1 + 1) * OWN_D]).reshape(OWN_D)
    small[1][:D] = rows[3:4, :].reshape(D)
    small[1][D:] = rows[4:5, :].reshape(D)
    for i in range(5):
        row = rows[5 + i:6 + i, :]
        value = jnp.where(core == 0, row[:, :OWN_D], row[:, OWN_D:]).reshape(OWN_D)
        small[3 + i][...] = value
        if i == 0:
            small[2][...] = value
    for c in range(3):
        loads[2 * c].wait()
        loads[2 * c + 1].wait()
        for at in range(8):
            value = ordered(c, at, place_ref, held, 64)
            row = c * 512 + at * 64
            if row < OWN_D:
                dense[row:row + 64, :] = value
            else:
                half, row = divmod(row - OWN_D, 3 * OWN_D // 2)
                t, row = divmod(row, OWN_D // 2)
                cols = pl.ds(pl.multiple_of((core if half == 0 else 1 - core) * OWN_D + t * D, 128), OWN_D)
                project[row:row + 64, cols] = value[:, :OWN_D]
                project[OWN_D // 2 + row:OWN_D // 2 + row + 64, cols] = value[:, OWN_D:]
        if c == 0:
            stores[1].start()
    stores[0].start()
    for store in stores:
        store.wait()


def finish(place, parts, rider, after):
    big = [(OWN_D, 3 * D), (OWN_D, D)]
    vectors = [3 * OWN_D, OWN_FF] + [OWN_D] * 6
    return pl.pallas_call(
        finish_kernel,
        in_specs=[SMEM_SPEC] + [ANY_SPEC] * 6 + [VMEM_SPEC] + [ANY_SPEC] * len(after),
        out_specs=[ANY_SPEC] * 2 + [VMEM_SPEC] * 8,
        out_shape=[shaped(*dims, kind=F32) for dims in big] + [shaped(n, kind=F32) for n in vectors],
        scratch_shapes=[pltpu.VMEM((6, 256, D), BF16)] + [pltpu.VMEM(dims, F32) for dims in big]
        + [pltpu.SemaphoreType.DMA((6,)), pltpu.SemaphoreType.DMA((2,))],
        compiler_params=params(28),
        cost_estimate=cost(1e8, 8 << 20),
        name="finish",
    )(place, *parts, rider, *after)


def partner(chip, dim):
    step = 4 ** (dim % 3)
    at = (chip // step) % 4
    return chip + ((at ^ 1 if dim < 3 else 3 - at) - at) * step


def side_of(chip, dim):
    at = (chip // (4 ** (dim % 3))) % 4
    return (at ^ (at // 2)) & 1 if dim < 3 else at // 2


def first_dims(axis):
    return [(r * 2 + s, partner(r, axis + 3 * s) * 2 + s) for r in range(64) for s in range(2)]


def second_dims(axis):
    return [(r * 2 + s, partner(r, axis + 3 * (1 - s)) * 2 + s) for r in range(64) for s in range(2)]


def first_side(axis):
    chip, core = lax.axis_index("replica"), lax.axis_index("shard")
    return jnp.where(core == 0, side_of(chip, axis), side_of(chip, axis + 3))


def add_low(left, right, done=None):
    total = left.astype(F32) + right.astype(F32)
    return (total if done is None else total + done[:, :1]).astype(BF16)


def scatter_start(parts, k):
    sends, keeps, got = [], [], []
    for c, part in enumerate(parts):
        side = first_side((c + k) % 3)
        if isinstance(part, tuple):
            sends.append(jnp.where(side == 0, part[1], part[0]))
            keeps.append(jnp.where(side == 0, part[0], part[1]))
        else:
            half = part.shape[0] // 2
            sends.append(lax.dynamic_slice_in_dim(part, (1 - side) * half, half, 0))
            keeps.append(lax.dynamic_slice_in_dim(part, side * half, half, 0))
    for c, send in enumerate(sends):
        got.append(lax.ppermute(send, BOTH, first_dims((c + k) % 3)))
    return sends, keeps, got


def scatter_end(keeps, got, done=None):
    return [add_low(a, b, done) for a, b in zip(keeps, got)]


def on_device(tokens, lengths, project_weight, project_bias, dense_weight, dense_bias, expand_weight, expand_bias,
              contract_weight, contract_bias, first_gain, first_shift, second_gain, second_shift, out_grad):
    core = lax.axis_index("shard")
    swap = lambda rows: lax.ppermute(rows, "shard", [(0, 1), (1, 0)])
    place = jnp.stack([core.astype(jnp.int32), lengths[0]] + [first_side(axis).astype(jnp.int32) for axis in range(3)])
    other_tokens = swap(tokens)
    other_grad = swap(out_grad)
    packed, b_expand = pack(
        project_bias, dense_bias, contract_bias, first_gain, first_shift, second_gain, second_shift, expand_bias)
    other_packed = swap(packed)
    other_expand = swap(expand_weight)
    other_project = swap(project_weight)
    tables = [jnp.asarray(t) for t in rotary_arrays()]

    n1, n2, seed, tok, seed_sum, b_project, vec = prep(
        place, tokens, other_tokens, out_grad, other_grad, packed, other_packed)
    gc0, gc1, gc2, ge0, ge1, ge_send0, ge_send1, gbe, act, gh, w_expand = ffn(
        place, n2, seed, expand_weight, other_expand, b_expand, contract_weight)

    parts = [(gc0, gc1), (gc2, ge0), (jnp.concatenate([ge1, swap(ge_send0)], axis=0), swap(ge_send1))]

    sends, keeps, got = scatter_start(parts, 0)
    *qkvc, w_project = heads(place, n1, seed, tables, project_weight, other_project, b_project, dense_weight, sends)
    pieces, done = attend(0, 0, qkvc, tables, None, [])
    parts = scatter_end(keeps, got, done)
    sends, keeps, got = scatter_start(parts, 1)
    pieces, done = attend(0, 1, qkvc, tables, pieces, sends)
    parts = scatter_end(keeps, got, done)
    sends, keeps, got = scatter_start(parts, 2)
    pieces, done = attend(1, 0, qkvc, tables, pieces, sends)
    parts = scatter_end(keeps, got, done)
    block = jnp.concatenate(parts, axis=0)
    for axis, (pair, head) in enumerate(((1, 1), (2, 0), (2, 1))):
        got = lax.ppermute(block, BOTH, second_dims(axis))
        pieces, done = attend(pair, head, qkvc, tables, pieces, [block])
        if axis == 0:
            *merged, done = merge(0, act, gh, w_expand, contract_weight, [], [pieces])
        if axis == 1:
            mlp, q2, done = merge(1, act, gh, w_expand, contract_weight, merged, [pieces])
        if axis == 2:
            low, mid, gw_send0, gw_send1, gb, done = weights(place, n1, seed, pieces, [got])
        block = add_low(block, got, done)
    units = [low, jnp.concatenate([mid, swap(gw_send0)], axis=0), swap(gw_send1)]
    sends, keeps, late = scatter_start(units, 0)
    keep_out, send_out, keep_in, send_in, sums = tail(
        place, tok, mlp, q2, w_project, dense_weight, vec, gb, pieces, sends + [block])

    parts = [block[c * 128:(c + 1) * 128] for c in range(3)]
    for k in (2, 1, 0):
        got = [lax.ppermute(part, BOTH, first_dims((c + k) % 3)) for c, part in enumerate(parts)]
        if k > 0:
            parts = [jnp.concatenate(pair, axis=0) for pair in zip(parts, got)]
    ffn_ends = [a for pair in zip(parts, got) for a in pair]

    rider, done = make_rider(place, sums, swap(sums), gbe, seed_sum)
    units = scatter_end(keeps, late, done)
    for k in (1, 2):
        sends, keeps, late = scatter_start(units, k)
        units = scatter_end(keeps, late)
    other_out, other_in = swap(send_out), swap(send_in)

    block = jnp.concatenate(units + [rider], axis=0)
    for axis in range(3):
        got, done = lax.ppermute(block, BOTH, second_dims(axis)), None
        if axis == 1:
            outputs, input_grad, done = last(
                place, tokens, out_grad, keep_out, other_out, keep_in, other_in, vec, [block])
        block = add_low(block, got, done)
    rider = block[192:]
    parts = [block[c * 64:(c + 1) * 64] for c in range(3)]
    for k in (2, 1, 0):
        size = parts[0].shape[0]
        sends = [jnp.concatenate([parts[0], rider], axis=0)] + parts[1:]
        late = [lax.ppermute(part, BOTH, first_dims((c + k) % 3)) for c, part in enumerate(sends)]
        rider = add_low(rider, late[0][size:])
        late[0] = late[0][:size]
        if k > 0:
            parts = [jnp.concatenate(pair, axis=0) for pair in zip(parts, late)]
    contract, expand = finish_ffn(place, ffn_ends, sends)
    project, dense, g_project, g_expand, g_dense, g_contract, gain_one, shift_one, gain_two, shift_two = finish(
        place, [a for pair in zip(parts, late) for a in pair], rider, [contract])
    return (outputs, input_grad, project, g_project, dense, g_dense, expand, g_expand, contract, g_contract,
            gain_one, shift_one, gain_two, shift_two)


def solution(mesh):
    rows, first = P(("replica", "shard"), None), P("shard", None)
    one = P("shard")
    return jax.shard_map(
        on_device,
        mesh=mesh,
        in_specs=(rows, P("replica"), first, one, first, one, first, one, first, one, one, one, one, one, rows),
        out_specs=(rows, rows, first, one, first, one, first, one, first, one, one, one, one, one),
        check_vma=False,
    )
```

```python
import jax
import jax.numpy as jnp
import numpy as np
from jax import lax
from jax.experimental import pallas as pl
from jax.experimental.pallas import tpu as pltpu
from jax.sharding import PartitionSpec as P

HEADS = 12
HEAD_DIM = 64
D = 768
ROT = 16
FF = 3072
SEQ = 1024
TOK_DEV = 512
EPSILON = 1e-05
SCORE_SCALE = 0.125
F32 = jnp.float32
BF16 = jnp.bfloat16
MIB = 1024 * 1024
OWN_FF = FF // 2
OWN_D = D // 2
PAIR = 2 * HEAD_DIM
PAIRS = OWN_D // PAIR
HIDDEN_BLOCK = 256
CHUNK = 256
CHUNKS = SEQ // CHUNK
BOTH = ("replica", "shard")


def product(left, right):
    return lax.dot_general(left, right, (((1,), (0,)), ((), ())), preferred_element_type=F32)


def product_nt(left, right):
    return lax.dot_general(left, right, (((1,), (1,)), ((), ())), preferred_element_type=F32)


def product_tn(left, right):
    return lax.dot_general(left, right, (((0,), (0,)), ((), ())), preferred_element_type=F32)


def chunk_rows(c):
    return slice(c * CHUNK, (c + 1) * CHUNK)


def params(mib, **kw):
    return pltpu.CompilerParams(vmem_limit_bytes=mib * MIB, **kw)


def cost(flops, size=8 << 20, exps=0):
    return pl.CostEstimate(flops=int(flops), bytes_accessed=int(size), transcendentals=int(exps))


VMEM_SPEC = pl.BlockSpec(memory_space=pltpu.VMEM)
SMEM_SPEC = pl.BlockSpec(memory_space=pltpu.SMEM)
ANY_SPEC = pl.BlockSpec(memory_space=pl.ANY)


def shaped(*dims, kind=BF16):
    return jax.ShapeDtypeStruct(dims, kind)


def standardise(rows):
    mean = jnp.mean(rows, axis=-1, keepdims=True)
    centered = rows - mean
    scale = lax.rsqrt(jnp.mean(centered * centered, axis=-1, keepdims=True) + EPSILON)
    return centered * scale, scale


def whole(*dims):
    return pl.BlockSpec(dims, lambda *i: (0,) * len(dims))


def pack_kernel(project_ref, *refs):
    out_ref, expand_out = refs[-2:]
    expand_out[...] = refs[-3][...].astype(F32).reshape(1, OWN_FF)
    for t in range(3):
        out_ref[t:t + 1, :] = project_ref[t * OWN_D:(t + 1) * OWN_D].astype(F32).reshape(1, OWN_D)
    for i, ref in enumerate(refs[:-3]):
        out_ref[3 + i:4 + i, :] = ref[...].astype(F32).reshape(1, OWN_D)


def pack(*vectors):
    return pl.pallas_call(
        pack_kernel,
        grid=(1,),
        in_specs=[whole(v.shape[0]) for v in vectors],
        out_specs=[whole(16, OWN_D), whole(1, OWN_FF)],
        out_shape=[shaped(16, OWN_D, kind=F32), shaped(1, OWN_FF, kind=F32)],
        compiler_params=params(60, dimension_semantics=("arbitrary",)),
        cost_estimate=cost(1e5, 1 << 16),
        name="pack",
    )(*vectors)


def prep_kernel(place_ref, mine_ref, other_ref, grad_ref, other_grad_ref, pack_ref, other_pack_ref,
                n1_ref, n2_ref, seed_ref, sum_ref, head_bias_ref, vec_ref):
    side = place_ref[0]
    length = place_ref[1]
    first = jnp.where(side == 0, pack_ref[...], other_pack_ref[...])
    second = jnp.where(side == 0, other_pack_ref[...], pack_ref[...])
    for t in range(3):
        blocks = [half[row % 3:row % 3 + 1, :] for row in (2 * t, 2 * t + 1) for half in ((first, second)[row // 3],)]
        head_bias_ref[:, t * OWN_D:(t + 1) * OWN_D] = jnp.where(side == 0, blocks[0], blocks[1])
    full = [jnp.concatenate([first[r:r + 1, :], second[r:r + 1, :]], axis=1) for r in range(3, 9)]
    vec_ref[0:1, :] = full[0] + full[1]
    vec_ref[1:2, :] = full[2]
    vec_ref[2:3, :] = full[4]
    step = pl.program_id(0)
    own = step < CHUNKS // 2
    normal, _ = standardise(jnp.where(own, mine_ref[...], other_ref[...]).astype(F32))
    n1_ref[...] = (normal * full[2] + full[3]).astype(BF16)
    n2_ref[...] = (normal * full[4] + full[5]).astype(BF16)
    position = (step + side * (CHUNKS // 2)) % CHUNKS * CHUNK + lax.broadcasted_iota(jnp.int32, (CHUNK, D), 0)
    cot = jnp.where(own, grad_ref[...], other_grad_ref[...])
    seed = jnp.where(position < length, cot.astype(F32), 0.0)
    seed_ref[...] = seed.astype(BF16)

    @pl.when(step == 0)
    def _():
        sum_ref[...] = jnp.zeros_like(sum_ref)

    sum_ref[...] += jnp.sum(seed, axis=0, keepdims=True)


FIRST_HALF = pl.BlockSpec((CHUNK, D), lambda i, at: (jnp.minimum(i, CHUNKS // 2 - 1), 0))
SECOND_HALF = pl.BlockSpec((CHUNK, D), lambda i, at: (jnp.maximum(i - CHUNKS // 2, 0), 0))


def prep(place, mine, other, grad, other_grad, packed, other_packed):
    rows = pl.BlockSpec((CHUNK, D), lambda i, at: ((i + CHUNKS // 2 * at[0]) % CHUNKS, 0))
    return pl.pallas_call(
        prep_kernel,
        grid_spec=pltpu.PrefetchScalarGridSpec(
            num_scalar_prefetch=1,
            grid=(CHUNKS,),
            in_specs=[FIRST_HALF, SECOND_HALF] * 2 + [whole(16, OWN_D)] * 2,
            out_specs=[rows] * 3 + [whole(1, D), whole(1, 3 * OWN_D), whole(8, D)],
        ),
        out_shape=[shaped(SEQ, D)] * 3 + [shaped(1, D, kind=F32), shaped(1, 3 * OWN_D, kind=F32), shaped(8, D, kind=F32)],
        compiler_params=params(60, dimension_semantics=("arbitrary",)),
        cost_estimate=cost(4e9),
        name="prep",
    )(place, mine, other, grad, other_grad, packed, other_packed)


def gelu_pair(hidden):
    size = jnp.abs(hidden)
    near = 1.0 / (1.0 + (0.3275911 * 0.7071067811865476) * size)
    bell = jnp.exp(-0.5 * hidden * hidden)
    poly = 0.5 * 1.061405429 * near - 0.5 * 1.453152027
    poly = poly * near + 0.5 * 1.421413741
    poly = poly * near - 0.5 * 0.284496736
    poly = poly * near + 0.5 * 0.254829592
    tail = poly * near * bell
    phi = jnp.where(hidden >= 0, 1.0 - tail, tail)
    return hidden * phi, phi + hidden * bell * 0.3989422804014327


def ffn_kernel(place_ref, n2_ref, seed_ref, mine_ref, other_ref, be_ref, wc_ref,
               gc0_ref, gc1_ref, gc2_ref, keep0_ref, keep1_ref, send0_ref, send1_ref, gbe_ref, act_ref, gh_ref, we_ref,
               n2t_ref):
    step = pl.program_id(0)

    @pl.when(step == 0)
    def _():
        for c in range(CHUNKS):
            rows = chunk_rows(c)
            n2t_ref[:, rows] = n2_ref[rows, :].T

    start = pl.multiple_of(place_ref[0] * OWN_D, OWN_D)
    we_ref[pl.ds(start, OWN_D), :] = mine_ref[...]
    we_ref[pl.ds(OWN_D - start, OWN_D), :] = other_ref[...]
    bias = be_ref[...]
    total = jnp.zeros((1, HIDDEN_BLOCK), F32)
    for c in range(CHUNKS):
        rows = chunk_rows(c)
        hidden = product(n2_ref[rows, :], we_ref[...]) + bias
        value, slope = gelu_pair(hidden)
        act_ref[rows, :] = value.astype(BF16)
        gh = (product_nt(seed_ref[rows, :], wc_ref[...]) * slope).astype(BF16)
        gh_ref[rows, :] = gh
        total += jnp.sum(gh.astype(F32), axis=0, keepdims=True)
    gbe_ref[...] = total
    gc = product_tn(act_ref[...], seed_ref[...]).astype(BF16)

    keep = product(n2t_ref[pl.ds(start, OWN_D), :], gh_ref[...]).astype(BF16)
    send = product(n2t_ref[pl.ds(OWN_D - start, OWN_D), :], gh_ref[...]).astype(BF16)
    for low, high, ref in ((0, 2, gc0_ref), (2, 4, gc1_ref), (4, 6, gc2_ref)):
        @pl.when((step >= low) & (step < high))
        def _(ref=ref):
            ref[...] = gc

    for low, high, ref, value in ((0, 4, keep0_ref, keep), (4, 6, keep1_ref, keep), (0, 2, send0_ref, send), (2, 6, send1_ref, send)):
        @pl.when((step >= low) & (step < high))
        def _(ref=ref, value=value):
            for g in range(3):
                ref[:, g * HIDDEN_BLOCK:(g + 1) * HIDDEN_BLOCK] = value[g * 128:(g + 1) * 128, :]


def ffn(place, n2, seed, mine, other, be, wc):
    steps = OWN_FF // HIDDEN_BLOCK
    rows_block = pl.BlockSpec((HIDDEN_BLOCK, D), lambda i, at: (i, 0))
    cols_block = pl.BlockSpec((OWN_D, HIDDEN_BLOCK), lambda i, at: (0, at[0] * steps + i))
    bias_block = pl.BlockSpec((1, HIDDEN_BLOCK), lambda i, at: (0, i))
    part = lambda rows, low, high: pl.BlockSpec((rows, D), lambda i, at: (jnp.clip(i, low, high - 1) - low, 0))
    tall_block = pl.BlockSpec((SEQ, HIDDEN_BLOCK), lambda i, at: (0, i))
    return pl.pallas_call(
        ffn_kernel,
        grid_spec=pltpu.PrefetchScalarGridSpec(
            num_scalar_prefetch=1,
            grid=(steps,),
            in_specs=[whole(SEQ, D), whole(SEQ, D), cols_block, cols_block, bias_block, rows_block],
            out_specs=[part(HIDDEN_BLOCK, 0, 2), part(HIDDEN_BLOCK, 2, 4), part(HIDDEN_BLOCK, 4, 6),
                       part(128, 0, 4), part(128, 4, 6), part(128, 0, 2), part(128, 2, 6), bias_block, tall_block, tall_block,
                       pl.BlockSpec((D, HIDDEN_BLOCK), lambda i, at: (0, i))],
            scratch_shapes=[pltpu.VMEM((D, SEQ), BF16)],
        ),
        out_shape=[shaped(512, D)] * 4 + [shaped(256, D)] * 2 + [shaped(512, D), shaped(1, OWN_FF, kind=F32),
                   shaped(SEQ, OWN_FF), shaped(SEQ, OWN_FF), shaped(D, OWN_FF)],
        compiler_params=params(60, dimension_semantics=("arbitrary",)),
        cost_estimate=cost(8 * SEQ * D * OWN_FF, 20 << 20, 2 * SEQ * OWN_FF),
        name="ffn",
    )(place, n2, seed, mine, other, be, wc)


def merge_kernel(act_ref, gh_ref, we_ref, wc_ref, *refs):
    mlp_ref, q2_ref, done_ref = refs[-3:]
    done_ref[...] = jnp.zeros_like(done_ref)
    mlp_ref[...] = product(act_ref[...], wc_ref[...]).astype(BF16)
    q2_ref[...] = product_nt(gh_ref[...], we_ref[...]).astype(BF16)


def merge(half, act, gh, we, wc, held, after):
    rows = lambda cols: pl.BlockSpec((CHUNK, cols), lambda i: (2 * half + i, 0))
    return pl.pallas_call(
        merge_kernel,
        grid=(2,),
        in_specs=[rows(OWN_FF), rows(OWN_FF), whole(D, OWN_FF), whole(OWN_FF, D)] + [ANY_SPEC] * (len(held) + len(after)),
        out_specs=[rows(D), rows(D), whole(1, 128)],
        out_shape=[shaped(SEQ, D)] * 2 + [shaped(1, 128, kind=F32)],
        input_output_aliases={4: 0, 5: 1} if held else {},
        compiler_params=params(28, dimension_semantics=("arbitrary",)),
        cost_estimate=cost(2 * SEQ * D * OWN_FF),
        name="merge",
    )(act, gh, we, wc, *held, *after)


def rotary_arrays():
    frequency = (np.float32(10000.0) ** (-np.arange(0, ROT, 2, dtype=np.float32) / np.float32(ROT))).astype(np.float32)
    angles = (np.arange(SEQ, dtype=np.float32)[:, None] * frequency[None, :]).astype(np.float64)
    cos, sin = np.cos(angles), np.sin(angles)
    half = ROT // 2
    keep = np.ones((SEQ, HEAD_DIM))
    up = np.zeros((SEQ, HEAD_DIM))
    down = np.zeros((SEQ, HEAD_DIM))
    keep[:, :half] = cos
    keep[:, half:ROT] = cos
    down[:, :half] = -sin
    up[:, half:ROT] = sin
    return [np.tile(t, (1, 2)).astype(np.float32) for t in (keep, up, down)]


def turn(rows, keep, up, down):
    return rows * keep + pltpu.roll(rows, ROT // 2, 1) * up + pltpu.roll(rows, PAIR - ROT // 2, 1) * down


def heads_kernel(place_ref, n1_ref, seed_ref, keep_ref, up_ref, down_ref, mine_ref, other_ref, bp_ref, wd_ref, *rest):
    q_ref, k_ref, v_ref, c_ref, wp_ref = rest[-5:]

    @pl.when(pl.program_id(0) == 0)
    def _():
        start = pl.multiple_of(place_ref[0] * OWN_D, OWN_D)
        for t in range(3):
            cols = pl.ds(pl.multiple_of(start + t * D, 128), OWN_D)
            wp_ref[pl.ds(start, OWN_D), t * OWN_D:(t + 1) * OWN_D] = mine_ref[:, cols]
            wp_ref[pl.ds(OWN_D - start, OWN_D), t * OWN_D:(t + 1) * OWN_D] = other_ref[:, cols]

    packed = product(n1_ref[...], wp_ref[...]) + bp_ref[...]
    tables = keep_ref[...], up_ref[...], down_ref[...]
    for p in range(PAIRS):
        cols = slice(p * PAIR, (p + 1) * PAIR)
        q = packed[:, p * PAIR:(p + 1) * PAIR]
        k = packed[:, OWN_D + p * PAIR:OWN_D + (p + 1) * PAIR]
        q_ref[:, cols] = (turn(q, *tables).astype(BF16) * SCORE_SCALE).astype(BF16)
        k_ref[:, cols] = turn(k, *tables).astype(BF16)
    v_ref[...] = packed[:, 2 * OWN_D:].astype(BF16)
    c_ref[...] = product_nt(seed_ref[...], wd_ref[...]).astype(BF16)


def by_rows(columns):
    return pl.BlockSpec((CHUNK, columns), lambda i, *at: (i, 0))


def heads(place, n1, seed, tables, mine, other, bp, wd, after):
    return pl.pallas_call(
        heads_kernel,
        grid=(CHUNKS,),
        in_specs=[SMEM_SPEC] + [by_rows(D)] * 2 + [by_rows(PAIR)] * 3
        + [whole(OWN_D, 3 * D), whole(OWN_D, 3 * D), whole(1, 3 * OWN_D), whole(OWN_D, D)] + [ANY_SPEC] * len(after),
        out_specs=[by_rows(OWN_D)] * 4 + [whole(D, 3 * OWN_D)],
        out_shape=[shaped(SEQ, OWN_D)] * 4 + [shaped(D, 3 * OWN_D)],
        compiler_params=params(28, dimension_semantics=("arbitrary",)),
        cost_estimate=cost(2 * SEQ * D * 4 * OWN_D),
        name="heads",
    )(place, n1, seed, *tables, mine, other, bp, wd, *after)


def attend_kernel(head, *refs):
    q_ref, k_ref, v_ref, c_ref, keep_ref, up_ref, down_ref = refs[:7]
    before_ref = refs[7]
    out_ref, done_ref, dk_s, dv_s = refs[-4:]
    done_ref[...] = jnp.zeros_like(done_ref)
    lane = lax.broadcasted_iota(jnp.int32, (CHUNK, PAIR), 1)
    mine = (lane < HEAD_DIM) if head == 0 else (lane >= HEAD_DIM)
    diagonal = lax.broadcasted_iota(jnp.int32, (CHUNK, CHUNK), 0) >= lax.broadcasted_iota(jnp.int32, (CHUNK, CHUNK), 1)

    def put(at, rows, value):
        low = value.astype(BF16)
        out_ref[at, rows, :] = low if head == 0 else jnp.where(mine, low, before_ref[at, rows, :])

    for c in reversed(range(CHUNKS)):
        rows = chunk_rows(c)
        span = (c + 1) * CHUNK
        q = jnp.where(mine, q_ref[rows, :], 0)
        gc = jnp.where(mine, c_ref[rows, :], 0)
        scores = jnp.where(diagonal, product_nt(q, k_ref[c * CHUNK:span, :]), -1e30)
        if c > 0:
            scores = jnp.concatenate([product_nt(q, k_ref[:c * CHUNK, :]), scores], axis=1)
        top = jnp.max(scores, axis=1, keepdims=True)
        power = jnp.exp(scores - top)
        inverse = 1.0 / jnp.sum(power, axis=1, keepdims=True)
        power_low = power.astype(BF16)
        ctx = jnp.where(mine, product(power_low, v_ref[:span, :]), 0.0) * inverse
        put(0, rows, ctx)
        gc_scaled = (gc.astype(F32) * inverse).astype(BF16)
        delta = jnp.sum(ctx * gc_scaled.astype(F32), axis=1, keepdims=True)
        grad_prob = product_nt(gc_scaled, v_ref[:span, :])
        grad_scores = (power * (grad_prob - delta)).astype(BF16)
        back = keep_ref[rows, :], -up_ref[rows, :], -down_ref[rows, :]
        grad_q = jnp.where(mine, product(grad_scores, k_ref[:span, :]), 0.0) * SCORE_SCALE
        put(1, rows, turn(grad_q, *back))
        dv = product_tn(power_low, gc_scaled)
        dk = product_tn(grad_scores, q)
        if c == CHUNKS - 1:
            dv_s[...] = dv
            dk_s[...] = dk
        else:
            dv_s[:span, :] += dv
            dk_s[:span, :] += dk
    for c in range(CHUNKS):
        rows = chunk_rows(c)
        back = keep_ref[rows, :], -up_ref[rows, :], -down_ref[rows, :]
        put(2, rows, turn(dk_s[rows, :], *back))
        put(3, rows, dv_s[rows, :])


def attend(pair, head, qkvc, tables, pieces, after):
    def kernel(*refs):
        attend_kernel(head, *refs)

    spec = pl.BlockSpec((SEQ, PAIR), lambda i: (0, pair))
    block = pl.BlockSpec((4, SEQ, PAIR), lambda i: (0, 0, pair))
    first = pieces is None
    held = [] if first else [pieces]
    return pl.pallas_call(
        kernel,
        grid=(1,),
        in_specs=[spec] * 4 + [whole(SEQ, PAIR)] * 3 + ([] if first else [block if head == 1 else ANY_SPEC]) + [ANY_SPEC] * len(after),
        out_specs=[block, whole(1, 128)],
        out_shape=[shaped(4, SEQ, OWN_D), shaped(1, 128, kind=F32)],
        input_output_aliases={} if first else {7: 0},
        scratch_shapes=[pltpu.VMEM((SEQ, PAIR), F32)] * 2,
        compiler_params=params(28, dimension_semantics=("arbitrary",)),
        cost_estimate=cost(5e9, 4 << 20, SEQ * SEQ),
        name="attend",
    )(*qkvc, *tables, *held, *after)


def weights_kernel(place_ref, n1_ref, seed_ref, piece_ref, *refs):
    gd_ref, own0_ref, own1_ref, send0_ref, send1_ref, gb_ref, done_ref, n1t_ref = refs[-8:]
    done_ref[...] = jnp.zeros_like(done_ref)
    step = pl.program_id(0)
    half = OWN_D // 2

    @pl.when(step == 0)
    def _():
        gd_ref[...] = product_tn(piece_ref[0], seed_ref[...]).astype(BF16)
        for c in range(CHUNKS):
            rows = chunk_rows(c)
            n1t_ref[:, rows] = n1_ref[rows, :].T

    own = [(own0_ref, 0), (own0_ref, half), (own1_ref, 0)]
    sent = [(send0_ref, 0), (send1_ref, 0), (send1_ref, half)]
    for t in range(3):
        @pl.when(step == t + 1)
        def _(t=t):
            start = pl.multiple_of(place_ref[0] * OWN_D, OWN_D)
            grads = piece_ref[0]
            for (ref, row), at in ((sent[t], OWN_D - start), (own[t], start)):
                full = product(n1t_ref[pl.ds(at, OWN_D), :], grads).astype(BF16)
                ref[row:row + half, :OWN_D] = full[:half]
                ref[row:row + half, OWN_D:] = full[half:]
            gb_ref[0] = jnp.sum(grads.astype(F32), axis=0, keepdims=True)


def weights(place, n1, seed, pieces, after):
    half = OWN_D // 2
    return pl.pallas_call(
        weights_kernel,
        grid=(4,),
        in_specs=[SMEM_SPEC, whole(SEQ, D), whole(SEQ, D), pl.BlockSpec((1, SEQ, OWN_D), lambda i: (i, 0, 0))]
        + [ANY_SPEC] * len(after),
        out_specs=[whole(OWN_D, D), whole(OWN_D, D), whole(half, D), whole(half, D), whole(OWN_D, D),
                   pl.BlockSpec((1, 1, OWN_D), lambda i: (jnp.maximum(i - 1, 0), 0, 0)), whole(1, 128)],
        out_shape=[shaped(OWN_D, D), shaped(OWN_D, D), shaped(half, D), shaped(half, D), shaped(OWN_D, D),
                   shaped(3, 1, OWN_D, kind=F32), shaped(1, 128, kind=F32)],
        scratch_shapes=[pltpu.VMEM((D, SEQ), BF16)],
        compiler_params=params(28, dimension_semantics=("arbitrary",)),
        cost_estimate=cost(2 * SEQ * D * 4 * OWN_D),
        name="weights",
    )(place, n1, seed, pieces, *after)


def tail_kernel(place_ref, other_ref, mine_ref, mlp_ref, q2_ref, wp_ref, wd_ref, vec_ref, gb_ref, piece_ref, *refs):
    keep_out, send_out, keep_in, send_in, sums_ref = refs[-5:]
    step = pl.program_id(0)
    grads = jnp.concatenate([piece_ref[t] for t in (1, 2, 3)], axis=1)
    out = mlp_ref[...].astype(F32) + product(piece_ref[0], wd_ref[...])
    q1 = product_nt(grads, wp_ref[...])
    q2 = q2_ref[...].astype(F32)
    normal, _ = standardise(jnp.where(step < CHUNKS // 2, other_ref[...], mine_ref[...]).astype(F32))
    sums = jnp.concatenate([jnp.sum(term, axis=0, keepdims=True) for term in (q1 * normal, q1, q2 * normal, q2)], axis=0)
    mixed = q1 * vec_ref[1:2, :] + q2 * vec_ref[2:3, :]

    @pl.when(step < CHUNKS // 2)
    def _():
        send_out[...] = out.astype(BF16)
        send_in[...] = mixed.astype(BF16)

    @pl.when(step >= CHUNKS // 2)
    def _():
        keep_out[...] = out.astype(BF16)
        keep_in[...] = mixed.astype(BF16)

    @pl.when(step == 0)
    def _():
        sums_ref[0:4, :] = sums
        for t in range(3):
            sums_ref[4 + t:5 + t, :OWN_D] = gb_ref[t]
            sums_ref[4 + t:5 + t, OWN_D:] = gb_ref[t]

    @pl.when(step > 0)
    def _():
        sums_ref[0:4, :] += sums


def tail(place, other, mine, mlp, q2, wp, wd, vec, gb, pieces, after):
    half = CHUNKS // 2
    rows = lambda cols: pl.BlockSpec((CHUNK, cols), lambda i, at: ((i + half * (1 - at[0])) % CHUNKS, 0))
    still = lambda *dims: pl.BlockSpec(dims, lambda i, at: (0,) * len(dims))
    sent = pl.BlockSpec((CHUNK, D), lambda i, at: (jnp.minimum(i, half - 1), 0))
    kept = pl.BlockSpec((CHUNK, D), lambda i, at: (jnp.maximum(i - half, 0), 0))
    return pl.pallas_call(
        tail_kernel,
        grid_spec=pltpu.PrefetchScalarGridSpec(
            num_scalar_prefetch=1,
            grid=(CHUNKS,),
            in_specs=[FIRST_HALF, SECOND_HALF] + [rows(D)] * 2 + [still(D, 3 * OWN_D), still(OWN_D, D), still(8, D), still(3, 1, OWN_D)]
            + [pl.BlockSpec((4, CHUNK, OWN_D), lambda i, at: (0, (i + half * (1 - at[0])) % CHUNKS, 0))]
            + [ANY_SPEC] * len(after),
            out_specs=[kept, sent, kept, sent, still(8, D)],
        ),
        out_shape=[shaped(TOK_DEV, D)] * 4 + [shaped(8, D, kind=F32)],
        compiler_params=params(60, dimension_semantics=("arbitrary",)),
        cost_estimate=cost(2 * SEQ * D * 4 * OWN_D, 16 << 20),
        name="tail",
    )(place, other, mine, mlp, q2, wp, wd, vec, gb, pieces, *after)


def last_kernel(place_ref, tok_ref, grad_ref, keep_out, got_out, keep_in, got_in, vec_ref, *refs):
    out_ref, in_ref, done_ref = refs[-3:]
    done_ref[...] = jnp.zeros_like(done_ref)
    tok = tok_ref[...].astype(F32)
    out_ref[...] = (tok + keep_out[...].astype(F32) + got_out[...].astype(F32) + vec_ref[0:1, :]).astype(BF16)
    normal, scale = standardise(tok)
    mixed = keep_in[...].astype(F32) + got_in[...].astype(F32)
    base = place_ref[0] * TOK_DEV + pl.program_id(0) * CHUNK
    position = base + lax.broadcasted_iota(jnp.int32, (CHUNK, D), 0)
    seed = jnp.where(position < place_ref[1], grad_ref[...].astype(F32), 0.0)
    mean = jnp.mean(mixed, axis=-1, keepdims=True)
    along = jnp.mean(mixed * normal, axis=-1, keepdims=True)
    in_ref[...] = seed + scale * (mixed - mean - normal * along)


def last(place, tok, grad, keep_out, got_out, keep_in, got_in, vec, after):
    return pl.pallas_call(
        last_kernel,
        grid=(TOK_DEV // CHUNK,),
        in_specs=[SMEM_SPEC] + [by_rows(D)] * 6 + [whole(8, D)] + [ANY_SPEC] * len(after),
        out_specs=[by_rows(D)] * 2 + [whole(1, 128)],
        out_shape=[shaped(TOK_DEV, D), shaped(TOK_DEV, D, kind=F32), shaped(1, 128, kind=F32)],
        compiler_params=params(60, dimension_semantics=("arbitrary",)),
        cost_estimate=cost(1e9),
        name="last",
    )(place, tok, grad, keep_out, got_out, keep_in, got_in, vec, *after)


def rider_kernel(place_ref, mine_ref, other_ref, expand_ref, seed_ref, *refs):
    out_ref, done_ref = refs[-2:]
    done_ref[...] = jnp.zeros_like(done_ref)
    first = place_ref[0] == 0
    mine, other = mine_ref[...], other_ref[...]
    left = jnp.where(first, mine[4:7, :OWN_D], other[4:7, :OWN_D])
    right = jnp.where(first, other[4:7, OWN_D:], mine[4:7, OWN_D:])
    out_ref[...] = jnp.concatenate([
        jnp.concatenate([left, right], axis=1), expand_ref[:, :D], expand_ref[:, D:], seed_ref[...],
        mine[0:4, :] + other[0:4, :], jnp.zeros((6, D), F32),
    ], axis=0).astype(BF16)


def make_rider(place, mine, other, expand, seed, after):
    return pl.pallas_call(
        rider_kernel,
        grid=(1,),
        in_specs=[SMEM_SPEC, whole(8, D), whole(8, D), whole(1, OWN_FF), whole(1, D)] + [ANY_SPEC] * len(after),
        out_specs=[whole(16, D), whole(1, 128)],
        out_shape=[shaped(16, D), shaped(1, 128, kind=F32)],
        compiler_params=params(60, dimension_semantics=("arbitrary",)),
        cost_estimate=cost(1e5, 1 << 16),
        name="rider",
    )(place, mine, other, expand, seed, *after)


def held_block(bits, place_ref, held, rows):
    a, b, c = [bit ^ place_ref[2 + axis] for axis, bit in enumerate(bits)]
    which = 2 * a + c + a * (b - c)
    return which, pl.multiple_of((b + a * (c - b)) * rows, rows)


def finish_ffn_kernel(place_ref, *refs):
    ins, (contract_out, expand_out, done_ref, held, contract, expand, in_sems, out_sems) = refs[:4], refs[-8:]
    done_ref[...] = jnp.zeros_like(done_ref)
    core = place_ref[0]
    loads = [pltpu.make_async_copy(ins[i], held.at[i], in_sems.at[i]) for i in range(4)]
    stores = [pltpu.make_async_copy(contract, contract_out, out_sems.at[0]),
              pltpu.make_async_copy(expand, expand_out, out_sems.at[1])]
    for load in loads:
        load.start()
    for load in loads:
        load.wait()
    for c in range(3):
        for at in range(8):
            bits = [at >> (2 - (axis - c) % 3) & 1 for axis in range(3)]
            which, start = held_block(bits, place_ref, held, OWN_D)
            value = held[which, pl.ds(pl.multiple_of(start + c * 128, 128), 128), :].astype(F32)
            row = c * 1024 + at * 128
            if row < OWN_FF:
                contract[row:row + 128, :] = value
            else:
                half, block = divmod((row - OWN_FF) // 128, 6)
                base = (core if half == 0 else 1 - core) * OWN_FF + block * HIDDEN_BLOCK
                for g in range(3):
                    expand[g * 128:(g + 1) * 128, pl.ds(pl.multiple_of(base, 128), HIDDEN_BLOCK)] = (
                        value[:, g * HIDDEN_BLOCK:(g + 1) * HIDDEN_BLOCK])
        if c == 1:
            stores[0].start()
    stores[1].start()
    for store in stores:
        store.wait()


def finish_ffn(place, parts):
    big = [(OWN_FF, D), (OWN_D, FF)]
    return pl.pallas_call(
        finish_ffn_kernel,
        in_specs=[SMEM_SPEC] + [ANY_SPEC] * 4,
        out_specs=[ANY_SPEC] * 2 + [VMEM_SPEC],
        out_shape=[shaped(*dims, kind=F32) for dims in big] + [shaped(1, 128, kind=F32)],
        scratch_shapes=[pltpu.VMEM((4, 768, D), BF16)] + [pltpu.VMEM(dims, F32) for dims in big]
        + [pltpu.SemaphoreType.DMA((4,)), pltpu.SemaphoreType.DMA((2,))],
        compiler_params=params(40),
        cost_estimate=cost(1e8, 16 << 20),
        name="finish_ffn",
    )(place, *parts)


def finish_kernel(place_ref, *refs):
    ins = refs[:4]
    rider_ref = refs[4]
    outs = refs[-15:-13]
    small = refs[-13:-5]
    held, project, dense, in_sems, out_sems = refs[-5:]
    core = place_ref[0]
    loads = [pltpu.make_async_copy(ins[i], held.at[i], in_sems.at[i]) for i in range(4)]
    stores = [pltpu.make_async_copy(stage, outs[i], out_sems.at[i]) for i, stage in enumerate((project, dense))]
    for load in loads:
        load.start()
    rows = rider_ref[...].astype(F32)
    pieces = [(0, 0, 1, 1), (0, 1, 2, 0), (1, 0, 2, 1)]
    for t, (r0, h0, r1, h1) in enumerate(pieces):
        small[0][t * OWN_D:(t + 1) * OWN_D] = jnp.where(
            core == 0, rows[r0:r0 + 1, h0 * OWN_D:(h0 + 1) * OWN_D], rows[r1:r1 + 1, h1 * OWN_D:(h1 + 1) * OWN_D]).reshape(OWN_D)
    small[1][:D] = rows[3:4, :].reshape(D)
    small[1][D:] = rows[4:5, :].reshape(D)
    for i in range(5):
        row = rows[5 + i:6 + i, :]
        value = jnp.where(core == 0, row[:, :OWN_D], row[:, OWN_D:]).reshape(OWN_D)
        small[3 + i][...] = value
        if i == 0:
            small[2][...] = value
    for load in loads:
        load.wait()
    for at in range(8):
        bits = a, b, c = at // 4, at // 2 % 2, at % 2
        which, start = held_block(bits, place_ref, held, 192)
        for piece in range(3):
            value = held[which, pl.ds(pl.multiple_of(start + piece * 64, 64), 64), :].astype(F32)
            row = a * 768 + (c * 2 + b if a else b * 2 + c) * 192 + piece * 64
            if row < OWN_D:
                dense[row:row + 64, :] = value
            else:
                half, row = divmod(row - OWN_D, 3 * OWN_D // 2)
                t, row = divmod(row, OWN_D // 2)
                cols = pl.ds(pl.multiple_of((core if half == 0 else 1 - core) * OWN_D + t * D, 128), OWN_D)
                project[row:row + 64, cols] = value[:, :OWN_D]
                project[OWN_D // 2 + row:OWN_D // 2 + row + 64, cols] = value[:, OWN_D:]
        if at == 3:
            stores[1].start()
    stores[0].start()
    for store in stores:
        store.wait()


def finish(place, parts, rider, after):
    big = [(OWN_D, 3 * D), (OWN_D, D)]
    vectors = [3 * OWN_D, OWN_FF] + [OWN_D] * 6
    return pl.pallas_call(
        finish_kernel,
        in_specs=[SMEM_SPEC] + [ANY_SPEC] * 4 + [VMEM_SPEC] + [ANY_SPEC] * len(after),
        out_specs=[ANY_SPEC] * 2 + [VMEM_SPEC] * 8,
        out_shape=[shaped(*dims, kind=F32) for dims in big] + [shaped(n, kind=F32) for n in vectors],
        scratch_shapes=[pltpu.VMEM((4, 384, D), BF16)] + [pltpu.VMEM(dims, F32) for dims in big]
        + [pltpu.SemaphoreType.DMA((4,)), pltpu.SemaphoreType.DMA((2,))],
        compiler_params=params(28),
        cost_estimate=cost(1e8, 8 << 20),
        name="finish",
    )(place, *parts, rider, *after)


def partner(chip, dim):
    step = 4 ** (dim % 3)
    at = (chip // step) % 4
    return chip + ((at ^ 1 if dim < 3 else 3 - at) - at) * step


def side_of(chip, dim):
    at = (chip // (4 ** (dim % 3))) % 4
    return (at ^ (at // 2)) & 1 if dim < 3 else at // 2


def first_dims(axis):
    return [(r * 2 + s, partner(r, axis + 3 * s) * 2 + s) for r in range(64) for s in range(2)]


def second_dims(axis):
    return [(r * 2 + s, partner(r, axis + 3 * (1 - s)) * 2 + s) for r in range(64) for s in range(2)]


def first_side(axis):
    chip, core = lax.axis_index("replica"), lax.axis_index("shard")
    return jnp.where(core == 0, side_of(chip, axis), side_of(chip, axis + 3))


def add_low(left, right, done=None):
    total = left.astype(F32) + right.astype(F32)
    return (total if done is None else total + done[:, :1]).astype(BF16)


def scatter_start(parts, k):
    return halve(parts, [(c + k) % 3 for c in range(3)])


def halve(parts, axes):
    sends, keeps, got = [], [], []
    for part, axis in zip(parts, axes):
        side = first_side(axis)
        if isinstance(part, tuple):
            sends.append(jnp.where(side == 0, part[1], part[0]))
            keeps.append(jnp.where(side == 0, part[0], part[1]))
        else:
            half = part.shape[0] // 2
            sends.append(lax.dynamic_slice_in_dim(part, (1 - side) * half, half, 0))
            keeps.append(lax.dynamic_slice_in_dim(part, side * half, half, 0))
    for send, axis in zip(sends, axes):
        got.append(lax.ppermute(send, BOTH, first_dims(axis)))
    return sends, keeps, got


def scatter_end(keeps, got, done=None):
    return [add_low(a, b, done) for a, b in zip(keeps, got)]


def gather(block, rider, done=None):
    size = block.shape[0]
    steps = []
    extend = lambda part: part if rider is None else jnp.concatenate([part, rider], axis=0)
    send = lambda part, axis: lax.ppermute(part, BOTH, first_dims(axis))
    near, far = extend(block), None
    for axis in range(3):
        got = send(near, axis)
        if far is None:
            far = got[:size]
            left, right = block, far
        else:
            far = send(right, 3 - axis)
            ends = [left, got[:left.shape[0]], right, far]
            if axis == 1:
                left, right = jnp.concatenate(ends[:2], axis=0), jnp.concatenate(ends[2:], axis=0)
        if rider is not None:
            rider = add_low(rider, got[-rider.shape[0]:], done if axis == 0 else None)
        near = extend(left)
        steps.append([got, far])
    return ends, rider, steps


def nothing_of(arrays):
    return sum(jnp.minimum(jnp.abs(a[:1, :1].astype(F32)), 0.0) for a in arrays)


def on_device(tokens, lengths, project_weight, project_bias, dense_weight, dense_bias, expand_weight, expand_bias,
              contract_weight, contract_bias, first_gain, first_shift, second_gain, second_shift, out_grad):
    core = lax.axis_index("shard")
    swap = lambda rows: lax.ppermute(rows, "shard", [(0, 1), (1, 0)])
    place = jnp.stack([core.astype(jnp.int32), lengths[0]] + [first_side(axis).astype(jnp.int32) for axis in range(3)])
    other_tokens = swap(tokens)
    other_grad = swap(out_grad)
    packed, b_expand = pack(
        project_bias, dense_bias, contract_bias, first_gain, first_shift, second_gain, second_shift, expand_bias)
    other_packed = swap(packed)
    other_expand = swap(expand_weight)
    other_project = swap(project_weight)
    tables = [jnp.asarray(t) for t in rotary_arrays()]

    n1, n2, seed, seed_sum, b_project, vec = prep(
        place, tokens, other_tokens, out_grad, other_grad, packed, other_packed)
    gc0, gc1, gc2, ge0, ge1, ge_send0, ge_send1, gbe, act, gh, w_expand = ffn(
        place, n2, seed, expand_weight, other_expand, b_expand, contract_weight)

    parts = [(gc0, gc1), (gc2, ge0), (jnp.concatenate([ge1, swap(ge_send0)], axis=0), swap(ge_send1))]

    sends, keeps, got = scatter_start(parts, 0)
    *qkvc, w_project = heads(place, n1, seed, tables, project_weight, other_project, b_project, dense_weight, sends)
    pieces, done = attend(0, 0, qkvc, tables, None, [])
    parts = scatter_end(keeps, got, done)
    sends, keeps, got = scatter_start(parts, 1)
    pieces, done = attend(0, 1, qkvc, tables, pieces, sends)
    parts = scatter_end(keeps, got, done)
    sends, keeps, got = scatter_start(parts, 2)
    pieces, done = attend(1, 0, qkvc, tables, pieces, sends)
    parts = scatter_end(keeps, got, done)
    block = jnp.concatenate(parts, axis=0)
    for axis, (pair, head) in enumerate(((1, 1), (2, 0), (2, 1))):
        got = lax.ppermute(block, BOTH, second_dims(axis))
        pieces, done = attend(pair, head, qkvc, tables, pieces, [block])
        if axis == 0:
            *merged, done = merge(0, act, gh, w_expand, contract_weight, [], [pieces])
        if axis == 1:
            mlp, q2, done = merge(1, act, gh, w_expand, contract_weight, merged, [pieces])
        if axis == 2:
            gd, gw0, gw1, gw_send0, gw_send1, gb, done = weights(place, n1, seed, pieces, [got])
        block = add_low(block, got, done)
    units = [(gd, gw0), (jnp.concatenate([gw1, swap(gw_send0)], axis=0), swap(gw_send1))]
    sends, keeps, late = halve(units, (1, 2))
    keep_out, send_out, keep_in, send_in, sums = tail(
        place, other_tokens, tokens, mlp, q2, w_project, dense_weight, vec, gb, pieces, sends + [block])
    ffn_ends, _, steps = gather(block, None)
    contract, expand, placed = finish_ffn(place, ffn_ends)

    rider, done = make_rider(place, sums, swap(sums), gbe, seed_sum, steps[0][:1])
    units = scatter_end(keeps, late, done)
    sends, keeps, late = halve(units, (2, 1))
    units = scatter_end(keeps, late)
    side = first_side(0)
    got = lax.ppermute(jnp.where(side == 0, units[1], units[0]), BOTH, first_dims(0))
    block = add_low(jnp.where(side == 0, units[0], units[1]), got)
    other_out, other_in = swap(send_out), swap(send_in)

    block = jnp.concatenate([block, rider], axis=0)
    for axis in (2, 0, 1):
        got, done = lax.ppermute(block, BOTH, second_dims(axis)), None
        if axis == 2:
            done = nothing_of(steps[1])
        if axis == 0:
            outputs, input_grad, done = last(
                place, tokens, out_grad, keep_out, other_out, keep_in, other_in, vec, [block])
        if axis == 1:
            done = nothing_of(steps[2])
        block = add_low(block, got, done)
    ends, rider, _ = gather(block[:192], block[192:], placed)
    project, dense, g_project, g_expand, g_dense, g_contract, gain_one, shift_one, gain_two, shift_two = finish(
        place, ends, rider, [])
    return (outputs, input_grad, project, g_project, dense, g_dense, expand, g_expand, contract, g_contract,
            gain_one, shift_one, gain_two, shift_two)


def solution(mesh):
    rows, first = P(("replica", "shard"), None), P("shard", None)
    one = P("shard")
    return jax.shard_map(
        on_device,
        mesh=mesh,
        in_specs=(rows, P("replica"), first, one, first, one, first, one, first, one, one, one, one, one, rows),
        out_specs=(rows, rows, first, one, first, one, first, one, first, one, one, one, one, one),
        check_vma=False,
    )
```

```python
import jax
import jax.numpy as jnp
import numpy as np
from jax import lax
from jax.experimental import pallas as pl
from jax.experimental.pallas import tpu as pltpu
from jax.sharding import PartitionSpec as P

HEADS = 12
HEAD_DIM = 64
D = 768
ROT = 16
FF = 3072
SEQ = 1024
TOK_DEV = 512
EPSILON = 1e-05
SCORE_SCALE = 0.125
F32 = jnp.float32
BF16 = jnp.bfloat16
MIB = 1024 * 1024
OWN_FF = FF // 2
OWN_D = D // 2
PAIR = 2 * HEAD_DIM
PAIRS = OWN_D // PAIR
HIDDEN_BLOCK = 256
CHUNK = 256
CHUNKS = SEQ // CHUNK
BOTH = ("replica", "shard")


def product(left, right):
    return lax.dot_general(left, right, (((1,), (0,)), ((), ())), preferred_element_type=F32)


def product_nt(left, right):
    return lax.dot_general(left, right, (((1,), (1,)), ((), ())), preferred_element_type=F32)


def product_tn(left, right):
    return lax.dot_general(left, right, (((0,), (0,)), ((), ())), preferred_element_type=F32)


def chunk_rows(c):
    return slice(c * CHUNK, (c + 1) * CHUNK)


def params(mib, **kw):
    return pltpu.CompilerParams(vmem_limit_bytes=mib * MIB, **kw)


def cost(flops, size=8 << 20, exps=0):
    return pl.CostEstimate(flops=int(flops), bytes_accessed=int(size), transcendentals=int(exps))


VMEM_SPEC = pl.BlockSpec(memory_space=pltpu.VMEM)
SMEM_SPEC = pl.BlockSpec(memory_space=pltpu.SMEM)
ANY_SPEC = pl.BlockSpec(memory_space=pl.ANY)


def shaped(*dims, kind=BF16):
    return jax.ShapeDtypeStruct(dims, kind)


def standardise(rows):
    mean = jnp.mean(rows, axis=-1, keepdims=True)
    centered = rows - mean
    scale = lax.rsqrt(jnp.mean(centered * centered, axis=-1, keepdims=True) + EPSILON)
    return centered * scale, scale


def whole(*dims):
    return pl.BlockSpec(dims, lambda *i: (0,) * len(dims))


def pack_kernel(project_ref, *refs):
    out_ref, expand_out = refs[-2:]
    expand_out[...] = refs[-3][...].astype(F32).reshape(1, OWN_FF)
    for t in range(3):
        out_ref[t:t + 1, :] = project_ref[t * OWN_D:(t + 1) * OWN_D].astype(F32).reshape(1, OWN_D)
    for i, ref in enumerate(refs[:-3]):
        out_ref[3 + i:4 + i, :] = ref[...].astype(F32).reshape(1, OWN_D)


def pack(*vectors):
    return pl.pallas_call(
        pack_kernel,
        grid=(1,),
        in_specs=[whole(v.shape[0]) for v in vectors],
        out_specs=[whole(16, OWN_D), whole(1, OWN_FF)],
        out_shape=[shaped(16, OWN_D, kind=F32), shaped(1, OWN_FF, kind=F32)],
        compiler_params=params(60, dimension_semantics=("arbitrary",)),
        cost_estimate=cost(1e5, 1 << 16),
        name="pack",
    )(*vectors)


def prepare(place_ref, mine_ref, other_ref, grad_ref, other_grad_ref, pack_ref, other_pack_ref,
            n1_ref, n2_ref, n2t_ref, seed_ref, sum_ref, head_bias_ref, vec_ref):
    side = place_ref[0]
    length = place_ref[1]
    first = jnp.where(side == 0, pack_ref[...], other_pack_ref[...])
    second = jnp.where(side == 0, other_pack_ref[...], pack_ref[...])
    for t in range(3):
        blocks = [(first, second)[row // 3][row % 3:row % 3 + 1, :] for row in (2 * t, 2 * t + 1)]
        head_bias_ref[:, t * OWN_D:(t + 1) * OWN_D] = jnp.where(side == 0, blocks[0], blocks[1])
    full = [jnp.concatenate([first[r:r + 1, :], second[r:r + 1, :]], axis=1) for r in range(3, 9)]
    vec_ref[0:1, :] = full[0] + full[1]
    vec_ref[1:2, :] = full[2]
    vec_ref[2:3, :] = full[4]
    total = jnp.zeros((1, D), F32)
    for part in range(2):
        source, cot = (mine_ref, grad_ref) if part == 0 else (other_ref, other_grad_ref)
        base = (side if part == 0 else 1 - side) * TOK_DEV
        for c in range(TOK_DEV // CHUNK):
            rows = chunk_rows(c)
            start = pl.multiple_of(base + c * CHUNK, CHUNK)
            dest = pl.ds(start, CHUNK)
            normal, _ = standardise(source[rows, :].astype(F32))
            n1_ref[dest, :] = (normal * full[2] + full[3]).astype(BF16)
            two = (normal * full[4] + full[5]).astype(BF16)
            n2_ref[dest, :] = two
            n2t_ref[:, dest] = two.T
            position = start + lax.broadcasted_iota(jnp.int32, (CHUNK, D), 0)
            seed = jnp.where(position < length, cot[rows, :].astype(F32), 0.0)
            total += jnp.sum(seed, axis=0, keepdims=True)
            seed_ref[dest, :] = seed.astype(BF16)
    sum_ref[...] = total


FIRST_HALF = pl.BlockSpec((CHUNK, D), lambda i, at: (jnp.minimum(i, CHUNKS // 2 - 1), 0))
SECOND_HALF = pl.BlockSpec((CHUNK, D), lambda i, at: (jnp.maximum(i - CHUNKS // 2, 0), 0))


def gelu_pair(hidden):
    size = jnp.abs(hidden)
    near = 1.0 / (1.0 + (0.3275911 * 0.7071067811865476) * size)
    bell = jnp.exp(-0.5 * hidden * hidden)
    poly = 0.5 * 1.061405429 * near - 0.5 * 1.453152027
    poly = poly * near + 0.5 * 1.421413741
    poly = poly * near - 0.5 * 0.284496736
    poly = poly * near + 0.5 * 0.254829592
    tail = poly * near * bell
    phi = jnp.where(hidden >= 0, 1.0 - tail, tail)
    return hidden * phi, phi + hidden * bell * 0.3989422804014327


def ffn_kernel(place_ref, tok_ref, other_tok_ref, grad_ref, other_grad_ref, pack_ref, other_pack_ref,
               mine_ref, other_ref, be_ref, wc_ref,
               gc0_ref, gc1_ref, gc2_ref, keep0_ref, keep1_ref, send0_ref, send1_ref, gbe_ref, act_ref, gh_ref, we_ref,
               n1_out, seed_out, sum_ref, head_bias_ref, vec_ref, n1_ref, n2_ref, n2t_ref, seed_ref, sems):
    step = pl.program_id(0)
    stores = [pltpu.make_async_copy(n1_ref, n1_out, sems.at[0]), pltpu.make_async_copy(seed_ref, seed_out, sems.at[1])]

    @pl.when(step == 0)
    def _():
        prepare(place_ref, tok_ref, other_tok_ref, grad_ref, other_grad_ref, pack_ref, other_pack_ref,
                n1_ref, n2_ref, n2t_ref, seed_ref, sum_ref, head_bias_ref, vec_ref)
        for store in stores:
            store.start()

    @pl.when(step == pl.num_programs(0) - 1)
    def _():
        for store in stores:
            store.wait()

    start = pl.multiple_of(place_ref[0] * OWN_D, OWN_D)
    we_ref[pl.ds(start, OWN_D), :] = mine_ref[...]
    we_ref[pl.ds(OWN_D - start, OWN_D), :] = other_ref[...]
    bias = be_ref[...]
    total = jnp.zeros((1, HIDDEN_BLOCK), F32)
    for c in range(CHUNKS):
        rows = chunk_rows(c)
        hidden = product(n2_ref[rows, :], we_ref[...]) + bias
        value, slope = gelu_pair(hidden)
        act_ref[rows, :] = value.astype(BF16)
        gh = (product_nt(seed_ref[rows, :], wc_ref[...]) * slope).astype(BF16)
        gh_ref[rows, :] = gh
        total += jnp.sum(gh.astype(F32), axis=0, keepdims=True)
    gbe_ref[...] = total
    gc = product_tn(act_ref[...], seed_ref[...]).astype(BF16)

    keep = product(n2t_ref[pl.ds(start, OWN_D), :], gh_ref[...]).astype(BF16)
    send = product(n2t_ref[pl.ds(OWN_D - start, OWN_D), :], gh_ref[...]).astype(BF16)
    for low, high, ref in ((0, 2, gc0_ref), (2, 4, gc1_ref), (4, 6, gc2_ref)):
        @pl.when((step >= low) & (step < high))
        def _(ref=ref):
            ref[...] = gc

    for low, high, ref, value in ((0, 4, keep0_ref, keep), (4, 6, keep1_ref, keep), (0, 2, send0_ref, send), (2, 6, send1_ref, send)):
        @pl.when((step >= low) & (step < high))
        def _(ref=ref, value=value):
            for g in range(3):
                ref[:, g * HIDDEN_BLOCK:(g + 1) * HIDDEN_BLOCK] = value[g * 128:(g + 1) * 128, :]


def ffn(place, tokens, other_tokens, grad, other_grad, packed, other_packed, mine, other, be, wc):
    steps = OWN_FF // HIDDEN_BLOCK
    rows_block = pl.BlockSpec((HIDDEN_BLOCK, D), lambda i, at: (i, 0))
    cols_block = pl.BlockSpec((OWN_D, HIDDEN_BLOCK), lambda i, at: (0, at[0] * steps + i))
    bias_block = pl.BlockSpec((1, HIDDEN_BLOCK), lambda i, at: (0, i))
    part = lambda rows, low, high: pl.BlockSpec((rows, D), lambda i, at: (jnp.clip(i, low, high - 1) - low, 0))
    tall_block = pl.BlockSpec((SEQ, HIDDEN_BLOCK), lambda i, at: (0, i))
    return pl.pallas_call(
        ffn_kernel,
        grid_spec=pltpu.PrefetchScalarGridSpec(
            num_scalar_prefetch=1,
            grid=(steps,),
            in_specs=[whole(TOK_DEV, D)] * 4 + [whole(16, OWN_D)] * 2 + [cols_block, cols_block, bias_block, rows_block],
            out_specs=[part(HIDDEN_BLOCK, 0, 2), part(HIDDEN_BLOCK, 2, 4), part(HIDDEN_BLOCK, 4, 6),
                       part(128, 0, 4), part(128, 4, 6), part(128, 0, 2), part(128, 2, 6), bias_block, tall_block, tall_block,
                       pl.BlockSpec((D, HIDDEN_BLOCK), lambda i, at: (0, i)), ANY_SPEC, ANY_SPEC,
                       whole(1, D), whole(1, 3 * OWN_D), whole(8, D)],
            scratch_shapes=[pltpu.VMEM((SEQ, D), BF16), pltpu.VMEM((SEQ, D), BF16), pltpu.VMEM((D, SEQ), BF16),
                            pltpu.VMEM((SEQ, D), BF16), pltpu.SemaphoreType.DMA((2,))],
        ),
        out_shape=[shaped(512, D)] * 4 + [shaped(256, D)] * 2 + [shaped(512, D), shaped(1, OWN_FF, kind=F32),
                   shaped(SEQ, OWN_FF), shaped(SEQ, OWN_FF), shaped(D, OWN_FF), shaped(SEQ, D), shaped(SEQ, D),
                   shaped(1, D, kind=F32), shaped(1, 3 * OWN_D, kind=F32), shaped(8, D, kind=F32)],
        compiler_params=params(60, dimension_semantics=("arbitrary",)),
        cost_estimate=cost(8 * SEQ * D * OWN_FF, 20 << 20, 2 * SEQ * OWN_FF),
        name="ffn",
    )(place, tokens, other_tokens, grad, other_grad, packed, other_packed, mine, other, be, wc)


def merge_kernel(act_ref, gh_ref, we_ref, wc_ref, *refs):
    mlp_ref, q2_ref, done_ref = refs[-3:]
    done_ref[...] = jnp.zeros_like(done_ref)
    mlp_ref[...] = product(act_ref[...], wc_ref[...]).astype(BF16)
    q2_ref[...] = product_nt(gh_ref[...], we_ref[...]).astype(BF16)


def merge(half, act, gh, we, wc, held, after):
    rows = lambda cols: pl.BlockSpec((CHUNK, cols), lambda i: (2 * half + i, 0))
    return pl.pallas_call(
        merge_kernel,
        grid=(2,),
        in_specs=[rows(OWN_FF), rows(OWN_FF), whole(D, OWN_FF), whole(OWN_FF, D)] + [ANY_SPEC] * (len(held) + len(after)),
        out_specs=[rows(D), rows(D), whole(1, 128)],
        out_shape=[shaped(SEQ, D)] * 2 + [shaped(1, 128, kind=F32)],
        input_output_aliases={4: 0, 5: 1} if held else {},
        compiler_params=params(28, dimension_semantics=("arbitrary",)),
        cost_estimate=cost(2 * SEQ * D * OWN_FF),
        name="merge",
    )(act, gh, we, wc, *held, *after)


def rotary_arrays():
    frequency = (np.float32(10000.0) ** (-np.arange(0, ROT, 2, dtype=np.float32) / np.float32(ROT))).astype(np.float32)
    angles = (np.arange(SEQ, dtype=np.float32)[:, None] * frequency[None, :]).astype(np.float64)
    cos, sin = np.cos(angles), np.sin(angles)
    half = ROT // 2
    keep = np.ones((SEQ, HEAD_DIM))
    up = np.zeros((SEQ, HEAD_DIM))
    down = np.zeros((SEQ, HEAD_DIM))
    keep[:, :half] = cos
    keep[:, half:ROT] = cos
    down[:, :half] = -sin
    up[:, half:ROT] = sin
    return [np.tile(t, (1, 2)).astype(np.float32) for t in (keep, up, down)]


def turn(rows, keep, up, down):
    return rows * keep + pltpu.roll(rows, ROT // 2, 1) * up + pltpu.roll(rows, PAIR - ROT // 2, 1) * down


def heads_kernel(place_ref, n1_ref, seed_ref, keep_ref, up_ref, down_ref, mine_ref, other_ref, bp_ref, wd_ref, *rest):
    q_ref, k_ref, v_ref, c_ref, wp_ref = rest[-5:]

    @pl.when(pl.program_id(0) == 0)
    def _():
        start = pl.multiple_of(place_ref[0] * OWN_D, OWN_D)
        for t in range(3):
            cols = pl.ds(pl.multiple_of(start + t * D, 128), OWN_D)
            wp_ref[pl.ds(start, OWN_D), t * OWN_D:(t + 1) * OWN_D] = mine_ref[:, cols]
            wp_ref[pl.ds(OWN_D - start, OWN_D), t * OWN_D:(t + 1) * OWN_D] = other_ref[:, cols]

    packed = product(n1_ref[...], wp_ref[...]) + bp_ref[...]
    tables = keep_ref[...], up_ref[...], down_ref[...]
    for p in range(PAIRS):
        cols = slice(p * PAIR, (p + 1) * PAIR)
        q = packed[:, p * PAIR:(p + 1) * PAIR]
        k = packed[:, OWN_D + p * PAIR:OWN_D + (p + 1) * PAIR]
        q_ref[:, cols] = (turn(q, *tables).astype(BF16) * SCORE_SCALE).astype(BF16)
        k_ref[:, cols] = turn(k, *tables).astype(BF16)
    v_ref[...] = packed[:, 2 * OWN_D:].astype(BF16)
    c_ref[...] = product_nt(seed_ref[...], wd_ref[...]).astype(BF16)


def by_rows(columns):
    return pl.BlockSpec((CHUNK, columns), lambda i, *at: (i, 0))


def heads(place, n1, seed, tables, mine, other, bp, wd, after):
    return pl.pallas_call(
        heads_kernel,
        grid=(CHUNKS,),
        in_specs=[SMEM_SPEC] + [by_rows(D)] * 2 + [by_rows(PAIR)] * 3
        + [whole(OWN_D, 3 * D), whole(OWN_D, 3 * D), whole(1, 3 * OWN_D), whole(OWN_D, D)] + [ANY_SPEC] * len(after),
        out_specs=[by_rows(OWN_D)] * 4 + [whole(D, 3 * OWN_D)],
        out_shape=[shaped(SEQ, OWN_D)] * 4 + [shaped(D, 3 * OWN_D)],
        compiler_params=params(28, dimension_semantics=("arbitrary",)),
        cost_estimate=cost(2 * SEQ * D * 4 * OWN_D),
        name="heads",
    )(place, n1, seed, *tables, mine, other, bp, wd, *after)


def attend_kernel(head, *refs):
    q_ref, k_ref, v_ref, c_ref, keep_ref, up_ref, down_ref = refs[:7]
    before_ref = refs[7]
    out_ref, done_ref, dk_s, dv_s = refs[-4:]
    done_ref[...] = jnp.zeros_like(done_ref)
    lane = lax.broadcasted_iota(jnp.int32, (CHUNK, PAIR), 1)
    mine = (lane < HEAD_DIM) if head == 0 else (lane >= HEAD_DIM)
    diagonal = lax.broadcasted_iota(jnp.int32, (CHUNK, CHUNK), 0) >= lax.broadcasted_iota(jnp.int32, (CHUNK, CHUNK), 1)

    def put(at, rows, value):
        low = value.astype(BF16)
        out_ref[at, rows, :] = low if head == 0 else jnp.where(mine, low, before_ref[at, rows, :])

    for c in reversed(range(CHUNKS)):
        rows = chunk_rows(c)
        span = (c + 1) * CHUNK
        q = jnp.where(mine, q_ref[rows, :], 0)
        gc = jnp.where(mine, c_ref[rows, :], 0)
        scores = jnp.where(diagonal, product_nt(q, k_ref[c * CHUNK:span, :]), -1e30)
        if c > 0:
            scores = jnp.concatenate([product_nt(q, k_ref[:c * CHUNK, :]), scores], axis=1)
        top = jnp.max(scores, axis=1, keepdims=True)
        power = jnp.exp(scores - top)
        inverse = 1.0 / jnp.sum(power, axis=1, keepdims=True)
        power_low = power.astype(BF16)
        ctx = jnp.where(mine, product(power_low, v_ref[:span, :]), 0.0) * inverse
        put(0, rows, ctx)
        gc_scaled = (gc.astype(F32) * inverse).astype(BF16)
        delta = jnp.sum(ctx * gc_scaled.astype(F32), axis=1, keepdims=True)
        grad_prob = product_nt(gc_scaled, v_ref[:span, :])
        grad_scores = (power * (grad_prob - delta)).astype(BF16)
        back = keep_ref[rows, :], -up_ref[rows, :], -down_ref[rows, :]
        grad_q = jnp.where(mine, product(grad_scores, k_ref[:span, :]), 0.0) * SCORE_SCALE
        put(1, rows, turn(grad_q, *back))
        dv = product_tn(power_low, gc_scaled)
        dk = product_tn(grad_scores, q)
        if c == CHUNKS - 1:
            dv_s[...] = dv
            dk_s[...] = dk
        else:
            dv_s[:span, :] += dv
            dk_s[:span, :] += dk
    for c in range(CHUNKS):
        rows = chunk_rows(c)
        back = keep_ref[rows, :], -up_ref[rows, :], -down_ref[rows, :]
        put(2, rows, turn(dk_s[rows, :], *back))
        put(3, rows, dv_s[rows, :])


def attend(pair, head, qkvc, tables, pieces, after):
    def kernel(*refs):
        attend_kernel(head, *refs)

    spec = pl.BlockSpec((SEQ, PAIR), lambda i: (0, pair))
    block = pl.BlockSpec((4, SEQ, PAIR), lambda i: (0, 0, pair))
    first = pieces is None
    held = [] if first else [pieces]
    return pl.pallas_call(
        kernel,
        grid=(1,),
        in_specs=[spec] * 4 + [whole(SEQ, PAIR)] * 3 + ([] if first else [block if head == 1 else ANY_SPEC]) + [ANY_SPEC] * len(after),
        out_specs=[block, whole(1, 128)],
        out_shape=[shaped(4, SEQ, OWN_D), shaped(1, 128, kind=F32)],
        input_output_aliases={} if first else {7: 0},
        scratch_shapes=[pltpu.VMEM((SEQ, PAIR), F32)] * 2,
        compiler_params=params(28, dimension_semantics=("arbitrary",)),
        cost_estimate=cost(5e9, 4 << 20, SEQ * SEQ),
        name="attend",
    )(*qkvc, *tables, *held, *after)


def weights_kernel(place_ref, n1_ref, seed_ref, piece_ref, *refs):
    gd_ref, own0_ref, own1_ref, send0_ref, send1_ref, gb_ref, done_ref, n1t_ref = refs[-8:]
    done_ref[...] = jnp.zeros_like(done_ref)
    step = pl.program_id(0)
    half = OWN_D // 2

    @pl.when(step == 0)
    def _():
        gd_ref[...] = product_tn(piece_ref[0], seed_ref[...]).astype(BF16)
        for c in range(CHUNKS):
            rows = chunk_rows(c)
            n1t_ref[:, rows] = n1_ref[rows, :].T

    own = [(own0_ref, 0), (own0_ref, half), (own1_ref, 0)]
    sent = [(send0_ref, 0), (send1_ref, 0), (send1_ref, half)]
    for t in range(3):
        @pl.when(step == t + 1)
        def _(t=t):
            start = pl.multiple_of(place_ref[0] * OWN_D, OWN_D)
            grads = piece_ref[0]
            for (ref, row), at in ((sent[t], OWN_D - start), (own[t], start)):
                full = product(n1t_ref[pl.ds(at, OWN_D), :], grads).astype(BF16)
                ref[row:row + half, :OWN_D] = full[:half]
                ref[row:row + half, OWN_D:] = full[half:]
            gb_ref[0] = jnp.sum(grads.astype(F32), axis=0, keepdims=True)


def weights(place, n1, seed, pieces, after):
    half = OWN_D // 2
    return pl.pallas_call(
        weights_kernel,
        grid=(4,),
        in_specs=[SMEM_SPEC, whole(SEQ, D), whole(SEQ, D), pl.BlockSpec((1, SEQ, OWN_D), lambda i: (i, 0, 0))]
        + [ANY_SPEC] * len(after),
        out_specs=[whole(OWN_D, D), whole(OWN_D, D), whole(half, D), whole(half, D), whole(OWN_D, D),
                   pl.BlockSpec((1, 1, OWN_D), lambda i: (jnp.maximum(i - 1, 0), 0, 0)), whole(1, 128)],
        out_shape=[shaped(OWN_D, D), shaped(OWN_D, D), shaped(half, D), shaped(half, D), shaped(OWN_D, D),
                   shaped(3, 1, OWN_D, kind=F32), shaped(1, 128, kind=F32)],
        scratch_shapes=[pltpu.VMEM((D, SEQ), BF16)],
        compiler_params=params(28, dimension_semantics=("arbitrary",)),
        cost_estimate=cost(2 * SEQ * D * 4 * OWN_D),
        name="weights",
    )(place, n1, seed, pieces, *after)


def tail_kernel(place_ref, other_ref, mine_ref, mlp_ref, q2_ref, wp_ref, wd_ref, vec_ref, gb_ref, piece_ref, *refs):
    keep_out, send_out, keep_in, send_in, sums_ref = refs[-5:]
    step = pl.program_id(0)
    grads = jnp.concatenate([piece_ref[t] for t in (1, 2, 3)], axis=1)
    out = mlp_ref[...].astype(F32) + product(piece_ref[0], wd_ref[...])
    q1 = product_nt(grads, wp_ref[...])
    q2 = q2_ref[...].astype(F32)
    normal, _ = standardise(jnp.where(step < CHUNKS // 2, other_ref[...], mine_ref[...]).astype(F32))
    sums = jnp.concatenate([jnp.sum(term, axis=0, keepdims=True) for term in (q1 * normal, q1, q2 * normal, q2)], axis=0)
    mixed = q1 * vec_ref[1:2, :] + q2 * vec_ref[2:3, :]

    @pl.when(step < CHUNKS // 2)
    def _():
        send_out[...] = out.astype(BF16)
        send_in[...] = mixed.astype(BF16)

    @pl.when(step >= CHUNKS // 2)
    def _():
        keep_out[...] = out.astype(BF16)
        keep_in[...] = mixed.astype(BF16)

    @pl.when(step == 0)
    def _():
        sums_ref[0:4, :] = sums
        for t in range(3):
            sums_ref[4 + t:5 + t, :OWN_D] = gb_ref[t]
            sums_ref[4 + t:5 + t, OWN_D:] = gb_ref[t]

    @pl.when(step > 0)
    def _():
        sums_ref[0:4, :] += sums


def tail(place, other, mine, mlp, q2, wp, wd, vec, gb, pieces, after):
    half = CHUNKS // 2
    rows = lambda cols: pl.BlockSpec((CHUNK, cols), lambda i, at: ((i + half * (1 - at[0])) % CHUNKS, 0))
    still = lambda *dims: pl.BlockSpec(dims, lambda i, at: (0,) * len(dims))
    sent = pl.BlockSpec((CHUNK, D), lambda i, at: (jnp.minimum(i, half - 1), 0))
    kept = pl.BlockSpec((CHUNK, D), lambda i, at: (jnp.maximum(i - half, 0), 0))
    return pl.pallas_call(
        tail_kernel,
        grid_spec=pltpu.PrefetchScalarGridSpec(
            num_scalar_prefetch=1,
            grid=(CHUNKS,),
            in_specs=[FIRST_HALF, SECOND_HALF] + [rows(D)] * 2 + [still(D, 3 * OWN_D), still(OWN_D, D), still(8, D), still(3, 1, OWN_D)]
            + [pl.BlockSpec((4, CHUNK, OWN_D), lambda i, at: (0, (i + half * (1 - at[0])) % CHUNKS, 0))]
            + [ANY_SPEC] * len(after),
            out_specs=[kept, sent, kept, sent, still(8, D)],
        ),
        out_shape=[shaped(TOK_DEV, D)] * 4 + [shaped(8, D, kind=F32)],
        compiler_params=params(60, dimension_semantics=("arbitrary",)),
        cost_estimate=cost(2 * SEQ * D * 4 * OWN_D, 16 << 20),
        name="tail",
    )(place, other, mine, mlp, q2, wp, wd, vec, gb, pieces, *after)


def last_kernel(place_ref, tok_ref, grad_ref, keep_out, got_out, keep_in, got_in, vec_ref, *refs):
    out_ref, in_ref, done_ref = refs[-3:]
    done_ref[...] = jnp.zeros_like(done_ref)
    tok = tok_ref[...].astype(F32)
    out_ref[...] = (tok + keep_out[...].astype(F32) + got_out[...].astype(F32) + vec_ref[0:1, :]).astype(BF16)
    normal, scale = standardise(tok)
    mixed = keep_in[...].astype(F32) + got_in[...].astype(F32)
    base = place_ref[0] * TOK_DEV + pl.program_id(0) * CHUNK
    position = base + lax.broadcasted_iota(jnp.int32, (CHUNK, D), 0)
    seed = jnp.where(position < place_ref[1], grad_ref[...].astype(F32), 0.0)
    mean = jnp.mean(mixed, axis=-1, keepdims=True)
    along = jnp.mean(mixed * normal, axis=-1, keepdims=True)
    in_ref[...] = seed + scale * (mixed - mean - normal * along)


def last(place, tok, grad, keep_out, got_out, keep_in, got_in, vec, after):
    return pl.pallas_call(
        last_kernel,
        grid=(TOK_DEV // CHUNK,),
        in_specs=[SMEM_SPEC] + [by_rows(D)] * 6 + [whole(8, D)] + [ANY_SPEC] * len(after),
        out_specs=[by_rows(D)] * 2 + [whole(1, 128)],
        out_shape=[shaped(TOK_DEV, D), shaped(TOK_DEV, D, kind=F32), shaped(1, 128, kind=F32)],
        compiler_params=params(60, dimension_semantics=("arbitrary",)),
        cost_estimate=cost(1e9),
        name="last",
    )(place, tok, grad, keep_out, got_out, keep_in, got_in, vec, *after)


def rider_kernel(place_ref, mine_ref, other_ref, expand_ref, seed_ref, *refs):
    out_ref, done_ref = refs[-2:]
    done_ref[...] = jnp.zeros_like(done_ref)
    first = place_ref[0] == 0
    mine, other = mine_ref[...], other_ref[...]
    left = jnp.where(first, mine[4:7, :OWN_D], other[4:7, :OWN_D])
    right = jnp.where(first, other[4:7, OWN_D:], mine[4:7, OWN_D:])
    out_ref[...] = jnp.concatenate([
        jnp.concatenate([left, right], axis=1), expand_ref[:, :D], expand_ref[:, D:], seed_ref[...],
        mine[0:4, :] + other[0:4, :], jnp.zeros((6, D), F32),
    ], axis=0).astype(BF16)


def make_rider(place, mine, other, expand, seed, after):
    return pl.pallas_call(
        rider_kernel,
        grid=(1,),
        in_specs=[SMEM_SPEC, whole(8, D), whole(8, D), whole(1, OWN_FF), whole(1, D)] + [ANY_SPEC] * len(after),
        out_specs=[whole(16, D), whole(1, 128)],
        out_shape=[shaped(16, D), shaped(1, 128, kind=F32)],
        compiler_params=params(60, dimension_semantics=("arbitrary",)),
        cost_estimate=cost(1e5, 1 << 16),
        name="rider",
    )(place, mine, other, expand, seed, *after)


def held_block(bits, place_ref, held, rows):
    a, b, c = [bit ^ place_ref[2 + axis] for axis, bit in enumerate(bits)]
    which = 2 * a + c + a * (b - c)
    return which, pl.multiple_of((b + a * (c - b)) * rows, rows)


def finish_ffn_kernel(place_ref, *refs):
    ins, (contract_out, expand_out, done_ref, held, contract, expand, in_sems, out_sems) = refs[:4], refs[-8:]
    done_ref[...] = jnp.zeros_like(done_ref)
    core = place_ref[0]
    loads = [pltpu.make_async_copy(ins[i], held.at[i], in_sems.at[i]) for i in range(4)]
    stores = [pltpu.make_async_copy(contract, contract_out, out_sems.at[0]),
              pltpu.make_async_copy(expand, expand_out, out_sems.at[1])]
    for load in loads:
        load.start()
    for load in loads:
        load.wait()
    for c in range(3):
        for at in range(8):
            bits = [at >> (2 - (axis - c) % 3) & 1 for axis in range(3)]
            which, start = held_block(bits, place_ref, held, OWN_D)
            value = held[which, pl.ds(pl.multiple_of(start + c * 128, 128), 128), :].astype(F32)
            row = c * 1024 + at * 128
            if row < OWN_FF:
                contract[row:row + 128, :] = value
            else:
                half, block = divmod((row - OWN_FF) // 128, 6)
                base = (core if half == 0 else 1 - core) * OWN_FF + block * HIDDEN_BLOCK
                for g in range(3):
                    expand[g * 128:(g + 1) * 128, pl.ds(pl.multiple_of(base, 128), HIDDEN_BLOCK)] = (
                        value[:, g * HIDDEN_BLOCK:(g + 1) * HIDDEN_BLOCK])
        if c == 1:
            stores[0].start()
    stores[1].start()
    for store in stores:
        store.wait()


def finish_ffn(place, parts):
    big = [(OWN_FF, D), (OWN_D, FF)]
    return pl.pallas_call(
        finish_ffn_kernel,
        in_specs=[SMEM_SPEC] + [ANY_SPEC] * 4,
        out_specs=[ANY_SPEC] * 2 + [VMEM_SPEC],
        out_shape=[shaped(*dims, kind=F32) for dims in big] + [shaped(1, 128, kind=F32)],
        scratch_shapes=[pltpu.VMEM((4, 768, D), BF16)] + [pltpu.VMEM(dims, F32) for dims in big]
        + [pltpu.SemaphoreType.DMA((4,)), pltpu.SemaphoreType.DMA((2,))],
        compiler_params=params(40),
        cost_estimate=cost(1e8, 16 << 20),
        name="finish_ffn",
    )(place, *parts)


def finish_kernel(place_ref, *refs):
    ins = refs[:4]
    rider_ref = refs[4]
    outs = refs[-15:-13]
    small = refs[-13:-5]
    held, project, dense, in_sems, out_sems = refs[-5:]
    core = place_ref[0]
    loads = [pltpu.make_async_copy(ins[i], held.at[i], in_sems.at[i]) for i in range(4)]
    stores = [pltpu.make_async_copy(stage, outs[i], out_sems.at[i]) for i, stage in enumerate((project, dense))]
    for load in loads:
        load.start()
    rows = rider_ref[...].astype(F32)
    pieces = [(0, 0, 1, 1), (0, 1, 2, 0), (1, 0, 2, 1)]
    for t, (r0, h0, r1, h1) in enumerate(pieces):
        small[0][t * OWN_D:(t + 1) * OWN_D] = jnp.where(
            core == 0, rows[r0:r0 + 1, h0 * OWN_D:(h0 + 1) * OWN_D], rows[r1:r1 + 1, h1 * OWN_D:(h1 + 1) * OWN_D]).reshape(OWN_D)
    small[1][:D] = rows[3:4, :].reshape(D)
    small[1][D:] = rows[4:5, :].reshape(D)
    for i in range(5):
        row = rows[5 + i:6 + i, :]
        value = jnp.where(core == 0, row[:, :OWN_D], row[:, OWN_D:]).reshape(OWN_D)
        small[3 + i][...] = value
        if i == 0:
            small[2][...] = value
    for load in loads:
        load.wait()
    for at in range(8):
        bits = a, b, c = at // 4, at // 2 % 2, at % 2
        which, start = held_block(bits, place_ref, held, 192)
        for piece in range(3):
            value = held[which, pl.ds(pl.multiple_of(start + piece * 64, 64), 64), :].astype(F32)
            row = a * 768 + (c * 2 + b if a else b * 2 + c) * 192 + piece * 64
            if row < OWN_D:
                dense[row:row + 64, :] = value
            else:
                half, row = divmod(row - OWN_D, 3 * OWN_D // 2)
                t, row = divmod(row, OWN_D // 2)
                cols = pl.ds(pl.multiple_of((core if half == 0 else 1 - core) * OWN_D + t * D, 128), OWN_D)
                project[row:row + 64, cols] = value[:, :OWN_D]
                project[OWN_D // 2 + row:OWN_D // 2 + row + 64, cols] = value[:, OWN_D:]
        if at == 3:
            stores[1].start()
    stores[0].start()
    for store in stores:
        store.wait()


def finish(place, parts, rider, after):
    big = [(OWN_D, 3 * D), (OWN_D, D)]
    vectors = [3 * OWN_D, OWN_FF] + [OWN_D] * 6
    return pl.pallas_call(
        finish_kernel,
        in_specs=[SMEM_SPEC] + [ANY_SPEC] * 4 + [VMEM_SPEC] + [ANY_SPEC] * len(after),
        out_specs=[ANY_SPEC] * 2 + [VMEM_SPEC] * 8,
        out_shape=[shaped(*dims, kind=F32) for dims in big] + [shaped(n, kind=F32) for n in vectors],
        scratch_shapes=[pltpu.VMEM((4, 384, D), BF16)] + [pltpu.VMEM(dims, F32) for dims in big]
        + [pltpu.SemaphoreType.DMA((4,)), pltpu.SemaphoreType.DMA((2,))],
        compiler_params=params(28),
        cost_estimate=cost(1e8, 8 << 20),
        name="finish",
    )(place, *parts, rider, *after)


def partner(chip, dim):
    step = 4 ** (dim % 3)
    at = (chip // step) % 4
    return chip + ((at ^ 1 if dim < 3 else 3 - at) - at) * step


def side_of(chip, dim):
    at = (chip // (4 ** (dim % 3))) % 4
    return (at ^ (at // 2)) & 1 if dim < 3 else at // 2


def first_dims(axis):
    return [(r * 2 + s, partner(r, axis + 3 * s) * 2 + s) for r in range(64) for s in range(2)]


def second_dims(axis):
    return [(r * 2 + s, partner(r, axis + 3 * (1 - s)) * 2 + s) for r in range(64) for s in range(2)]


def first_side(axis):
    chip, core = lax.axis_index("replica"), lax.axis_index("shard")
    return jnp.where(core == 0, side_of(chip, axis), side_of(chip, axis + 3))


def add_low(left, right, done=None):
    total = left.astype(F32) + right.astype(F32)
    return (total if done is None else total + done[:, :1]).astype(BF16)


def scatter_start(parts, k):
    return halve(parts, [(c + k) % 3 for c in range(3)])


def halve(parts, axes):
    sends, keeps, got = [], [], []
    for part, axis in zip(parts, axes):
        side = first_side(axis)
        if isinstance(part, tuple):
            sends.append(jnp.where(side == 0, part[1], part[0]))
            keeps.append(jnp.where(side == 0, part[0], part[1]))
        else:
            half = part.shape[0] // 2
            sends.append(lax.dynamic_slice_in_dim(part, (1 - side) * half, half, 0))
            keeps.append(lax.dynamic_slice_in_dim(part, side * half, half, 0))
    for send, axis in zip(sends, axes):
        got.append(lax.ppermute(send, BOTH, first_dims(axis)))
    return sends, keeps, got


def scatter_end(keeps, got, done=None):
    return [add_low(a, b, done) for a, b in zip(keeps, got)]


def gather(block, rider, done=None):
    size = block.shape[0]
    steps = []
    extend = lambda part: part if rider is None else jnp.concatenate([part, rider], axis=0)
    send = lambda part, axis: lax.ppermute(part, BOTH, first_dims(axis))
    near, far = extend(block), None
    for axis in range(3):
        got = send(near, axis)
        if far is None:
            far = got[:size]
            left, right = block, far
        else:
            far = send(right, 3 - axis)
            ends = [left, got[:left.shape[0]], right, far]
            if axis == 1:
                left, right = jnp.concatenate(ends[:2], axis=0), jnp.concatenate(ends[2:], axis=0)
        if rider is not None:
            rider = add_low(rider, got[-rider.shape[0]:], done if axis == 0 else None)
        near = extend(left)
        steps.append([got, far])
    return ends, rider, steps


def nothing_of(arrays):
    return sum(jnp.minimum(jnp.abs(a[:1, :1].astype(F32)), 0.0) for a in arrays)


def on_device(tokens, lengths, project_weight, project_bias, dense_weight, dense_bias, expand_weight, expand_bias,
              contract_weight, contract_bias, first_gain, first_shift, second_gain, second_shift, out_grad):
    core = lax.axis_index("shard")
    swap = lambda rows: lax.ppermute(rows, "shard", [(0, 1), (1, 0)])
    place = jnp.stack([core.astype(jnp.int32), lengths[0]] + [first_side(axis).astype(jnp.int32) for axis in range(3)])
    other_tokens = swap(tokens)
    other_grad = swap(out_grad)
    packed, b_expand = pack(
        project_bias, dense_bias, contract_bias, first_gain, first_shift, second_gain, second_shift, expand_bias)
    other_packed = swap(packed)
    other_expand = swap(expand_weight)
    other_project = swap(project_weight)
    tables = [jnp.asarray(t) for t in rotary_arrays()]

    (gc0, gc1, gc2, ge0, ge1, ge_send0, ge_send1, gbe, act, gh, w_expand, n1, seed, seed_sum, b_project, vec) = ffn(
        place, tokens, other_tokens, out_grad, other_grad, packed, other_packed,
        expand_weight, other_expand, b_expand, contract_weight)

    parts = [(gc0, gc1), (gc2, ge0), (jnp.concatenate([ge1, swap(ge_send0)], axis=0), swap(ge_send1))]

    sends, keeps, got = scatter_start(parts, 0)
    *qkvc, w_project = heads(place, n1, seed, tables, project_weight, other_project, b_project, dense_weight, sends)
    pieces, done = attend(0, 0, qkvc, tables, None, [])
    parts = scatter_end(keeps, got, done)
    sends, keeps, got = scatter_start(parts, 1)
    pieces, done = attend(0, 1, qkvc, tables, pieces, sends)
    parts = scatter_end(keeps, got, done)
    sends, keeps, got = scatter_start(parts, 2)
    pieces, done = attend(1, 0, qkvc, tables, pieces, sends)
    parts = scatter_end(keeps, got, done)
    block = jnp.concatenate(parts, axis=0)
    for axis, (pair, head) in enumerate(((1, 1), (2, 0), (2, 1))):
        got = lax.ppermute(block, BOTH, second_dims(axis))
        pieces, done = attend(pair, head, qkvc, tables, pieces, [block])
        if axis == 0:
            *merged, done = merge(0, act, gh, w_expand, contract_weight, [], [pieces])
        if axis == 1:
            mlp, q2, done = merge(1, act, gh, w_expand, contract_weight, merged, [pieces])
        if axis == 2:
            gd, gw0, gw1, gw_send0, gw_send1, gb, done = weights(place, n1, seed, pieces, [got])
        block = add_low(block, got, done)
    units = [(gd, gw0), (jnp.concatenate([gw1, swap(gw_send0)], axis=0), swap(gw_send1))]
    sends, keeps, late = halve(units, (1, 2))
    keep_out, send_out, keep_in, send_in, sums = tail(
        place, other_tokens, tokens, mlp, q2, w_project, dense_weight, vec, gb, pieces, sends + [block])
    ffn_ends, _, steps = gather(block, None)
    contract, expand, placed = finish_ffn(place, ffn_ends)

    rider, done = make_rider(place, sums, swap(sums), gbe, seed_sum, steps[0][:1])
    units = scatter_end(keeps, late, done)
    sends, keeps, late = halve(units, (2, 1))
    units = scatter_end(keeps, late)
    side = first_side(0)
    got = lax.ppermute(jnp.where(side == 0, units[1], units[0]), BOTH, first_dims(0))
    block = add_low(jnp.where(side == 0, units[0], units[1]), got)
    other_out, other_in = swap(send_out), swap(send_in)

    block = jnp.concatenate([block, rider], axis=0)
    for axis in (2, 0, 1):
        got, done = lax.ppermute(block, BOTH, second_dims(axis)), None
        if axis == 2:
            done = nothing_of(steps[1][1:])
        if axis == 0:
            outputs, input_grad, done = last(
                place, tokens, out_grad, keep_out, other_out, keep_in, other_in, vec, [block])
        if axis == 1:
            done = nothing_of(steps[2][1:])
        block = add_low(block, got, done)
    ends, rider, _ = gather(block[:192], block[192:], placed)
    project, dense, g_project, g_expand, g_dense, g_contract, gain_one, shift_one, gain_two, shift_two = finish(
        place, ends, rider, [])
    return (outputs, input_grad, project, g_project, dense, g_dense, expand, g_expand, contract, g_contract,
            gain_one, shift_one, gain_two, shift_two)


def solution(mesh):
    rows, first = P(("replica", "shard"), None), P("shard", None)
    one = P("shard")
    return jax.shard_map(
        on_device,
        mesh=mesh,
        in_specs=(rows, P("replica"), first, one, first, one, first, one, first, one, one, one, one, one, rows),
        out_specs=(rows, rows, first, one, first, one, first, one, first, one, one, one, one, one),
        check_vma=False,
    )
```
